128 devices in a mesh: dp: 32 (over z, x_hi, y), seq: 4 (over x_lo, core).
Axes of the slice: x: 4 (x_hi: 2, x_lo: 2; x = x_hi * 2 + x_lo), y: 4, z: 4, core: 2. Of those that a mesh axis runs over, the one named last changes fastest.
Arguments:
- src_x: bfloat16 [32, 1024, 768], P('dp', 'seq'), may hold values from -6 to 6
- tgt_x: bfloat16 [32, 512, 768], P('dp', 'seq'), may hold values from -6 to 6
- out_cot: bfloat16 [32, 512, 768], P('dp', 'seq'), may hold values from -6 to 6
- src_seg: int32 [32, 1024], P('dp', 'seq'), may hold values from 0 to 3, as said below
- tgt_seg: int32 [32, 512], P('dp', 'seq'), may hold values from 0 to 3, as said below
- src_pad: int32 [32, 1024], P('dp', 'seq'), may hold values from 0 to 1, as said below
- tgt_pad: int32 [32, 512], P('dp', 'seq'), may hold values from 0 to 1, as said below
- enc_master: float32 [768, 6144], P(('dp', 'seq'))
- dec_master: float32 [768, 9216], P(('dp', 'seq'))
- down_master: float32 [3072, 1536], P(('dp', 'seq'))
- small_master: float32 [768, 31], P(('dp', 'seq'))
- enc_first: float32 [768, 6144], P(('dp', 'seq'))
- dec_first: float32 [768, 9216], P(('dp', 'seq'))
- down_first: float32 [3072, 1536], P(('dp', 'seq'))
- small_first: float32 [768, 31], P(('dp', 'seq'))
- enc_second: float32 [768, 6144], P(('dp', 'seq'))
- dec_second: float32 [768, 9216], P(('dp', 'seq'))
- down_second: float32 [3072, 1536], P(('dp', 'seq'))
- small_second: float32 [768, 31], P(('dp', 'seq'))
Outputs:
- dec_out: float32 [32, 512, 768], P('dp', 'seq')
- src_grad: float32 [32, 1024, 768], P('dp', 'seq')
- tgt_grad: float32 [32, 512, 768], P('dp', 'seq')
- grad_norm: float32 [], replicated
- enc_new: float32 [768, 6144], P(('dp', 'seq'))
- dec_new: float32 [768, 9216], P(('dp', 'seq'))
- down_new: float32 [3072, 1536], P(('dp', 'seq'))
- small_new: float32 [768, 31], P(('dp', 'seq'))
- enc_first_new: float32 [768, 6144], P(('dp', 'seq'))
- dec_first_new: float32 [768, 9216], P(('dp', 'seq'))
- down_first_new: float32 [3072, 1536], P(('dp', 'seq'))
- small_first_new: float32 [768, 31], P(('dp', 'seq'))
- enc_second_new: float32 [768, 6144], P(('dp', 'seq'))
- dec_second_new: float32 [768, 9216], P(('dp', 'seq'))
- down_second_new: float32 [3072, 1536], P(('dp', 'seq'))
- small_second_new: float32 [768, 31], P(('dp', 'seq'))
- small_grad: float32 [768, 31], P(('dp', 'seq'))
The draws below stay inside these ranges and needn't reach their ends.
Inputs may be any that keep to these rules, and one draw needn't show every extreme that they name: `src_seg`: in every row the ids never fall and each of 0 to 3 names a run of positions; in a row, source id j and target id j are one document. `tgt_seg`: as for src_seg. `src_pad`: in every row the entries are 1 up to some position and 0 after it; the zeros lie in the row's last document, whose first position holds a 1. `tgt_pad`: as for src_pad.
All inputs are finite; a program needn't handle non-finite values.
Results may differ from the reference program's by a relative error of at most 0.02.
The reference program's roundings to bfloat16 on the way count: a program that leaves them out, or rounds other values in their place, can miss the bound.
Values may be sent and summed in bfloat16 or wider, within the bound.
No kernel may reach another device: no remote copies, remote signals or barrier semaphores. Data moves between devices by JAX's collectives and lax.ppermute only.
A program may use at most 256 MiB of HBM per device.

```python
import math
import jax
import jax.numpy as jnp
from jax import lax

D = 768
FF = 3072
HEADS = 12
HEAD = 64
SRC = 1024
TGT = 512
DOCS = 4
STEP = 10
NSMALL = 31
ROWS = 32
NPARAMS = 16538880


CLIP_LEVEL = 1.0


def layout(key, length, salt, small_lo, small_hi):
    longest = jax.random.randint(jax.random.fold_in(key, 21), (ROWS, 1), 0, DOCS)
    key = jax.random.fold_in(key, salt)
    key_len, key_pad = jax.random.split(key)
    doc_sizes = jax.random.randint(key_len, (ROWS, DOCS), small_lo, small_hi + 1)
    picked = jnp.arange(DOCS)[None, :] == longest
    doc_sizes = jnp.where(picked, 0, doc_sizes)
    doc_sizes = jnp.where(picked, length - jnp.sum(doc_sizes, axis=1, keepdims=True), doc_sizes)
    doc_ends = jnp.cumsum(doc_sizes, axis=1)
    places = jnp.arange(length)
    doc_ids = jnp.sum((places[None, :, None] >= doc_ends[:, None, :]).astype(jnp.int32), axis=2)
    padding = jax.random.randint(key_pad, (ROWS, 1), 0, doc_sizes[:, -1:] // 4 + 1)
    real_mask = (places[None, :] < length - padding).astype(jnp.int32)
    return (doc_ids.astype(jnp.int32), real_mask)


def source_layout(key):
    return layout(key, SRC, 11, max(1, SRC // (8 * DOCS)), SRC // (4 * DOCS))


def target_layout(key):
    return layout(key, TGT, 12, 1, max(2, TGT // (16 * DOCS)))


def draw_src_seg(key, part):
    shared = source_layout(key)
    return shared[0]


def draw_src_pad(key, part):
    shared = source_layout(key)
    return shared[1]


def draw_tgt_seg(key, part):
    shared = target_layout(key)
    return shared[0]


def draw_tgt_pad(key, part):
    shared = target_layout(key)
    return shared[1]


def draw_enc_master(key, part):
    key = jax.random.fold_in(key, 1)
    columns = jnp.arange(4 * D + FF)
    scaling = jnp.where((columns >= 3 * D) & (columns < 4 * D), 4.0, 1.0) / math.sqrt(D)
    return jax.random.normal(key, (D, 4 * D + FF), jnp.float32) * scaling[None, :]


def draw_dec_master(key, part):
    key = jax.random.fold_in(key, 2)
    columns = jnp.arange(8 * D + FF)
    outputs = (columns >= 3 * D) & (columns < 4 * D) | (columns >= 7 * D) & (columns < 8 * D)
    scaling = jnp.where(outputs, 4.0, 1.0) / math.sqrt(D)
    return jax.random.normal(key, (D, 8 * D + FF), jnp.float32) * scaling[None, :]


def draw_down_master(key, part):
    key = jax.random.fold_in(key, 3)
    return jax.random.normal(key, (FF, 2 * D), jnp.float32) / math.sqrt(FF)


def draw_small_master(key, part):
    key = jax.random.fold_in(key, 4)
    key_gain, key_bias = jax.random.split(key)
    columns = jnp.arange(NSMALL)
    is_gain = (columns == 0) | (columns == 5) | (columns == 12) | (columns == 14) | (columns == 19) | (columns == 24)
    rising = 0.6 + 1.2 * jnp.arange(D, dtype=jnp.float32) / (D - 1)
    gains = rising[:, None] * jax.random.uniform(key_gain, (D, NSMALL), jnp.float32, 0.85, 1.15)
    biases = 0.2 * jax.random.normal(key_bias, (D, NSMALL), jnp.float32)
    return jnp.where(is_gain[None, :], gains, biases)


def grad_scale(factor):
    return factor * CLIP_LEVEL / math.sqrt(NPARAMS)


def first_moment(key, shape, factor):
    return 0.11 * grad_scale(factor) * jax.random.normal(key, shape, jnp.float32)


def second_moment(key, shape, factor):
    spread = jnp.exp(jax.random.uniform(key, shape, jnp.float32, 0.0, math.log(4.0)))
    return spread * 0.001 * grad_scale(factor) ** 2


def draw_enc_first(key, part):
    key = jax.random.fold_in(key, 5)
    return first_moment(key, (D, 4 * D + FF), 1.0)


def draw_dec_first(key, part):
    key = jax.random.fold_in(key, 6)
    return first_moment(key, (D, 8 * D + FF), 1.0)


def draw_down_first(key, part):
    key = jax.random.fold_in(key, 7)
    return first_moment(key, (FF, 2 * D), 1.0)


def draw_small_first(key, part):
    key = jax.random.fold_in(key, 8)
    return first_moment(key, (D, NSMALL), 3.0)


def draw_enc_second(key, part):
    key = jax.random.fold_in(key, 9)
    return second_moment(key, (D, 4 * D + FF), 1.0)


def draw_dec_second(key, part):
    key = jax.random.fold_in(key, 10)
    return second_moment(key, (D, 8 * D + FF), 1.0)


def draw_down_second(key, part):
    key = jax.random.fold_in(key, 13)
    return second_moment(key, (FF, 2 * D), 1.0)


def draw_small_second(key, part):
    key = jax.random.fold_in(key, 14)
    return second_moment(key, (D, NSMALL), 3.0)


def level_of(key, dims, shards, smallest, top_value):
    factor_of, own = 1.0, jax.random.fold_in(key, 6)
    for dim, shards_of in shards:
        steps = jnp.exp(jax.random.uniform(jax.random.fold_in(own, dim), (shards_of,), jnp.float32, smallest / len(shards), top_value / len(shards)))
        factor_of = factor_of * jnp.repeat(steps, dims[dim] // shards_of).reshape([-1 if axis == dim else 1 for axis in range(len(dims))])
    return factor_of


def centred(rng, shape, scale, reach, cuts=(), kind=jnp.bfloat16):
    level = level_of(rng, shape, cuts, -0.22, 0.18) if cuts else 1.0
    result = jax.random.normal(rng, shape, jnp.float32) * scale * level
    return jnp.minimum(jnp.maximum(result, -reach), reach).astype(kind)


def setup_inputs(seed: int = 0) -> dict:
    splits = jax.random.split(jax.random.key(seed), 20)
    src_x = centred(splits[0], (ROWS, SRC, D), 1.0, 6.0, ((0, 32), (1, 4)))
    tgt_x = centred(splits[1], (ROWS, TGT, D), 1.0, 6.0, ((0, 32), (1, 4)))
    out_cot = centred(splits[2], (ROWS, TGT, D), 1.0, 6.0, ((0, 32), (1, 4)))
    src_seg = draw_src_seg(jax.random.fold_in(splits[19], 71), 0)
    tgt_seg = draw_tgt_seg(jax.random.fold_in(splits[19], 71), 0)
    src_pad = draw_src_pad(jax.random.fold_in(splits[19], 71), 0)
    tgt_pad = draw_tgt_pad(jax.random.fold_in(splits[19], 71), 0)
    enc_master = draw_enc_master(jax.random.fold_in(splits[19], 71), 0)
    dec_master = draw_dec_master(jax.random.fold_in(splits[19], 71), 0)
    down_master = draw_down_master(jax.random.fold_in(splits[19], 71), 0)
    small_master = draw_small_master(jax.random.fold_in(splits[19], 71), 0)
    enc_first = draw_enc_first(jax.random.fold_in(splits[19], 71), 0)
    dec_first = draw_dec_first(jax.random.fold_in(splits[19], 71), 0)
    down_first = draw_down_first(jax.random.fold_in(splits[19], 71), 0)
    small_first = draw_small_first(jax.random.fold_in(splits[19], 71), 0)
    enc_second = draw_enc_second(jax.random.fold_in(splits[19], 71), 0)
    dec_second = draw_dec_second(jax.random.fold_in(splits[19], 71), 0)
    down_second = draw_down_second(jax.random.fold_in(splits[19], 71), 0)
    small_second = draw_small_second(jax.random.fold_in(splits[19], 71), 0)
    return {"src_x": src_x, "tgt_x": tgt_x, "out_cot": out_cot, "src_seg": src_seg, "tgt_seg": tgt_seg, "src_pad": src_pad, "tgt_pad": tgt_pad, "enc_master": enc_master, "dec_master": dec_master, "down_master": down_master, "small_master": small_master, "enc_first": enc_first, "dec_first": dec_first, "down_first": down_first, "small_first": small_first, "enc_second": enc_second, "dec_second": dec_second, "down_second": down_second, "small_second": small_second}


@jax.custom_vjp
def low(v):
    return lax.optimization_barrier(v.astype(jnp.bfloat16)).astype(jnp.float32)

@jax.custom_vjp
def low_back(v):
    return v

def low_keep(v):
    return (low(v), None)

def low_pass(kept, grad):
    return (grad,)

def back_keep(v):
    return (v, None)

def back_low(kept, grad):
    return (low(grad),)
low.defvjp(low_keep, low_pass)
low_back.defvjp(back_keep, back_low)
HIGHEST = lax.Precision.HIGHEST
NORM_EPS = 1e-05
MASKED = -1000000000.0
BETA_FIRST = 0.9
BETA_SECOND = 0.999
ADAM_EPS = 1e-08
RATE_MATRIX = 0.1
RATE_SMALL = 0.5
DECAY_RATE = 0.01
CLIP_LEVEL = 1.0

def layer_norm(inputs, scaling, offset):
    center = inputs - lax.optimization_barrier(jnp.mean(inputs, axis=-1, keepdims=True))
    spread = lax.optimization_barrier(jnp.mean(center * center, axis=-1, keepdims=True))
    return center * lax.rsqrt(spread + NORM_EPS) * scaling + offset

def matmul(left, right):
    return jnp.dot(left, right, precision=HIGHEST)

def project_in(normed, weight, bias):
    return low(low_back(matmul(normed, weight) + bias))

def attend(query, keys, values, allowed):
    heads_query = query.reshape(query.shape[0], HEADS, HEAD)
    heads_keys = keys.reshape(keys.shape[0], HEADS, HEAD)
    heads_values = values.reshape(values.shape[0], HEADS, HEAD)
    raw_scores = jnp.einsum('qhe,khe->hqk', heads_query, heads_keys, precision=HIGHEST) * HEAD ** (-0.5)
    scores = jnp.where(allowed[None], low_back(raw_scores), MASKED)
    expo = jnp.exp(scores - lax.optimization_barrier(jnp.max(scores, axis=-1, keepdims=True)))
    probs = low(expo / lax.optimization_barrier(jnp.sum(expo, axis=-1, keepdims=True)))
    mixed = jnp.einsum('hqk,khe->qhe', probs, heads_values, precision=HIGHEST)
    return low(low_back(mixed.reshape(query.shape[0], D)))

def feed(resid, w_in, w_out, params, base):
    normed = low(layer_norm(resid, params[:, base], params[:, base + 1]))
    bias_in = params[:, base + 3:base + 7].T.reshape(FF)
    hidden = low_back(matmul(normed, w_in) + bias_in)
    active = low(jax.nn.gelu(hidden, approximate=False))
    return resid + low_back(matmul(active, w_out) + params[:, base + 2])

def forward(source, target, enc_w, dec_w, down_w, params, src_ids, src_mask, tgt_ids, tgt_mask):
    allow_enc = (src_ids[:, None] == src_ids[None, :]) & (src_mask[None, :] == 1)
    normed = low(layer_norm(source, params[:, 0], params[:, 1]))
    query = project_in(normed, enc_w[:, :D], params[:, 2])
    keys = project_in(normed, enc_w[:, D:2 * D], 0.0)
    values = project_in(normed, enc_w[:, 2 * D:3 * D], params[:, 3])
    resid = source + low_back(matmul(attend(query, keys, values, allow_enc), enc_w[:, 3 * D:4 * D]) + params[:, 4])
    resid = feed(resid, enc_w[:, 4 * D:], down_w[:, :D], params, 5)
    memory = low_back(low(layer_norm(resid, params[:, 12], params[:, 13])))
    spots = jnp.arange(TGT, dtype=jnp.int32)
    allow_self = (tgt_ids[:, None] == tgt_ids[None, :]) & (tgt_mask[None, :] == 1) & (spots[None, :] <= spots[:, None])
    allow_cross = (tgt_ids[:, None] == src_ids[None, :]) & (src_mask[None, :] == 1)
    normed = low(layer_norm(target, params[:, 14], params[:, 15]))
    query = project_in(normed, dec_w[:, :D], params[:, 16])
    keys = project_in(normed, dec_w[:, D:2 * D], 0.0)
    values = project_in(normed, dec_w[:, 2 * D:3 * D], params[:, 17])
    resid = target + low_back(matmul(attend(query, keys, values, allow_self), dec_w[:, 3 * D:4 * D]) + params[:, 18])
    normed = low(layer_norm(resid, params[:, 19], params[:, 20]))
    query = project_in(normed, dec_w[:, 4 * D:5 * D], params[:, 21])
    keys = low(matmul(memory, dec_w[:, 5 * D:6 * D]))
    values = low(matmul(memory, dec_w[:, 6 * D:7 * D]) + params[:, 22])
    resid = resid + low_back(matmul(attend(query, keys, values, allow_cross), dec_w[:, 7 * D:8 * D]) + params[:, 23])
    return feed(resid, dec_w[:, 8 * D:], down_w[:, D:], params, 24)

def adam_step(master, first, second, gradient, factor, rate, decay):
    clipped = gradient * factor
    first_new = BETA_FIRST * first + (1 - BETA_FIRST) * clipped
    second_new = BETA_SECOND * second + (1 - BETA_SECOND) * clipped * clipped
    first_hat = first_new / (1 - BETA_FIRST ** STEP)
    second_hat = second_new / (1 - BETA_SECOND ** STEP)
    master_new = master - rate * (first_hat / (jnp.sqrt(second_hat) + ADAM_EPS) + decay * master)
    return (master_new, first_new, second_new)

def reference(src_x, tgt_x, out_cot, src_seg, tgt_seg, src_pad, tgt_pad, enc_master, dec_master, down_master, small_master, enc_first, dec_first, down_first, small_first, enc_second, dec_second, down_second, small_second):
    enc_w = low(enc_master)
    dec_w = low(dec_master)
    down_w = low(down_master)
    small_w = low(small_master)

    def one_row(totals, row):
        source, target, cotangent, src_ids, src_mask, tgt_ids, tgt_mask = row

        def local_forward(src_in, tgt_in, enc_in, dec_in, down_in, small_in):
            return forward(src_in, tgt_in, enc_in, dec_in, down_in, small_in, src_ids, src_mask, tgt_ids, tgt_mask)
        output, pull = jax.vjp(local_forward, source.astype(jnp.float32), target.astype(jnp.float32), enc_w, dec_w, down_w, small_w)
        grads = pull(cotangent.astype(jnp.float32))
        summed = (totals[0] + grads[2], totals[1] + grads[3], totals[2] + grads[4], totals[3] + grads[5])
        return (summed, (output, grads[0], grads[1]))
    start = (jnp.zeros(enc_w.shape, jnp.float32), jnp.zeros(dec_w.shape, jnp.float32), jnp.zeros(down_w.shape, jnp.float32), jnp.zeros(small_w.shape, jnp.float32))
    totals, stacked = lax.scan(one_row, start, (src_x, tgt_x, out_cot, src_seg, src_pad, tgt_seg, tgt_pad))
    squares = jnp.sum(totals[0] * totals[0]) + jnp.sum(totals[1] * totals[1]) + jnp.sum(totals[2] * totals[2]) + jnp.sum(totals[3] * totals[3])
    grad_norm = jnp.sqrt(squares)
    factor = CLIP_LEVEL / jnp.maximum(grad_norm, CLIP_LEVEL)
    enc_all = adam_step(enc_master, enc_first, enc_second, totals[0], factor, RATE_MATRIX, DECAY_RATE)
    dec_all = adam_step(dec_master, dec_first, dec_second, totals[1], factor, RATE_MATRIX, DECAY_RATE)
    down_all = adam_step(down_master, down_first, down_second, totals[2], factor, RATE_MATRIX, DECAY_RATE)
    small_all = adam_step(small_master, small_first, small_second, totals[3], factor, RATE_SMALL, 0.0)
    return (stacked[0], stacked[1], stacked[2], grad_norm, enc_all[0], dec_all[0], down_all[0], small_all[0], enc_all[1], dec_all[1], down_all[1], small_all[1], enc_all[2], dec_all[2], down_all[2], small_all[2], totals[3] * factor)
```

```python
import jax
import jax.numpy as jnp
import numpy as np
from jax import lax
from jax.experimental import pallas as pl
from jax.experimental.pallas import tpu as pltpu
from jax.sharding import Mesh, PartitionSpec as P

HEAD = 64
STEP = 10
NORM_EPS = 1e-05
MASKED = -1000000000.0
BETA_FIRST = 0.9
BETA_SECOND = 0.999
ADAM_EPS = 1e-08
RATE_MATRIX = 0.1
RATE_SMALL = 0.5
DECAY_RATE = 0.01
CLIP_LEVEL = 1.0
BF = jnp.bfloat16
F32 = jnp.float32
PAIR = 2 * HEAD
LANES = 128
ROW_AXES = ("z", "xh", "y")
POS_AXES = ("xl", "c")
ALL_AXES = ("z", "xh", "y", "xl", "c")
SWAP = [(0, 1), (1, 0)]


def swap(value, axis):
    return lax.ppermute(value, axis, SWAP)


def join_core(value):
    return jnp.concatenate([value, swap(value, "c")], axis=0)


def sum_core(partial):
    mine = partial.shape[0] // 2
    return partial[:mine] + swap(partial[mine:], "c")


def swap_z(value):
    other = lax.ppermute(value, ("z", "c"), [(1, 4), (4, 1), (3, 6), (6, 3)])
    moved = (lax.axis_index("z") // 2) != lax.axis_index("c")
    return jnp.where(moved, other, value)


def feature_order(width):
    rest = width // 32
    new = np.arange(width)
    z, y, xh, r = new // (8 * rest), (new // (2 * rest)) % 4, (new // rest) % 2, new % rest
    old = ((z * 2 + xh) * 4 + y) * rest + r
    return old


def head_order(width):
    r = width // 128
    own = np.arange(width // 2)
    z, xh, y, xl, c, i = (
        own // (32 * r) // 2,
        (own // (16 * r)) % 2,
        (own // (4 * r)) % 4,
        (own // (2 * r)) % 2,
        (own // r) % 2,
        own % r,
    )
    z = own // (32 * r)
    places = []
    for half in range(2):
        place = (((((c * 2 + z) * 4 + y) * 2 + xh) * 2 + xl) * 2 + half) * r + i
        places.append(place)
    return np.concatenate(places)


def one_hot(picks, width):
    rows = lax.broadcasted_iota(jnp.int32, (width, len(picks)), 0)
    return (rows == jnp.asarray(picks, jnp.int32)[None, :]).astype(BF)


def dot(left, right, kind=F32):
    return jnp.dot(left, right, preferred_element_type=kind)


def dot_t(left, right, kind=F32):
    return lax.dot_general(left, right, (((0,), (0,)), ((), ())), preferred_element_type=kind)


def dot_b(left, right, kind=F32):
    return lax.dot_general(left, right, (((1,), (1,)), ((), ())), preferred_element_type=kind)


def two_parts(value):
    high = lax.reduce_precision(value, 8, 7)
    return high.astype(BF), (value - high).astype(BF)


def reorder_wide(value, order):
    high, low = two_parts(value)
    both = dot_b(jnp.concatenate([high, low], axis=0), order)
    return both[: value.shape[0]] + both[value.shape[0] :]


def norm_stats(x):
    center = x - jnp.mean(x, axis=-1, keepdims=True)
    spread = jnp.mean(center * center, axis=-1, keepdims=True)
    scale = lax.rsqrt(spread + NORM_EPS)
    return center * scale, scale


def norm(x, gain, shift):
    unit, scale = norm_stats(x)
    return (unit * gain + shift).astype(BF)


def norm_back(x, gain, gradient):
    unit, scale = norm_stats(x)
    inner = gradient * gain
    back = scale * (
        inner
        - jnp.mean(inner, axis=-1, keepdims=True)
        - unit * jnp.mean(inner * unit, axis=-1, keepdims=True)
    )
    return back, jnp.sum(gradient * unit, axis=0), jnp.sum(gradient, axis=0)


def gelu_parts(u):
    cdf = 0.5 * (1.0 + lax.erf(u * (0.5**0.5)))
    pdf = jnp.exp(-0.5 * u * u) * (1.0 / np.sqrt(2.0 * np.pi)).astype(np.float32)
    return u * cdf, cdf + u * pdf


def lane_mask(value, which):
    lane = lax.broadcasted_iota(jnp.int32, value.shape, 1)
    return jnp.where((lane // HEAD) == which, value, jnp.zeros_like(value))


def allowed_of(causal, ids_ref, qid_ref, part):
    seg = ids_ref[part, :, 0:1] == qid_ref[0:1, :]
    if causal:
        seg = seg & (ids_ref[part, :, 1:2] <= qid_ref[1:2, :])
    return seg


def scores_t(keys, query, allowed):
    raw = lax.dot_general(keys, query, (((1,), (1,)), ((), ())), preferred_element_type=F32)
    return jnp.where(allowed, raw, MASKED)


def attend_kernel(causal, q_ref, k0_ref, v0_ref, k1_ref, v1_ref, ids_ref, qid_ref, o_ref, lse_ref):
    query = q_ref[...] * jnp.asarray(HEAD**-0.5, BF)
    allowed = [allowed_of(causal, ids_ref, qid_ref, part) for part in range(2)]
    mixed = []
    for head in range(2):
        one = lane_mask(query, head)
        scores = [scores_t(ref[...], one, ok) for ref, ok in zip((k0_ref, k1_ref), allowed)]
        top = jnp.maximum(
            jnp.max(scores[0], axis=0, keepdims=True), jnp.max(scores[1], axis=0, keepdims=True)
        )
        expo = [jnp.exp(s - top) for s in scores]
        total = jnp.sum(expo[0], axis=0, keepdims=True) + jnp.sum(expo[1], axis=0, keepdims=True)
        share = 1.0 / total
        out = 0.0
        for ref, e in zip((v0_ref, v1_ref), expo):
            out = out + lax.dot_general(
                ref[...], (e * share).astype(BF), (((0,), (0,)), ((), ())), preferred_element_type=F32
            )
        mixed.append(out)
        lse_ref[0, head : head + 1, :] = top + jnp.log(total)
    both = jnp.concatenate([mixed[0][:HEAD], mixed[1][HEAD:]], axis=0)
    o_ref[...] = both.T.astype(BF)


def attend_back_kernel(
    causal, q_ref, k0_ref, v0_ref, k1_ref, v1_ref, g_ref, ids_ref, qid_ref, lse_ref,
    dq_ref, dk0_ref, dv0_ref, dk1_ref, dv1_ref,
):
    query = q_ref[...] * jnp.asarray(HEAD**-0.5, BF)
    grad = g_ref[...]
    allowed = [allowed_of(causal, ids_ref, qid_ref, part) for part in range(2)]
    keys = (k0_ref[...], k1_ref[...])
    values = (v0_ref[...], v1_ref[...])
    grad_q = 0.0
    grad_k = [0.0, 0.0]
    grad_v = [0.0, 0.0]
    for head in range(2):
        one = lane_mask(query, head)
        grad_one = lane_mask(grad, head)
        lse = lse_ref[0, head : head + 1, :]
        probs = [jnp.exp(scores_t(k, one, ok) - lse) for k, ok in zip(keys, allowed)]
        grad_p = [
            lax.dot_general(v, grad_one, (((1,), (1,)), ((), ())), preferred_element_type=F32)
            for v in values
        ]
        inner = jnp.sum(probs[0] * grad_p[0], axis=0, keepdims=True) + jnp.sum(
            probs[1] * grad_p[1], axis=0, keepdims=True
        )
        for part in range(2):
            grad_s = (probs[part] * (grad_p[part] - inner)).astype(BF)
            grad_v[part] = grad_v[part] + dot(probs[part].astype(BF), grad_one)
            grad_k[part] = grad_k[part] + dot(grad_s, one)
            grad_q = grad_q + lax.dot_general(
                lane_mask(keys[part], head), grad_s, (((0,), (0,)), ((), ())),
                preferred_element_type=F32,
            )
    dq_ref[...] = (grad_q * HEAD**-0.5).T.astype(BF)
    dk0_ref[...] = grad_k[0]
    dv0_ref[...] = grad_v[0]
    dk1_ref[...] = grad_k[1].astype(BF)
    dv1_ref[...] = grad_v[1].astype(BF)


def call_kernel(body, causal, arrays, ids, qid, extra, out_shape, out_specs, cost):
    in_specs = [
        pl.BlockSpec((a.shape[0], PAIR), lambda p, at=at: (0, at + p)) for a, at in arrays
    ]
    in_specs.append(pl.BlockSpec(ids.shape, lambda p: (0, 0, 0)))
    in_specs.append(pl.BlockSpec(qid.shape, lambda p: (0, 0)))
    in_specs += [pl.BlockSpec((1,) + e.shape[1:], lambda p: (p, 0, 0)) for e in extra]

    def kernel(*refs):
        body(causal, *refs)

    pairs = extra[0].shape[0] if extra else out_shape[1].shape[0]
    return pl.pallas_call(
        kernel,
        grid=(pairs,),
        in_specs=in_specs,
        out_specs=out_specs,
        out_shape=out_shape,
        compiler_params=pltpu.CompilerParams(vmem_limit_bytes=56 * 1024 * 1024),
        cost_estimate=cost,
    )(*[a for a, at in arrays], ids, qid, *extra)


def cost_of(n_q, n_k, width, products):
    return pl.CostEstimate(
        flops=4 * 2 * products * n_q * n_k * width,
        bytes_accessed=4 * (n_q + n_k) * width,
        transcendentals=n_q * n_k * width // HEAD,
    )


def attend_fwd(causal, arrays, ids, qid, pairs):
    n_q = qid.shape[1]
    out_shape = (
        jax.ShapeDtypeStruct((n_q, pairs * PAIR), BF),
        jax.ShapeDtypeStruct((pairs, 2, n_q), F32),
    )
    out_specs = (
        pl.BlockSpec((n_q, PAIR), lambda p: (0, p)),
        pl.BlockSpec((1, 2, n_q), lambda p: (p, 0, 0)),
    )
    return call_kernel(
        attend_kernel, causal, arrays, ids, qid, (), out_shape, out_specs,
        cost_of(n_q, 2 * ids.shape[1], pairs * PAIR, 2),
    )


def attend_back(causal, arrays, grad, ids, qid, lse):
    pairs, n_q, n_k = lse.shape[0], qid.shape[1], ids.shape[1]
    wide = pairs * PAIR
    out_shape = (
        jax.ShapeDtypeStruct((n_q, wide), BF),
        jax.ShapeDtypeStruct((n_k, wide), F32),
        jax.ShapeDtypeStruct((n_k, wide), F32),
        jax.ShapeDtypeStruct((n_k, wide), BF),
        jax.ShapeDtypeStruct((n_k, wide), BF),
    )
    out_specs = tuple(pl.BlockSpec((s.shape[0], PAIR), lambda p: (0, p)) for s in out_shape)
    return call_kernel(
        attend_back_kernel, causal, list(arrays) + [(grad, 0)], ids, qid, (lse,), out_shape, out_specs,
        cost_of(n_q, 2 * n_k, wide, 5),
    )


def adam_step(master, first, second, gradient, factor, rate, decay):
    clipped = gradient * factor
    first_new = BETA_FIRST * first + (1 - BETA_FIRST) * clipped
    second_new = BETA_SECOND * second + (1 - BETA_SECOND) * clipped * clipped
    first_hat = first_new / (1 - BETA_FIRST**STEP)
    second_hat = second_new / (1 - BETA_SECOND**STEP)
    master_new = master - rate * (first_hat / (jnp.sqrt(second_hat) + ADAM_EPS) + decay * master)
    return (master_new, first_new, second_new)


def per_device(
    src_x, tgt_x, out_cot, src_seg, tgt_seg, src_pad, tgt_pad,
    enc_master, dec_master, down_master, small_master,
    enc_first, dec_first, down_first, small_first,
    enc_second, dec_second, down_second, small_second,
):
    width = src_x.shape[-1]
    half = width // 2
    hid = 2 * width
    pairs = half // PAIR
    rows = enc_master.shape[0]
    down_rows = down_master.shape[0]
    n_small = small_master.shape[1]
    core = lax.axis_index("c")
    first_core = core == 0
    order = one_hot(feature_order(width), width)
    place = one_hot(head_order(width), width)

    encb, decb, downb = enc_master.astype(BF), dec_master.astype(BF), down_master.astype(BF)
    smallb = jnp.pad(small_master.astype(BF), ((0, 0), (0, LANES - n_small)))

    def block(matrix, index):
        return matrix[:, index * width : (index + 1) * width]

    def halves(matrix):
        n = matrix.shape[1] // 2
        return matrix[:, :n], matrix[:, n:]

    col_blocks = [
        halves(block(encb, 0)), halves(block(encb, 1)), halves(block(encb, 2)), (smallb, smallb),
        halves(encb[:, 4 * width :]),
        halves(block(decb, 0)), halves(block(decb, 1)), halves(block(decb, 2)),
        halves(block(decb, 4)), halves(block(decb, 5)), halves(block(decb, 6)),
        halves(decb[:, 8 * width :]),
    ]
    cols0 = jnp.concatenate([b[0] for b in col_blocks], axis=1)
    cols1 = jnp.concatenate([b[1] for b in col_blocks], axis=1)
    mine = jnp.where(first_core, cols0, cols1)
    theirs = swap(jnp.where(first_core, cols1, cols0), "c")
    cols = jnp.concatenate(
        [jnp.where(first_core, mine, theirs), jnp.where(first_core, theirs, mine)], axis=0
    )
    cols = lax.all_gather(cols, ("xh", "xl"), axis=0, tiled=True)

    row_shard = jnp.concatenate(
        [block(encb, 3), block(decb, 3), block(decb, 7), downb[:, :width], downb[:, width:]], axis=0
    )
    row_shard = swap_z(dot(row_shard, order, BF))
    row_shard = lax.all_gather(row_shard, ("xh", "xl"), axis=0)

    def pack_out(index):
        part = row_shard[:, index * rows : (index + 1) * rows].reshape(4, rows, 2, half)
        return part.transpose(0, 2, 1, 3).reshape(8 * rows, half)

    def pack_down(index):
        at = 3 * rows + index * down_rows
        part = row_shard[:, at : at + down_rows].reshape(2, 2 * down_rows, width)
        return [part[0], part[1]]

    n_qkv, n_one = 3 * half, 3 * half + LANES
    n_two, n_three = n_one + hid, n_one + hid + 6 * half
    shard_one = cols[:, :n_one]
    shard_two = jnp.concatenate([pack_out(0), cols[:, n_one:n_two]] + pack_down(0), axis=1)
    shard_three = jnp.concatenate([cols[:, n_two:n_three], pack_out(1), pack_out(2)], axis=1)
    shard_four = jnp.concatenate([cols[:, n_three:]] + pack_down(1), axis=1)

    def spread(shard):
        return lax.all_gather(shard, ("z", "y"), axis=0, tiled=True)

    full_one, full_two, full_three, full_four = (
        spread(shard_one), spread(shard_two), spread(shard_three), spread(shard_four),
    )

    def unpack_out(part):
        natural = dot_t(place, part, BF)
        return jnp.concatenate([natural[:half], natural[half:]], axis=1)

    def repack_out(grad):
        stacked = jnp.concatenate([grad[:, :half], grad[:, half:]], axis=0)
        return dot(place, stacked, BF)

    def unpack_down(part):
        part = jnp.stack([part[:, :width], part[:, width:]], axis=0)
        part = part.reshape(2, 2, 2, 4, 2, down_rows, width)
        return part.transpose(2, 0, 3, 4, 1, 5, 6).reshape(hid, width)

    def repack_down(grad):
        part = grad.reshape(2, 2, 4, 2, 2, down_rows, width)
        part = part.transpose(1, 4, 0, 2, 3, 5, 6).reshape(2, width, width)
        return [part[0], part[1]]

    w_eqkv, small_all = full_one[:, :n_qkv], full_one[:, n_qkv:]
    w_eo = unpack_out(full_two[:, :half])
    w_e1 = full_two[:, half : half + hid]
    w_e2 = unpack_down(full_two[:, half + hid :])
    w_dqkv = full_three[:, :n_qkv]
    w_cq = full_three[:, n_qkv : 4 * half]
    w_ckv = full_three[:, 4 * half : 6 * half]
    w_so = unpack_out(full_three[:, 6 * half : 7 * half])
    w_co = unpack_out(full_three[:, 7 * half :])
    w_d1 = full_four[:, :hid]
    w_d2 = unpack_down(full_four[:, hid:])

    eye = one_hot(np.arange(width), width)
    small_p = dot_t(small_all, eye)
    small_own = dot_b(small_all.T, order)

    def own_half(column):
        row = small_own[column]
        return jnp.where(first_core, row[:half], row[half:])

    def hidden_bias(column):
        low = jnp.concatenate([small_own[column], small_own[column + 1]])
        high = jnp.concatenate([small_own[column + 2], small_own[column + 3]])
        return jnp.where(first_core, low, high)

    none = jnp.zeros((half,), F32)

    def ids_of(seg, pad, at):
        n = seg.shape[1]
        spot = (lax.axis_index("xl") * 2 + core) * n + jnp.arange(n, dtype=jnp.int32)
        key = jnp.where(pad[0] == 1, seg[0], -1)
        return jnp.stack([key, spot, seg[0]], axis=1)

    src_ids = join_core(ids_of(src_seg, src_pad, 0))
    tgt_ids = join_core(ids_of(tgt_seg, tgt_pad, 0))
    src_keys = jnp.stack([src_ids[:, :2], swap(src_ids[:, :2], "xl")])
    tgt_keys = jnp.stack([tgt_ids[:, :2], swap(tgt_ids[:, :2], "xl")])
    src_q = jnp.stack([src_ids[:, 2], src_ids[:, 1]])
    tgt_q = jnp.stack([tgt_ids[:, 2], tgt_ids[:, 1]])

    source = dot(src_x[0], order)
    enc_norm = join_core(norm(source, small_p[0], small_p[1]))
    enc_qkv = (dot(enc_norm, w_eqkv) + jnp.concatenate([own_half(2), none, own_half(3)])).astype(BF)
    enc_far = swap(enc_qkv[:, half:], "xl")
    enc_arrays = [(enc_qkv, 0), (enc_qkv, pairs), (enc_qkv, 2 * pairs), (enc_far, 0), (enc_far, pairs)]

    target = dot(tgt_x[0], order)
    dec_norm = join_core(norm(target, small_p[14], small_p[15]))

    enc_att, enc_lse = attend_fwd(False, enc_arrays, src_keys, src_q, pairs)
    enc_one = source + sum_core(dot(enc_att, w_eo)) + small_p[4]

    def feed_fwd(resid, w_in, w_out, base):
        normed = join_core(norm(resid, small_p[base], small_p[base + 1]))
        active, slope = gelu_parts(dot(normed, w_in) + hidden_bias(base + 3))
        active = active.astype(BF)
        return normed, active, slope, resid + sum_core(dot(active, w_out)) + small_p[base + 2]

    enc_ffn = feed_fwd(enc_one, w_e1, w_e2, 5)
    enc_two = enc_ffn[3]
    memory = join_core(norm(enc_two, small_p[12], small_p[13]))

    dec_qkv = (dot(dec_norm, w_dqkv) + jnp.concatenate([own_half(16), none, own_half(17)])).astype(BF)
    dec_far = swap(dec_qkv[:, half:], "xl")
    dec_arrays = [(dec_qkv, 0), (dec_qkv, pairs), (dec_qkv, 2 * pairs), (dec_far, 0), (dec_far, pairs)]
    self_att, self_lse = attend_fwd(True, dec_arrays, tgt_keys, tgt_q, pairs)
    dec_one = target + sum_core(dot(self_att, w_so)) + small_p[18]
    cross_norm = join_core(norm(dec_one, small_p[19], small_p[20]))
    cross_q = (dot(cross_norm, w_cq) + own_half(21)).astype(BF)
    cross_kv = (dot(memory, w_ckv) + jnp.concatenate([none, own_half(22)])).astype(BF)
    cross_far = swap(cross_kv, "xl")
    cross_arrays = [(cross_q, 0), (cross_kv, 0), (cross_kv, pairs), (cross_far, 0), (cross_far, pairs)]
    cross_att, cross_lse = attend_fwd(False, cross_arrays, src_keys, tgt_q, pairs)
    dec_two = dec_one + sum_core(dot(cross_att, w_co)) + small_p[23]
    dec_ffn = feed_fwd(dec_two, w_d1, w_d2, 24)
    dec_out = reorder_wide(dec_ffn[3], order)

    small_grad = {}
    own_grad = {}

    def put_own(column, row):
        empty = jnp.zeros_like(row)
        own_grad[column] = jnp.where(
            first_core, jnp.concatenate([row, empty]), jnp.concatenate([empty, row])
        )

    def put_hidden(column, row):
        empty = jnp.zeros_like(row)
        low, high = jnp.where(first_core, row, empty), jnp.where(first_core, empty, row)
        for j, part in enumerate((low[:width], low[width:], high[:width], high[width:])):
            own_grad[column + j] = part

    def feed_back(resid, saved, w_in, w_out, base, gradient):
        normed, active, slope = saved[:3]
        branch = gradient.astype(BF)
        small_grad[base + 2] = jnp.sum(branch, axis=0, dtype=F32)
        branch = join_core(branch)
        grad_out = dot_t(active, branch, BF)
        grad_hidden = (dot_b(branch, w_out) * slope).astype(BF)
        put_hidden(base + 3, jnp.sum(grad_hidden, axis=0, dtype=F32))
        grad_in = dot_t(normed, grad_hidden, BF)
        grad_normed = sum_core(dot_b(grad_hidden, w_in))
        back, small_grad[base], small_grad[base + 1] = norm_back(resid, small_p[base], grad_normed)
        return gradient + back, grad_in, grad_out

    def out_back(gradient, attended, weight, column):
        branch = gradient.astype(BF)
        small_grad[column] = jnp.sum(branch, axis=0, dtype=F32)
        branch = join_core(branch)
        return dot_t(attended, branch, BF), dot_b(branch, weight, BF)

    def in_back(resid, normed, grad_proj, weight, column, gradient):
        grad_normed = sum_core(dot_b(grad_proj, weight))
        back, small_grad[column], small_grad[column + 1] = norm_back(
            resid, small_p[column], grad_normed
        )
        return gradient + back, dot_t(normed, grad_proj, BF)

    def gather_back(near_k, near_v, far_k, far_v):
        far = swap(jnp.concatenate([far_k, far_v], axis=1), "xl")
        return (jnp.concatenate([near_k, near_v], axis=1) + far).astype(BF)

    def reduce(parts):
        return lax.psum_scatter(
            jnp.concatenate(parts, axis=1), ("z", "y"), scatter_dimension=0, tiled=True
        )

    top = dot(out_cot[0], order)
    grad_two, g_d1, g_d2 = feed_back(dec_two, dec_ffn, w_d1, w_d2, 24, top)
    sum_four = reduce([g_d1] + repack_down(g_d2))

    g_co, grad_att = out_back(grad_two, cross_att, w_co, 23)
    cross_gq, ck0, cv0, ck1, cv1 = attend_back(
        False, cross_arrays, grad_att, src_keys, tgt_q, cross_lse
    )
    cross_gkv = gather_back(ck0, cv0, ck1, cv1)
    put_own(21, jnp.sum(cross_gq, axis=0, dtype=F32))
    put_own(22, jnp.sum(cross_gkv[:, half:], axis=0, dtype=F32))
    grad_one, g_cq = in_back(dec_one, cross_norm, cross_gq, w_cq, 19, grad_two)

    g_so, grad_att = out_back(grad_one, self_att, w_so, 18)
    self_gq, sk0, sv0, sk1, sv1 = attend_back(True, dec_arrays, grad_att, tgt_keys, tgt_q, self_lse)
    self_grad = jnp.concatenate([self_gq, gather_back(sk0, sv0, sk1, sv1)], axis=1)
    self_sum = jnp.sum(self_grad, axis=0, dtype=F32)
    put_own(16, self_sum[:half])
    put_own(17, self_sum[2 * half :])
    tgt_grad, g_dqkv = in_back(target, dec_norm, self_grad, w_dqkv, 14, grad_one)
    tgt_grad = reorder_wide(tgt_grad, order)

    g_ckv = dot_t(memory, cross_gkv, BF)
    sum_three = reduce([g_dqkv, g_cq, g_ckv, repack_out(g_so), repack_out(g_co)])
    grad_memory = sum_core(dot_b(cross_gkv, w_ckv))
    grad_memory = lax.reduce_precision(grad_memory, 8, 7)
    enc_grad_two, small_grad[12], small_grad[13] = norm_back(enc_two, small_p[12], grad_memory)

    enc_grad_one, g_e1, g_e2 = feed_back(enc_one, enc_ffn, w_e1, w_e2, 5, enc_grad_two)
    g_eo, grad_att = out_back(enc_grad_one, enc_att, w_eo, 4)
    spare = jnp.zeros((width, LANES), BF)
    sum_two = reduce([repack_out(g_eo), g_e1] + repack_down(g_e2) + [spare])
    enc_gq, ek0, ev0, ek1, ev1 = attend_back(False, enc_arrays, grad_att, src_keys, src_q, enc_lse)
    enc_grad = jnp.concatenate([enc_gq, gather_back(ek0, ev0, ek1, ev1)], axis=1)
    enc_sum = jnp.sum(enc_grad, axis=0, dtype=F32)
    put_own(2, enc_sum[:half])
    put_own(3, enc_sum[2 * half :])
    src_grad, g_eqkv = in_back(source, enc_norm, enc_grad, w_eqkv, 0, enc_grad_one)
    src_grad = reorder_wide(src_grad, order)

    empty = jnp.zeros((width,), F32)
    stored = jnp.stack([small_grad.get(j, empty) for j in range(LANES)]).astype(BF)
    owned = jnp.stack([own_grad.get(j, empty) for j in range(LANES)]).astype(BF)
    g_small = (dot_b(eye, stored) + lax.dot_general(
        order, owned, (((0,), (1,)), ((), ())), preferred_element_type=F32
    )).astype(BF)
    sum_one = reduce([g_eqkv, g_small])

    xh, xl = lax.axis_index("xh"), lax.axis_index("xl")

    def pick(which, low, high):
        return jnp.where(which == 0, low, high), jnp.where(which == 0, high, low)

    def sum_x(value):
        n = value.shape[0] // 2
        keep, send = pick(xh, value[:n], value[n:])
        value = keep.astype(F32) + swap(send, "xh").astype(F32)
        n = n // 2
        keep, send = pick(xl, value[:n], value[n:])
        return keep + swap(send.astype(BF), "xl").astype(F32)

    def sum_x_down(value):
        keep, send = pick(xh, value[:, :width], value[:, width:])
        value = keep.astype(F32) + swap(send, "xh").astype(F32)
        keep, send = pick(xl, value[:down_rows], value[down_rows:])
        return keep + swap(send.astype(BF), "xl").astype(F32)

    def from_cores(value):
        keep, send = pick(core, value[:rows], value[rows:])
        other = swap(send, "c")
        return pick(core, keep, other)

    def wide(low, high, start, stop):
        return [jnp.concatenate([low[:, start:stop], high[:, start:stop]], axis=1)]

    def own_columns(shards):
        shards = swap_z(jnp.concatenate(shards, axis=0))
        return reorder_wide(shards, order)

    def out_shard(value):
        return jnp.concatenate([value[:rows], value[rows:]], axis=1)

    cols = sum_x(jnp.concatenate(
        [sum_one, sum_two[:, : half + hid], sum_three, sum_four[:, :hid]], axis=1
    ))
    at_two = n_one + half
    at_three = at_two + hid
    at_four = at_three + 8 * half
    low, high = from_cores(jnp.concatenate(
        [cols[:, :n_one], cols[:, at_two : at_three + 6 * half], cols[:, at_four:]], axis=1
    ))
    outs = own_columns([
        out_shard(cols[:, n_one:at_two]),
        out_shard(cols[:, at_three + 6 * half : at_three + 7 * half]),
        out_shard(cols[:, at_three + 7 * half : at_four]),
        sum_x_down(sum_two[:, half + hid : half + hid + 2 * width]),
        sum_x_down(sum_four[:, hid:]),
    ])

    def pieces(start, count):
        result = []
        for j in range(count):
            result += wide(low, high, start + j * half, start + (j + 1) * half)
        return result

    grad_small = (low[:, n_qkv:n_one] + high[:, n_qkv:n_one])[:, :n_small]
    grad_enc = jnp.concatenate(
        pieces(0, 3) + [outs[:rows]] + wide(low, high, n_one, n_two), axis=1
    )
    grad_dec = jnp.concatenate(
        pieces(n_two, 3) + [outs[rows : 2 * rows]] + pieces(n_two + 3 * half, 3)
        + [outs[2 * rows : 3 * rows]] + wide(low, high, n_three, n_three + hid), axis=1
    )
    grad_down = jnp.concatenate(
        [outs[3 * rows : 3 * rows + down_rows], outs[3 * rows + down_rows :]], axis=1
    )

    squares = (
        jnp.sum(grad_enc * grad_enc) + jnp.sum(grad_dec * grad_dec)
        + jnp.sum(grad_down * grad_down) + jnp.sum(grad_small * grad_small)
    )
    squares = jnp.full((8, LANES), squares)
    for axis, pairs_of in (
        ("c", SWAP), ("xl", SWAP), ("xh", SWAP),
        ("y", [(0, 1), (1, 0), (2, 3), (3, 2)]), ("y", [(0, 2), (2, 0), (1, 3), (3, 1)]),
        ("z", [(0, 1), (1, 0), (2, 3), (3, 2)]), ("z", [(0, 2), (2, 0), (1, 3), (3, 1)]),
    ):
        squares = squares + lax.ppermute(squares, axis, pairs_of)
    grad_norm = jnp.sqrt(squares[0, 0])
    factor = CLIP_LEVEL / jnp.maximum(grad_norm, CLIP_LEVEL)
    enc_all = adam_step(enc_master, enc_first, enc_second, grad_enc, factor, RATE_MATRIX, DECAY_RATE)
    dec_all = adam_step(dec_master, dec_first, dec_second, grad_dec, factor, RATE_MATRIX, DECAY_RATE)
    down_all = adam_step(
        down_master, down_first, down_second, grad_down, factor, RATE_MATRIX, DECAY_RATE
    )
    small_all_new = adam_step(
        small_master, small_first, small_second, grad_small, factor, RATE_SMALL, 0.0
    )
    return (
        dec_out[None], src_grad[None], tgt_grad[None], grad_norm,
        enc_all[0], dec_all[0], down_all[0], small_all_new[0],
        enc_all[1], dec_all[1], down_all[1], small_all_new[1],
        enc_all[2], dec_all[2], down_all[2], small_all_new[2],
        grad_small * factor,
    )


def solution(mesh):
    split = Mesh(mesh.devices.reshape(4, 2, 4, 2, 2), ALL_AXES)
    tokens = P(ROW_AXES, POS_AXES, None)
    marks = P(ROW_AXES, POS_AXES)
    shard = P(ALL_AXES, None)
    in_specs = (tokens,) * 3 + (marks,) * 4 + (shard,) * 12
    out_specs = (tokens,) * 3 + (P(),) + (shard,) * 13
    return jax.shard_map(
        per_device, mesh=split, in_specs=in_specs, out_specs=out_specs, check_vma=False
    )
```

```python
import jax
import jax.numpy as jnp
import numpy as np
from jax import lax
from jax.experimental import pallas as pl
from jax.experimental.pallas import tpu as pltpu
from jax.sharding import Mesh, PartitionSpec as P

HEAD = 64
STEP = 10
NORM_EPS = 1e-05
MASKED = -1000000000.0
BETA_FIRST = 0.9
BETA_SECOND = 0.999
ADAM_EPS = 1e-08
RATE_MATRIX = 0.1
RATE_SMALL = 0.5
DECAY_RATE = 0.01
CLIP_LEVEL = 1.0
BF = jnp.bfloat16
F32 = jnp.float32
PAIR = 2 * HEAD
LANES = 128
ROW_AXES = ("z", "xh", "y")
POS_AXES = ("xl", "c")
ALL_AXES = ("z", "xh", "y", "xl", "c")
SWAP = [(0, 1), (1, 0)]


def swap(value, axis):
    return lax.ppermute(value, axis, SWAP)


def flip(value, bits):
    return lax.ppermute(value, ("xh", "xl"), [(i, i ^ bits) for i in range(4)])


def join_core(value):
    return jnp.concatenate([value, swap(value, "c")], axis=0)


def sum_core(partial):
    mine = partial.shape[0] // 2
    return partial[:mine] + swap(partial[mine:], "c")


def move_blocks(sources, specs, outs, steps):
    n = len(sources)

    def kernel(*refs):
        sems = refs[-1]
        copies = [
            pltpu.make_async_copy(refs[src].at[cut], refs[n + out].at[to], sems.at[j])
            for j, (src, cut, out, to) in enumerate(steps)
        ]
        for copy in copies:
            copy.start()
        for copy in copies:
            copy.wait()

    moved = 2 * sum(o.size * 2 for o in outs)
    return pl.pallas_call(
        kernel,
        grid=(1,),
        in_specs=specs,
        out_specs=[pl.BlockSpec(memory_space=pl.ANY)] * len(outs),
        out_shape=outs,
        scratch_shapes=[pltpu.SemaphoreType.DMA((len(steps),))],
        compiler_params=pltpu.CompilerParams(vmem_limit_bytes=56 * 1024 * 1024),
        cost_estimate=pl.CostEstimate(flops=0, bytes_accessed=moved, transcendentals=0),
    )(*sources)


def spread_down(value, half):
    n = value.shape[0] // 16

    def plan():
        steps = []
        for z in range(4):
            for y in range(4):
                for x in range(4):
                    row = ((((z % 2) * 2 + x // 2) * 4 + y) * 2 + x % 2) * n
                    stored = (pl.ds((z * 4 + y) * n, n), pl.ds(x * half, half))
                    own = (pl.ds(row, n), pl.ds((z // 2) * half, half))
                    steps.append((stored, own))
        return steps

    return plan()


def unpack_down(full, half):
    rows = full.shape[0]
    block = jax.ShapeDtypeStruct((rows, 4 * half), BF)
    steps = [(0, stored, 0, own) for stored, own in spread_down(block, half)]
    return move_blocks(
        [full], [pl.BlockSpec((rows, 4 * half), lambda i: (0, 0))],
        [jax.ShapeDtypeStruct((4 * half, 2 * half), BF)], steps,
    )[0]


def pack_grads(parts, down, half, total):
    rows = 2 * half
    sources = [down] + list(parts)
    steps = [(0, own, 0, stored) for stored, own in spread_down(jax.ShapeDtypeStruct((rows, 4 * half), BF), half)]
    at = 4 * half
    for j, part in enumerate(parts):
        n = part.shape[1]
        steps.append((j + 1, (slice(None), slice(None)), 0, (slice(None), pl.ds(at, n))))
        at += n
    specs = [pl.BlockSpec(s.shape, lambda i: (0, 0)) for s in sources]
    return move_blocks(sources, specs, [jax.ShapeDtypeStruct((rows, total), BF)], steps)[0]


def after(value, *earlier):
    return lax.optimization_barrier((value,) + earlier)[0]


def gather_x(value):
    here = lax.axis_index("xh") * 2 + lax.axis_index("xl")
    found = [value] + [flip(value, bits) for bits in (1, 2, 3)]
    result = []
    for spot in range(4):
        part = found[0]
        for bits in (1, 2, 3):
            part = jnp.where((here ^ bits) == spot, found[bits], part)
        result.append(part)
    return result


def gather_by_trade(value, axes, n):
    return lax.all_to_all(jnp.broadcast_to(value[None], (n,) + value.shape), axes, 0, 0)


def sum_by_trade(value, axes):
    return jnp.sum(lax.all_to_all(value, axes, 0, 0).astype(F32), axis=0)


def feature_order(width):
    rest = width // 32
    new = np.arange(width)
    z, y, xh, r = new // (8 * rest), (new // (2 * rest)) % 4, (new // rest) % 2, new % rest
    return ((z * 2 + xh) * 4 + y) * rest + r


def head_order(width):
    r = width // 64
    own = np.arange(width // 2)
    zz, xh = own // (16 * r), (own // (8 * r)) % 2
    y, xl, i = (own // (2 * r)) % 4, (own // r) % 2, own % r
    places = []
    for cols in range(2):
        places.append((((cols * 2 + zz) * 4 + y) * 4 + xh * 2 + xl) * r + i)
    return np.concatenate(places)


def one_hot(picks, width):
    rows = lax.broadcasted_iota(jnp.int32, (width, len(picks)), 0)
    return (rows == jnp.asarray(picks, jnp.int32)[None, :]).astype(BF)


def dot(left, right, kind=F32):
    return jnp.dot(left, right, preferred_element_type=kind)


def dot_t(left, right, kind=F32):
    return lax.dot_general(left, right, (((0,), (0,)), ((), ())), preferred_element_type=kind)


def dot_b(left, right, kind=F32):
    return lax.dot_general(left, right, (((1,), (1,)), ((), ())), preferred_element_type=kind)


def two_parts(value):
    high = lax.reduce_precision(value, 8, 7)
    return high.astype(BF), (value - high).astype(BF)


def reorder_wide(value, order):
    high, low = two_parts(value)
    both = dot_b(jnp.concatenate([high, low], axis=0), order)
    return both[: value.shape[0]] + both[value.shape[0] :]


def norm_stats(x):
    center = x - jnp.mean(x, axis=-1, keepdims=True)
    spread = jnp.mean(center * center, axis=-1, keepdims=True)
    scale = lax.rsqrt(spread + NORM_EPS)
    return center * scale, scale


def norm(x, gain, shift):
    unit, scale = norm_stats(x)
    return (unit * gain + shift).astype(BF)


def norm_back(x, gain, gradient):
    unit, scale = norm_stats(x)
    inner = gradient * gain
    back = scale * (
        inner
        - jnp.mean(inner, axis=-1, keepdims=True)
        - unit * jnp.mean(inner * unit, axis=-1, keepdims=True)
    )
    return back, jnp.sum(gradient * unit, axis=0), jnp.sum(gradient, axis=0)


def gelu_parts(u):
    cdf = 0.5 * (1.0 + lax.erf(u * (0.5**0.5)))
    pdf = jnp.exp(-0.5 * u * u) * (1.0 / np.sqrt(2.0 * np.pi)).astype(np.float32)
    return u * cdf, cdf + u * pdf


def lane_mask(value, which):
    lane = lax.broadcasted_iota(jnp.int32, value.shape, 1)
    return jnp.where((lane // HEAD) == which, value, jnp.zeros_like(value))


def allowed_of(causal, ids_ref, qid_ref, part):
    seg = ids_ref[part, :, 0:1] == qid_ref[0:1, :]
    if causal:
        seg = seg & (ids_ref[part, :, 1:2] <= qid_ref[1:2, :])
    return seg


def scores_t(keys, query, allowed):
    raw = lax.dot_general(keys, query, (((1,), (1,)), ((), ())), preferred_element_type=F32)
    return jnp.where(allowed, raw, MASKED)


def attend_kernel(causal, q_ref, k0_ref, v0_ref, k1_ref, v1_ref, ids_ref, qid_ref, o_ref, lse_ref):
    query = q_ref[...] * jnp.asarray(HEAD**-0.5, BF)
    allowed = [allowed_of(causal, ids_ref, qid_ref, part) for part in range(2)]
    mixed = []
    for head in range(2):
        one = lane_mask(query, head)
        scores = [scores_t(ref[...], one, ok) for ref, ok in zip((k0_ref, k1_ref), allowed)]
        top = jnp.maximum(
            jnp.max(scores[0], axis=0, keepdims=True), jnp.max(scores[1], axis=0, keepdims=True)
        )
        expo = [jnp.exp(s - top) for s in scores]
        total = jnp.sum(expo[0], axis=0, keepdims=True) + jnp.sum(expo[1], axis=0, keepdims=True)
        share = 1.0 / total
        out = 0.0
        for ref, e in zip((v0_ref, v1_ref), expo):
            out = out + lax.dot_general(
                ref[...], (e * share).astype(BF), (((0,), (0,)), ((), ())), preferred_element_type=F32
            )
        mixed.append(out)
        lse_ref[0, head : head + 1, :] = top + jnp.log(total)
    both = jnp.concatenate([mixed[0][:HEAD], mixed[1][HEAD:]], axis=0)
    o_ref[...] = both.T.astype(BF)


def attend_back_kernel(
    causal, q_ref, k0_ref, v0_ref, k1_ref, v1_ref, g_ref, ids_ref, qid_ref, lse_ref,
    dq_ref, dk0_ref, dv0_ref, dk1_ref, dv1_ref,
):
    query = q_ref[...] * jnp.asarray(HEAD**-0.5, BF)
    grad = g_ref[...]
    allowed = [allowed_of(causal, ids_ref, qid_ref, part) for part in range(2)]
    keys = (k0_ref[...], k1_ref[...])
    values = (v0_ref[...], v1_ref[...])
    grad_q = 0.0
    grad_k = [0.0, 0.0]
    grad_v = [0.0, 0.0]
    for head in range(2):
        one = lane_mask(query, head)
        grad_one = lane_mask(grad, head)
        lse = lse_ref[0, head : head + 1, :]
        probs = [jnp.exp(scores_t(k, one, ok) - lse) for k, ok in zip(keys, allowed)]
        grad_p = [
            lax.dot_general(v, grad_one, (((1,), (1,)), ((), ())), preferred_element_type=F32)
            for v in values
        ]
        inner = jnp.sum(probs[0] * grad_p[0], axis=0, keepdims=True) + jnp.sum(
            probs[1] * grad_p[1], axis=0, keepdims=True
        )
        for part in range(2):
            grad_s = (probs[part] * (grad_p[part] - inner)).astype(BF)
            grad_v[part] = grad_v[part] + dot(probs[part].astype(BF), grad_one)
            grad_k[part] = grad_k[part] + dot(grad_s, one)
            grad_q = grad_q + lax.dot_general(
                lane_mask(keys[part], head), grad_s, (((0,), (0,)), ((), ())),
                preferred_element_type=F32,
            )
    dq_ref[...] = (grad_q * HEAD**-0.5).T.astype(BF)
    dk0_ref[...] = grad_k[0]
    dv0_ref[...] = grad_v[0]
    dk1_ref[...] = grad_k[1].astype(BF)
    dv1_ref[...] = grad_v[1].astype(BF)


def call_kernel(body, causal, arrays, ids, qid, extra, out_shape, out_specs, cost):
    in_specs = [
        pl.BlockSpec((a.shape[0], PAIR), lambda p, at=at: (0, at + p)) for a, at in arrays
    ]
    in_specs.append(pl.BlockSpec(ids.shape, lambda p: (0, 0, 0)))
    in_specs.append(pl.BlockSpec(qid.shape, lambda p: (0, 0)))
    in_specs += [pl.BlockSpec((1,) + e.shape[1:], lambda p: (p, 0, 0)) for e in extra]

    def kernel(*refs):
        body(causal, *refs)

    pairs = extra[0].shape[0] if extra else out_shape[1].shape[0]
    return pl.pallas_call(
        kernel,
        grid=(pairs,),
        in_specs=in_specs,
        out_specs=out_specs,
        out_shape=out_shape,
        compiler_params=pltpu.CompilerParams(vmem_limit_bytes=56 * 1024 * 1024),
        cost_estimate=cost,
    )(*[a for a, at in arrays], ids, qid, *extra)


def cost_of(n_q, n_k, width, products):
    return pl.CostEstimate(
        flops=4 * 2 * products * n_q * n_k * width,
        bytes_accessed=4 * (n_q + n_k) * width,
        transcendentals=n_q * n_k * width // HEAD,
    )


def attend_fwd(causal, arrays, ids, qid, pairs):
    n_q = qid.shape[1]
    out_shape = (
        jax.ShapeDtypeStruct((n_q, pairs * PAIR), BF),
        jax.ShapeDtypeStruct((pairs, 2, n_q), F32),
    )
    out_specs = (
        pl.BlockSpec((n_q, PAIR), lambda p: (0, p)),
        pl.BlockSpec((1, 2, n_q), lambda p: (p, 0, 0)),
    )
    return call_kernel(
        attend_kernel, causal, arrays, ids, qid, (), out_shape, out_specs,
        cost_of(n_q, 2 * ids.shape[1], pairs * PAIR, 2),
    )


def attend_back(causal, arrays, grad, ids, qid, lse):
    pairs, n_q, n_k = lse.shape[0], qid.shape[1], ids.shape[1]
    wide = pairs * PAIR
    out_shape = (
        jax.ShapeDtypeStruct((n_q, wide), BF),
        jax.ShapeDtypeStruct((n_k, wide), F32),
        jax.ShapeDtypeStruct((n_k, wide), F32),
        jax.ShapeDtypeStruct((n_k, wide), BF),
        jax.ShapeDtypeStruct((n_k, wide), BF),
    )
    out_specs = tuple(pl.BlockSpec((s.shape[0], PAIR), lambda p: (0, p)) for s in out_shape)
    return call_kernel(
        attend_back_kernel, causal, list(arrays) + [(grad, 0)], ids, qid, (lse,), out_shape, out_specs,
        cost_of(n_q, 2 * n_k, wide, 5),
    )


def adam_step(master, first, second, gradient, factor, rate, decay):
    clipped = gradient * factor
    first_new = BETA_FIRST * first + (1 - BETA_FIRST) * clipped
    second_new = BETA_SECOND * second + (1 - BETA_SECOND) * clipped * clipped
    first_hat = first_new / (1 - BETA_FIRST**STEP)
    second_hat = second_new / (1 - BETA_SECOND**STEP)
    master_new = master - rate * (first_hat / (jnp.sqrt(second_hat) + ADAM_EPS) + decay * master)
    return (master_new, first_new, second_new)


def per_device(
    src_x, tgt_x, out_cot, src_seg, tgt_seg, src_pad, tgt_pad,
    enc_master, dec_master, down_master, small_master,
    enc_first, dec_first, down_first, small_first,
    enc_second, dec_second, down_second, small_second,
):
    width = src_x.shape[-1]
    half = width // 2
    hid = 2 * width
    pairs = half // PAIR
    rows = enc_master.shape[0]
    down_rows = down_master.shape[0]
    n_small = small_master.shape[1]
    core = lax.axis_index("c")
    first_core = core == 0
    order = one_hot(feature_order(width), width)
    place = one_hot(head_order(width), width)

    encb, decb, downb = enc_master.astype(BF), dec_master.astype(BF), down_master.astype(BF)
    smallb = jnp.pad(small_master.astype(BF), ((0, 0), (0, LANES - n_small)))

    def block(matrix, index):
        return matrix[:, index * width : (index + 1) * width]

    def halves(matrix):
        n = matrix.shape[1] // 2
        return matrix[:, :n], matrix[:, n:]

    col_blocks = [
        halves(block(encb, 0)), halves(block(encb, 1)), halves(block(encb, 2)), (smallb, smallb),
        halves(encb[:, 4 * width :]), halves(block(decb, 5)), halves(block(decb, 6)),
        halves(block(decb, 0)), halves(block(decb, 1)), halves(block(decb, 2)), halves(block(decb, 4)),
        halves(decb[:, 8 * width :]),
    ]
    cols0 = jnp.concatenate([b[0] for b in col_blocks], axis=1)
    cols1 = jnp.concatenate([b[1] for b in col_blocks], axis=1)
    mine = jnp.where(first_core, cols0, cols1)
    theirs = swap(jnp.where(first_core, cols1, cols0), "c")
    cols = jnp.concatenate(
        [jnp.where(first_core, mine, theirs), jnp.where(first_core, theirs, mine)], axis=0
    )
    n_qkv, n_one = 3 * half, 3 * half + LANES
    n_two, n_three = n_one + hid + 2 * half, n_one + hid + 6 * half
    cols = gather_by_trade(cols, ("xh", "xl"), 4).reshape(8 * rows, cols.shape[1])

    z_half = lax.axis_index("z") // 2
    active = z_half == core
    row_shard = dot(jnp.concatenate(
        [block(encb, 3), downb[:, :width], block(decb, 3), block(decb, 7), downb[:, width:]], axis=0
    ), order, BF)
    other = swap(row_shard, "c")
    row_shard = jnp.stack([
        jnp.where(first_core, row_shard, other), jnp.where(first_core, other, row_shard)
    ])
    low, high = row_shard[..., :half], row_shard[..., half:]
    kept = jnp.where(z_half == 0, low, high)
    sent = jnp.where(z_half == 0, high, low)
    row_shard = jnp.where(
        active, kept, lax.ppermute(sent, ("z", "c"), [(0, 4), (2, 6), (5, 1), (7, 3)])
    )
    row_shard = jnp.stack(gather_x(row_shard))

    def pack_out(at):
        return row_shard[:, :, at : at + rows].reshape(8 * rows, half)

    def pack_down(at):
        part = row_shard[:, :, at : at + down_rows].reshape(4, 2 * down_rows, half)
        return [part[j] for j in range(4)]

    dec_rows = rows + down_rows
    shard_one = cols[:, :n_one]
    shard_two = jnp.concatenate(
        pack_down(rows) + [cols[:, n_one:n_three]]
        + [pack_out(0), pack_out(dec_rows), pack_out(dec_rows + rows)], axis=1
    )
    shard_three = jnp.concatenate(pack_down(dec_rows + 2 * rows) + [cols[:, n_three:]], axis=1)
    full_two, full_three = [
        lax.all_gather(shard, ("z", "y"), axis=0, tiled=True) for shard in (shard_two, shard_three)
    ]
    full_one = gather_by_trade(shard_one, ("z", "y"), 16).reshape(width, n_one)

    def cut(full, *counts):
        starts = [int(v) for v in np.cumsum((hid,) + counts)]
        return [full[:, a:b] for a, b in zip(starts[:-1], starts[1:])]

    w_eqkv, small_all = full_one[:, :n_qkv], full_one[:, n_qkv:]
    w_e1, w_ckv, w_dqkv, w_cq, w_eo, w_so, w_co = cut(full_two, hid, 2 * half, n_qkv, half, half, half, half)
    w_d1 = full_three[:, hid:]
    w_e2, w_d2 = unpack_down(full_two, half), unpack_down(full_three, half)

    def unpack_out(part):
        natural = dot_t(place, part, BF)
        return jnp.concatenate([natural[:half], natural[half:]], axis=1)

    def repack_out(grad):
        stacked = jnp.concatenate([grad[:, :half], grad[:, half:]], axis=0)
        return dot(place, stacked, BF)

    w_eo, w_so, w_co = unpack_out(w_eo), unpack_out(w_so), unpack_out(w_co)

    eye = one_hot(np.arange(width), width)
    small_p = dot_t(small_all, eye)
    small_own = dot_b(small_all.T, order)

    def own_half(column):
        row = small_own[column]
        return jnp.where(first_core, row[:half], row[half:])

    def hidden_bias(column):
        low = jnp.concatenate([small_own[column], small_own[column + 1]])
        high = jnp.concatenate([small_own[column + 2], small_own[column + 3]])
        return jnp.where(first_core, low, high)

    none = jnp.zeros((half,), F32)

    def ids_of(seg, pad, at):
        n = seg.shape[1]
        spot = (lax.axis_index("xl") * 2 + core) * n + jnp.arange(n, dtype=jnp.int32)
        key = jnp.where(pad[0] == 1, seg[0], -1)
        return jnp.stack([key, spot, seg[0]], axis=1)

    src_ids = join_core(ids_of(src_seg, src_pad, 0))
    tgt_ids = join_core(ids_of(tgt_seg, tgt_pad, 0))
    src_keys = jnp.stack([src_ids[:, :2], swap(src_ids[:, :2], "xl")])
    tgt_keys = jnp.stack([tgt_ids[:, :2], swap(tgt_ids[:, :2], "xl")])
    src_q = jnp.stack([src_ids[:, 2], src_ids[:, 1]])
    tgt_q = jnp.stack([tgt_ids[:, 2], tgt_ids[:, 1]])

    source = dot(src_x[0], order)
    enc_norm = join_core(norm(source, small_p[0], small_p[1]))
    enc_qkv = (dot(enc_norm, w_eqkv) + jnp.concatenate([own_half(2), none, own_half(3)])).astype(BF)
    enc_far = swap(enc_qkv[:, half:], "xl")
    enc_arrays = [(enc_qkv, 0), (enc_qkv, pairs), (enc_qkv, 2 * pairs), (enc_far, 0), (enc_far, pairs)]

    target = dot(tgt_x[0], order)
    dec_norm = join_core(norm(target, small_p[14], small_p[15]))

    enc_att, enc_lse = attend_fwd(False, enc_arrays, src_keys, src_q, pairs)
    enc_one = source + sum_core(dot(enc_att, w_eo)) + small_p[4]

    def feed_fwd(resid, w_in, w_out, small_p, base):
        normed = join_core(norm(resid, small_p[base], small_p[base + 1]))
        active, slope = gelu_parts(dot(normed, w_in) + hidden_bias(base + 3))
        active = active.astype(BF)
        return normed, active, slope, resid + sum_core(dot(active, w_out)) + small_p[base + 2]

    enc_ffn = feed_fwd(enc_one, w_e1, w_e2, small_p, 5)
    enc_two = enc_ffn[3]
    memory = join_core(norm(enc_two, small_p[12], small_p[13]))

    dec_qkv = (dot(dec_norm, w_dqkv) + jnp.concatenate([own_half(16), none, own_half(17)])).astype(BF)
    dec_far = swap(dec_qkv[:, half:], "xl")
    dec_arrays = [(dec_qkv, 0), (dec_qkv, pairs), (dec_qkv, 2 * pairs), (dec_far, 0), (dec_far, pairs)]
    self_att, self_lse = attend_fwd(True, dec_arrays, tgt_keys, tgt_q, pairs)
    dec_one = target + sum_core(dot(self_att, w_so)) + small_p[18]
    cross_norm = join_core(norm(dec_one, small_p[19], small_p[20]))
    cross_q = (dot(cross_norm, w_cq) + own_half(21)).astype(BF)
    cross_kv = (dot(memory, w_ckv) + jnp.concatenate([none, own_half(22)])).astype(BF)
    cross_far = swap(cross_kv, "xl")
    cross_arrays = [(cross_q, 0), (cross_kv, 0), (cross_kv, pairs), (cross_far, 0), (cross_far, pairs)]
    cross_att, cross_lse = attend_fwd(False, cross_arrays, src_keys, tgt_q, pairs)
    dec_two = dec_one + sum_core(dot(cross_att, w_co)) + small_p[23]
    dec_ffn = feed_fwd(dec_two, w_d1, w_d2, small_p, 24)
    dec_out = reorder_wide(dec_ffn[3], order)

    small_grad = {}
    own_grad = {}

    def put_own(column, row):
        empty = jnp.zeros_like(row)
        own_grad[column] = jnp.where(
            first_core, jnp.concatenate([row, empty]), jnp.concatenate([empty, row])
        )

    def put_hidden(column, row):
        empty = jnp.zeros_like(row)
        low, high = jnp.where(first_core, row, empty), jnp.where(first_core, empty, row)
        for j, part in enumerate((low[:width], low[width:], high[:width], high[width:])):
            own_grad[column + j] = part

    def feed_back(resid, saved, w_in, w_out, small_p, base, gradient):
        normed, active, slope = saved[:3]
        branch = gradient.astype(BF)
        small_grad[base + 2] = jnp.sum(branch, axis=0, dtype=F32)
        branch = join_core(branch)
        grad_out = dot_t(active, branch, BF)
        grad_hidden = (dot_b(branch, w_out) * slope).astype(BF)
        put_hidden(base + 3, jnp.sum(grad_hidden, axis=0, dtype=F32))
        grad_in = dot_t(normed, grad_hidden, BF)
        grad_normed = sum_core(dot_b(grad_hidden, w_in))
        back, small_grad[base], small_grad[base + 1] = norm_back(resid, small_p[base], grad_normed)
        return gradient + back, grad_in, grad_out

    def out_back(gradient, attended, weight, column):
        branch = gradient.astype(BF)
        small_grad[column] = jnp.sum(branch, axis=0, dtype=F32)
        branch = join_core(branch)
        return dot_t(attended, branch, BF), dot_b(branch, weight, BF)

    def in_back(resid, normed, grad_proj, weight, small_p, column, gradient):
        grad_normed = sum_core(dot_b(grad_proj, weight))
        back, small_grad[column], small_grad[column + 1] = norm_back(
            resid, small_p[column], grad_normed
        )
        return gradient + back, dot_t(normed, grad_proj, BF)

    def gather_back(near_k, near_v, far_k, far_v, *earlier):
        far = swap(jnp.concatenate([far_k, far_v], axis=1), "xl")
        far = after(far, *earlier)
        return (jnp.concatenate([near_k, near_v], axis=1) + far).astype(BF)

    def reduce(value):
        return lax.psum_scatter(value, ("z", "y"), scatter_dimension=0, tiled=True)

    top = dot(out_cot[0], order)
    grad_two, g_d1, g_d2 = feed_back(dec_two, dec_ffn, w_d1, w_d2, small_p, 24, top)
    sum_dec = reduce(pack_grads([g_d1], g_d2, half, 2 * hid))

    g_co, grad_att = out_back(grad_two, cross_att, w_co, 23)
    cross_gq, ck0, cv0, ck1, cv1 = attend_back(
        False, cross_arrays, grad_att, src_keys, tgt_q, cross_lse
    )
    put_own(21, jnp.sum(cross_gq, axis=0, dtype=F32))
    grad_one, g_cq = in_back(dec_one, cross_norm, cross_gq, w_cq, small_p, 19, grad_two)

    g_so, grad_att = out_back(grad_one, self_att, w_so, 18)
    self_gq, sk0, sv0, sk1, sv1 = attend_back(True, dec_arrays, grad_att, tgt_keys, tgt_q, self_lse)
    cross_gkv = gather_back(ck0, cv0, ck1, cv1, self_gq[0, 0])
    put_own(22, jnp.sum(cross_gkv[:, half:], axis=0, dtype=F32))
    self_grad = jnp.concatenate([self_gq, gather_back(sk0, sv0, sk1, sv1)], axis=1)
    self_sum = jnp.sum(self_grad, axis=0, dtype=F32)
    put_own(16, self_sum[:half])
    put_own(17, self_sum[2 * half :])
    tgt_grad, g_dqkv = in_back(target, dec_norm, self_grad, w_dqkv, small_p, 14, grad_one)
    tgt_grad = reorder_wide(tgt_grad, order)

    g_ckv = dot_t(memory, cross_gkv, BF)
    grad_memory = sum_core(dot_b(cross_gkv, w_ckv))
    grad_memory = lax.reduce_precision(grad_memory, 8, 7)
    enc_grad_two, small_grad[12], small_grad[13] = norm_back(enc_two, small_p[12], grad_memory)

    enc_grad_one, g_e1, g_e2 = feed_back(enc_one, enc_ffn, w_e1, w_e2, small_p, 5, enc_grad_two)
    g_eo, grad_att = out_back(enc_grad_one, enc_att, w_eo, 4)
    rest = [g_e1, g_ckv, g_dqkv, g_cq, repack_out(g_eo), repack_out(g_so), repack_out(g_co)]
    n_rest = 2 * hid + 9 * half
    sum_rest = reduce(pack_grads(rest, g_e2, half, n_rest + n_rest % (2 * LANES)))
    enc_gq, ek0, ev0, ek1, ev1 = attend_back(False, enc_arrays, grad_att, src_keys, src_q, enc_lse)
    enc_grad = jnp.concatenate([enc_gq, gather_back(ek0, ev0, ek1, ev1)], axis=1)
    enc_sum = jnp.sum(enc_grad, axis=0, dtype=F32)
    put_own(2, enc_sum[:half])
    put_own(3, enc_sum[2 * half :])
    src_grad, g_eqkv = in_back(source, enc_norm, enc_grad, w_eqkv, small_p, 0, enc_grad_one)
    src_grad = reorder_wide(src_grad, order)

    def stacked(rows_of):
        spot = lax.broadcasted_iota(jnp.int32, (LANES, width), 0)
        total = jnp.zeros((LANES, width), F32)
        for column, row in rows_of.items():
            total = jnp.where(spot == column, row[None], total)
        return total

    stored, owned = stacked(small_grad), stacked(own_grad)
    g_small = (dot_b(eye, stored.astype(BF)) + lax.dot_general(
        order, owned.astype(BF), (((0,), (1,)), ((), ())), preferred_element_type=F32
    )).astype(BF)
    sum_one = jnp.concatenate([g_eqkv, g_small], axis=1).reshape(16, 8 * rows, n_one)
    sum_one = sum_by_trade(sum_one, ("z", "y")).astype(BF)

    def pick(which, low, high):
        return jnp.where(which, low, high), jnp.where(which, high, low)

    def from_cores(value):
        keep, send = pick(first_core, value[:rows], value[rows:])
        other = swap(send, "c")
        return pick(first_core, keep, other)

    def wide(low, high, start, stop):
        return [jnp.concatenate([low[:, start:stop], high[:, start:stop]], axis=1)]

    def pieces(low, high, start, count):
        result = []
        for j in range(count):
            result += wide(low, high, start + j * half, start + (j + 1) * half)
        return result

    def by_x(part, n_down):
        return part[:, n_down:].reshape(4, 2 * rows, part.shape[1] - n_down)

    def by_x_down(part):
        part = part[:, :hid].reshape(4, 2 * rows, 4, half)
        return part.transpose(2, 1, 0, 3).reshape(4, 2 * rows, hid)

    last = sum_by_trade(jnp.concatenate([
        by_x(sum_rest[:, :n_rest], hid), by_x(sum_dec, hid), by_x_down(sum_rest), by_x_down(sum_dec),
        sum_one.reshape(4, 2 * rows, n_one),
    ], axis=2), ("xh", "xl"))
    sizes = (hid, 2 * half, n_qkv, half, half, half, half, hid, hid, hid, n_one)
    starts = [int(v) for v in np.cumsum((0,) + sizes)]
    s_e1, s_ckv, s_dqkv, s_cq, s_eo, s_so, s_co, s_d1, s_e2, s_d2, s_one = [
        last[:, a:b] for a, b in zip(starts[:-1], starts[1:])
    ]

    def down_shard(part):
        return part.reshape(2 * rows, 4, half).transpose(1, 0, 2).reshape(8 * rows, half)

    by_rows = [s_eo, down_shard(s_e2), s_so, s_co, down_shard(s_d2)]
    by_rows = jnp.stack([
        jnp.concatenate([p[: p.shape[0] // 2] for p in by_rows], axis=0),
        jnp.concatenate([p[p.shape[0] // 2 :] for p in by_rows], axis=0),
    ])
    other = lax.ppermute(by_rows, ("z", "c"), [(4, 0), (6, 2), (1, 5), (3, 7)])
    low, high = pick(z_half == 0, by_rows, other)
    by_rows = jnp.concatenate([low, high], axis=2)
    mine = jnp.where(first_core, by_rows[0], by_rows[1])
    other = swap(jnp.where(first_core, by_rows[1], by_rows[0]), "c")
    by_rows = jnp.where(active, mine, other)
    by_rows = reorder_wide(by_rows, order)
    outs_e, outs_d = by_rows[:dec_rows], by_rows[dec_rows:]

    low, high = from_cores(jnp.concatenate([s_e1, s_ckv, s_dqkv, s_cq, s_d1], axis=1))
    low_one, high_one = from_cores(s_one)

    grad_small = (low_one[:, n_qkv:] + high_one[:, n_qkv:])[:, :n_small]
    grad_enc = jnp.concatenate(
        pieces(low_one, high_one, 0, 3) + [outs_e[:rows]] + wide(low, high, 0, hid), axis=1
    )
    at = hid + 2 * half
    grad_dec = jnp.concatenate(
        pieces(low, high, at, 3) + [outs_d[:rows]] + pieces(low, high, at + 3 * half, 1)
        + pieces(low, high, hid, 2) + [outs_d[rows : 2 * rows]]
        + wide(low, high, at + 4 * half, at + 4 * half + hid), axis=1
    )
    grad_down = jnp.concatenate([outs_e[rows:], outs_d[2 * rows :]], axis=1)

    lasts = last[:, : starts[-2]], s_one[:, :n_qkv], grad_small
    squares = sum(jnp.sum(part * part) for part in lasts)
    squares = jnp.full((8, LANES), squares)
    squares = squares + swap(squares, "c")
    squares = jnp.sum(gather_by_trade(squares, ("z", "xh", "y", "xl"), 64), axis=0)
    grad_norm = jnp.sqrt(squares[0, 0])
    factor = CLIP_LEVEL / jnp.maximum(grad_norm, CLIP_LEVEL)
    enc_all = adam_step(enc_master, enc_first, enc_second, grad_enc, factor, RATE_MATRIX, DECAY_RATE)
    dec_all = adam_step(dec_master, dec_first, dec_second, grad_dec, factor, RATE_MATRIX, DECAY_RATE)
    down_all = adam_step(
        down_master, down_first, down_second, grad_down, factor, RATE_MATRIX, DECAY_RATE
    )
    small_all_new = adam_step(
        small_master, small_first, small_second, grad_small, factor, RATE_SMALL, 0.0
    )
    return (
        dec_out[None], src_grad[None], tgt_grad[None], grad_norm,
        enc_all[0], dec_all[0], down_all[0], small_all_new[0],
        enc_all[1], dec_all[1], down_all[1], small_all_new[1],
        enc_all[2], dec_all[2], down_all[2], small_all_new[2],
        grad_small * factor,
    )


def solution(mesh):
    split = Mesh(mesh.devices.reshape(4, 2, 4, 2, 2), ALL_AXES)
    tokens = P(ROW_AXES, POS_AXES, None)
    marks = P(ROW_AXES, POS_AXES)
    shard = P(ALL_AXES, None)
    in_specs = (tokens,) * 3 + (marks,) * 4 + (shard,) * 12
    out_specs = (tokens,) * 3 + (P(),) + (shard,) * 13
    return jax.shard_map(
        per_device, mesh=split, in_specs=in_specs, out_specs=out_specs, check_vma=False
    )
```

```python
import jax
import jax.numpy as jnp
import numpy as np
from jax import lax
from jax.experimental import pallas as pl
from jax.experimental.pallas import tpu as pltpu
from jax.sharding import Mesh, PartitionSpec as P

HEAD = 64
STEP = 10
NORM_EPS = 1e-05
MASKED = -1000000000.0
BETA_FIRST = 0.9
BETA_SECOND = 0.999
ADAM_EPS = 1e-08
RATE_MATRIX = 0.1
RATE_SMALL = 0.5
DECAY_RATE = 0.01
CLIP_LEVEL = 1.0
BF = jnp.bfloat16
F32 = jnp.float32
PAIR = 2 * HEAD
LANES = 128
ROW_AXES = ("z", "xh", "y")
POS_AXES = ("xl", "c")
ALL_AXES = ("z", "xh", "y", "xl", "c")
SWAP = [(0, 1), (1, 0)]


def swap(value, axis):
    return lax.ppermute(value, axis, SWAP)


def flip(value, bits):
    return lax.ppermute(value, ("xh", "xl"), [(i, i ^ bits) for i in range(4)])


def join_core(value):
    return jnp.concatenate([value, swap(value, "c")], axis=0)


def sum_core(partial):
    mine = partial.shape[0] // 2
    return partial[:mine] + swap(partial[mine:], "c")


def after(value, earlier):
    one = lax.slice(earlier, (0,) * earlier.ndim, (1,) * earlier.ndim)
    return value + one.reshape(()).astype(value.dtype) * 0


def scatter_x(values):
    here = lax.axis_index("xh") * 2 + lax.axis_index("xl")

    def piece(spot):
        return jnp.concatenate(
            [lax.dynamic_index_in_dim(value, spot, 0, keepdims=False) for value in values], axis=1
        )

    total = piece(here).astype(F32)
    for bits in (1, 2, 3):
        total = total + flip(piece(here ^ bits), bits).astype(F32)
    return total


def gather_by_trade(value, axes, n):
    return lax.all_to_all(jnp.broadcast_to(value[None], (n,) + value.shape), axes, 0, 0)


def sum_by_trade(value, axes):
    return jnp.sum(lax.all_to_all(value, axes, 0, 0).astype(F32), axis=0)


def feature_order(width):
    rest = width // 32
    new = np.arange(width)
    z, y, xh, r = new // (8 * rest), (new // (2 * rest)) % 4, (new // rest) % 2, new % rest
    return ((z * 2 + xh) * 4 + y) * rest + r


def hidden_order(width):
    n = width // 64
    new = np.arange(width)
    c, g, y = new // (32 * n), (new // (16 * n)) % 2, (new // (4 * n)) % 4
    xh, xl, i = (new // (2 * n)) % 2, (new // n) % 2, new % n
    return ((((xh * 4 + y) * 2 + xl) * 2 + c) * 2 + g) * n + i


def head_order(width, core):
    r = width // 128
    own = np.arange(width // 2)
    z, xh = own // (32 * r), (own // (16 * r)) % 2
    y, xl, c, i = (own // (4 * r)) % 4, (own // (2 * r)) % 2, (own // r) % 2, own % r
    return np.concatenate([
        (c != core) * (width // 2) + ((((z * 4 + y) * 2 + xh) * 2 + xl) * 2 + cols) * r + i
        for cols in range(2)
    ])


def one_hot(picks, width):
    rows = lax.broadcasted_iota(jnp.int32, (width, picks.shape[0]), 0)
    return (rows == jnp.asarray(picks, jnp.int32)[None, :]).astype(BF)


def dot(left, right, kind=F32):
    return jnp.dot(left, right, preferred_element_type=kind)


def dot_t(left, right, kind=F32):
    return lax.dot_general(left, right, (((0,), (0,)), ((), ())), preferred_element_type=kind)


def dot_b(left, right, kind=F32):
    return lax.dot_general(left, right, (((1,), (1,)), ((), ())), preferred_element_type=kind)


def two_parts(value):
    high = lax.reduce_precision(value, 8, 7)
    return high.astype(BF), (value - high).astype(BF)


def reorder_wide(value, order):
    high, low = two_parts(value)
    both = dot_b(jnp.concatenate([high, low], axis=0), order)
    return both[: value.shape[0]] + both[value.shape[0] :]


def norm_stats(x):
    center = x - jnp.mean(x, axis=-1, keepdims=True)
    spread = jnp.mean(center * center, axis=-1, keepdims=True)
    scale = lax.rsqrt(spread + NORM_EPS)
    return center * scale, scale


def norm(x, gain, shift):
    unit, scale = norm_stats(x)
    return (unit * gain + shift).astype(BF)


def norm_back(x, gain, gradient):
    unit, scale = norm_stats(x)
    inner = gradient * gain
    back = scale * (
        inner
        - jnp.mean(inner, axis=-1, keepdims=True)
        - unit * jnp.mean(inner * unit, axis=-1, keepdims=True)
    )
    return (
        back,
        jnp.sum(gradient * unit, axis=0, keepdims=True),
        jnp.sum(gradient, axis=0, keepdims=True),
    )


def gelu_parts(u):
    cdf = 0.5 * (1.0 + lax.erf(u * (0.5**0.5)))
    pdf = jnp.exp(-0.5 * u * u) * (1.0 / np.sqrt(2.0 * np.pi)).astype(np.float32)
    return u * cdf, cdf + u * pdf


def lane_mask(value, which):
    lane = lax.broadcasted_iota(jnp.int32, value.shape, 1)
    return jnp.where((lane // HEAD) == which, value, jnp.zeros_like(value))


def allowed_of(causal, ids_ref, qid_ref, part):
    seg = ids_ref[part, :, 0:1] == qid_ref[0:1, :]
    if causal:
        seg = seg & (ids_ref[part, :, 1:2] <= qid_ref[1:2, :])
    return seg


def scores_t(keys, query, allowed):
    raw = lax.dot_general(keys, query, (((1,), (1,)), ((), ())), preferred_element_type=F32)
    return jnp.where(allowed, raw, MASKED)


def attend_kernel(causal, q_ref, k0_ref, v0_ref, k1_ref, v1_ref, ids_ref, qid_ref, o_ref, lse_ref):
    query = q_ref[...] * jnp.asarray(HEAD**-0.5, BF)
    allowed = [allowed_of(causal, ids_ref, qid_ref, part) for part in range(2)]
    mixed = []
    for head in range(2):
        one = lane_mask(query, head)
        scores = [scores_t(ref[...], one, ok) for ref, ok in zip((k0_ref, k1_ref), allowed)]
        top = jnp.maximum(
            jnp.max(scores[0], axis=0, keepdims=True), jnp.max(scores[1], axis=0, keepdims=True)
        )
        expo = [jnp.exp(s - top) for s in scores]
        total = jnp.sum(expo[0], axis=0, keepdims=True) + jnp.sum(expo[1], axis=0, keepdims=True)
        share = 1.0 / total
        out = 0.0
        for ref, e in zip((v0_ref, v1_ref), expo):
            out = out + lax.dot_general(
                ref[...], (e * share).astype(BF), (((0,), (0,)), ((), ())), preferred_element_type=F32
            )
        mixed.append(out)
        lse_ref[0, head : head + 1, :] = top + jnp.log(total)
    both = jnp.concatenate([mixed[0][:HEAD], mixed[1][HEAD:]], axis=0)
    o_ref[...] = both.T.astype(BF)


def attend_back_kernel(
    causal, q_ref, k0_ref, v0_ref, k1_ref, v1_ref, g_ref, ids_ref, qid_ref, lse_ref,
    dq_ref, dk0_ref, dv0_ref, dk1_ref, dv1_ref,
):
    query = q_ref[...] * jnp.asarray(HEAD**-0.5, BF)
    grad = g_ref[...]
    allowed = [allowed_of(causal, ids_ref, qid_ref, part) for part in range(2)]
    keys = (k0_ref[...], k1_ref[...])
    values = (v0_ref[...], v1_ref[...])
    grad_q = 0.0
    grad_k = [0.0, 0.0]
    grad_v = [0.0, 0.0]
    for head in range(2):
        one = lane_mask(query, head)
        grad_one = lane_mask(grad, head)
        lse = lse_ref[0, head : head + 1, :]
        probs = [jnp.exp(scores_t(k, one, ok) - lse) for k, ok in zip(keys, allowed)]
        grad_p = [
            lax.dot_general(v, grad_one, (((1,), (1,)), ((), ())), preferred_element_type=F32)
            for v in values
        ]
        inner = jnp.sum(probs[0] * grad_p[0], axis=0, keepdims=True) + jnp.sum(
            probs[1] * grad_p[1], axis=0, keepdims=True
        )
        for part in range(2):
            grad_s = (probs[part] * (grad_p[part] - inner)).astype(BF)
            grad_v[part] = grad_v[part] + dot(probs[part].astype(BF), grad_one)
            grad_k[part] = grad_k[part] + dot(grad_s, one)
            grad_q = grad_q + lax.dot_general(
                lane_mask(keys[part], head), grad_s, (((0,), (0,)), ((), ())),
                preferred_element_type=F32,
            )
    dq_ref[...] = (grad_q * HEAD**-0.5).T.astype(BF)
    dk0_ref[...] = grad_k[0]
    dv0_ref[...] = grad_v[0]
    dk1_ref[...] = grad_k[1].astype(BF)
    dv1_ref[...] = grad_v[1].astype(BF)


def call_kernel(body, causal, arrays, ids, qid, extra, first, out_shape, out_specs):
    in_specs = [
        pl.BlockSpec(
            (a[0].shape[0], PAIR), lambda p, at=a[1], step=(a + (1,))[2]: (0, at + p * step)
        )
        for a in arrays
    ]
    in_specs.append(pl.BlockSpec(ids.shape, lambda p: (0, 0, 0)))
    in_specs.append(pl.BlockSpec(qid.shape, lambda p: (0, 0)))
    in_specs += [pl.BlockSpec((1,) + e.shape[1:], lambda p: (p, 0, 0)) for e in extra]

    in_specs += [pl.BlockSpec(memory_space=pl.ANY) for f in first]
    n_in = len(in_specs)

    def kernel(*refs):
        body(causal, *refs[: n_in - len(first)], *refs[n_in:])

    pairs = extra[0].shape[0] if extra else out_shape[1].shape[0]
    return pl.pallas_call(
        kernel,
        grid=(pairs,),
        in_specs=in_specs,
        out_specs=out_specs,
        out_shape=out_shape,
        compiler_params=pltpu.CompilerParams(vmem_limit_bytes=56 * 1024 * 1024),
        cost_estimate=pl.CostEstimate(flops=0, bytes_accessed=0, transcendentals=0),
    )(*[a[0] for a in arrays], ids, qid, *extra, *first)


def attend_fwd(causal, arrays, ids, qid, pairs, first=()):
    n_q = qid.shape[1]
    out_shape = (
        jax.ShapeDtypeStruct((n_q, pairs * PAIR), BF),
        jax.ShapeDtypeStruct((pairs, 2, n_q), F32),
    )
    out_specs = (
        pl.BlockSpec((n_q, PAIR), lambda p: (0, p)),
        pl.BlockSpec((1, 2, n_q), lambda p: (p, 0, 0)),
    )
    return call_kernel(
        attend_kernel, causal, arrays, ids, qid, (), first, out_shape, out_specs,
    )


def attend_back(causal, arrays, ids, qid, lse, first=()):
    pairs, n_q, n_k = lse.shape[0], qid.shape[1], ids.shape[1]
    wide = pairs * PAIR
    out_shape = (
        jax.ShapeDtypeStruct((n_q, wide), BF),
        jax.ShapeDtypeStruct((n_k, wide), F32),
        jax.ShapeDtypeStruct((n_k, wide), F32),
        jax.ShapeDtypeStruct((n_k, wide), BF),
        jax.ShapeDtypeStruct((n_k, wide), BF),
    )
    out_specs = tuple(pl.BlockSpec((s.shape[0], PAIR), lambda p: (0, p)) for s in out_shape)
    return call_kernel(
        attend_back_kernel, causal, arrays, ids, qid, (lse,), first, out_shape, out_specs,
    )


def far_pairs(keys_values, pairs):
    half = pairs * PAIR
    return [
        swap(jnp.concatenate([
            keys_values[:, p * PAIR : (p + 1) * PAIR],
            keys_values[:, half + p * PAIR : half + (p + 1) * PAIR],
        ], axis=1), "xl")
        for p in range(pairs)
    ]


def attend_pairs(query, near, at, far, ids, qid, pairs, first=()):
    done = []
    for p in range(pairs):
        arrays = [(query, p), (near, at + p), (near, at + pairs + p), (far[p], 0), (far[p], 1)]
        done.append(attend_fwd(False, arrays, ids, qid, 1, first))
    return jnp.concatenate([d[0] for d in done], axis=1), [d[1] for d in done]


def attend_pairs_back(query, near, at, far, grad, ids, qid, lse, first=()):
    pairs = len(lse)
    grad_q, near_k, near_v, sent = [], [], [], []
    for p in range(pairs):
        arrays = [
            (query, p), (near, at + p), (near, at + pairs + p), (far[p], 0), (far[p], 1), (grad, p)
        ]
        gq, k0, v0, k1, v1 = attend_back(False, arrays, ids, qid, lse[p], first)
        grad_q.append(gq)
        near_k.append(k0)
        near_v.append(v0)
        sent.append(swap(jnp.concatenate([k1, v1], axis=1), "xl"))
    far_k, far_v = [f[:, :PAIR] for f in sent], [f[:, PAIR:] for f in sent]
    return grad_q, near_k + near_v, far_k + far_v


def stack_rows(blocks, height, width):
    spots, parts = list(blocks), list(blocks.values())

    def kernel(*refs):
        out = refs[-1]
        out[...] = jnp.zeros(out.shape, F32)
        for spot, ref in zip(spots, refs):
            out[spot : spot + ref.shape[0], :] = ref[...]

    return pl.pallas_call(kernel, out_shape=jax.ShapeDtypeStruct((height, width), F32))(*parts)


def adam_step(master, first, second, gradient, factor, rate, decay):
    clipped = gradient * factor
    first_new = BETA_FIRST * first + (1 - BETA_FIRST) * clipped
    second_new = BETA_SECOND * second + (1 - BETA_SECOND) * clipped * clipped
    first_hat = first_new / (1 - BETA_FIRST**STEP)
    second_hat = second_new / (1 - BETA_SECOND**STEP)
    master_new = master - rate * (first_hat / (jnp.sqrt(second_hat) + ADAM_EPS) + decay * master)
    return (master_new, first_new, second_new)


def per_device(
    src_x, tgt_x, out_cot, src_seg, tgt_seg, src_pad, tgt_pad,
    enc_master, dec_master, down_master, small_master,
    enc_first, dec_first, down_first, small_first,
    enc_second, dec_second, down_second, small_second,
):
    width = src_x.shape[-1]
    half = width // 2
    hid = 2 * width
    pairs = half // PAIR
    rows = enc_master.shape[0]
    down_rows = down_master.shape[0]
    n_small = small_master.shape[1]
    core = lax.axis_index("c")
    first_core = core == 0
    order = one_hot(feature_order(width), width)
    hidden = one_hot(hidden_order(width), width)
    place = one_hot(jnp.where(first_core, head_order(width, 0), head_order(width, 1)), width)
    quarter = width // 4

    encb, decb, downb = enc_master.astype(BF), dec_master.astype(BF), down_master.astype(BF)
    smallb = jnp.pad(small_master.astype(BF), ((0, 0), (0, LANES - n_small)))

    def block(matrix, index):
        return matrix[:, index * width : (index + 1) * width]

    def halves(matrix):
        n = matrix.shape[1] // 2
        return matrix[:, :n], matrix[:, n:]

    ups = jnp.concatenate([encb[:, 4 * width :], decb[:, 8 * width :]], axis=0).reshape(-1, width)
    ups = dot(ups, hidden, BF).reshape(2, rows, 4, 2, 2, quarter)

    def up_halves(index):
        return [
            jnp.concatenate([ups[index, :, z, c, g] for g in range(2) for z in range(4)], axis=1)
            for c in range(2)
        ]

    col_blocks = [
        halves(block(encb, 0)), halves(block(encb, 1)), halves(block(encb, 2)), (smallb, smallb),
        up_halves(0), halves(block(decb, 5)), halves(block(decb, 6)),
        halves(block(decb, 0)), halves(block(decb, 1)), halves(block(decb, 2)), halves(block(decb, 4)),
        up_halves(1),
    ]
    cols0 = jnp.concatenate([b[0] for b in col_blocks], axis=1)
    cols1 = jnp.concatenate([b[1] for b in col_blocks], axis=1)
    mine = jnp.where(first_core, cols0, cols1)
    theirs = swap(jnp.where(first_core, cols1, cols0), "c")
    cols = jnp.concatenate(
        [jnp.where(first_core, mine, theirs), jnp.where(first_core, theirs, mine)], axis=0
    )
    shards = dot(jnp.concatenate(
        [block(encb, 3), block(decb, 3), block(decb, 7), downb[:, :width], downb[:, width:]], axis=0
    ), order, BF)
    out_rows = [shards[j * rows : (j + 1) * rows] for j in range(3)]
    out_rows = jnp.concatenate([
        jnp.concatenate([part[:, :half] for part in out_rows], axis=1),
        jnp.concatenate([part[:, half:] for part in out_rows], axis=1),
    ], axis=0)

    def down_packed(index):
        at = 3 * rows + index * down_rows
        middle = at + down_rows // 2
        return jnp.concatenate([shards[at:middle], shards[middle : at + down_rows]], axis=1)

    n_qkv, n_one = 3 * half, 3 * half + LANES
    n_up = cols.shape[1] - hid
    packed = jnp.concatenate([
        cols[:, :n_one], out_rows[:, :half], down_packed(0), cols[:, n_one:n_up],
        out_rows[:, half:], down_packed(1), cols[:, n_up:]
    ], axis=1)
    sizes = (n_qkv, LANES, half, hid, hid, 2 * half, n_qkv, half, 2 * half, hid, hid)
    starts = [int(v) for v in np.cumsum((0,) + sizes)]
    packed = lax.all_gather(packed, ("xh", "xl"), axis=0).reshape(8 * rows, starts[-1])

    def gather_blocks(value):
        return gather_by_trade(value, ("z", "y"), 16).reshape(width, value.shape[1])

    full_one = gather_blocks(packed[:, : starts[3]])
    full_two = lax.all_gather(packed[:, starts[3] : starts[9]], ("z", "y"), axis=0, tiled=True)
    packed_three = packed[:, starts[9] :]
    full_three = lax.all_gather(packed_three, ("z", "y"), axis=0, tiled=True)

    def cut(full, first, last):
        base = starts[first]
        return [full[:, starts[j] - base : starts[j + 1] - base] for j in range(first, last)]

    w_eqkv, small_all, w_eo = cut(full_one, 0, 3)
    w_e2, w_e1, w_ckv, w_dqkv, w_cq, w_out = cut(full_two, 3, 9)
    w_d2, w_d1 = cut(full_three, 9, 11)

    def pick(which, low, high):
        return jnp.where(which, low, high), jnp.where(which, high, low)

    def unpack_out(stored, count):
        kept, sent = pick(first_core, stored[:half], stored[half:])
        stored = dot_t(place, jnp.concatenate([kept, swap(sent, "c")], axis=0), BF)
        return [
            jnp.concatenate([stored[:half, cut], stored[half:, cut]], axis=1)
            for cut in (slice(j * half, (j + 1) * half) for j in range(count))
        ]

    def repack_out(grads):
        stacked = jnp.concatenate([
            jnp.concatenate([g[:, :half] for g in grads], axis=1),
            jnp.concatenate([g[:, half:] for g in grads], axis=1),
        ], axis=0)
        stored = dot(place, stacked, BF)
        low, high = pick(first_core, stored[:half], swap(stored[half:], "c"))
        return jnp.concatenate([low, high], axis=0)

    eye = one_hot(np.arange(width), width)
    small_p = dot_t(small_all, eye)
    small_own = dot_b(small_all.T, order)

    def own_half(column):
        row = small_own[column]
        return jnp.where(first_core, row[:half], row[half:])

    def hidden_bias(column):
        stored = dot(small_own[column : column + 4].astype(BF), hidden)
        stored = jnp.where(first_core, stored[:, :half], stored[:, half:])
        return stored.reshape(4, 2, quarter).transpose(1, 0, 2).reshape(1, hid)

    none = jnp.zeros((half,), F32)

    def ids_of(seg, pad, at):
        n = seg.shape[1]
        spot = (lax.axis_index("xl") * 2 + core) * n + jnp.arange(n, dtype=jnp.int32)
        key = jnp.where(pad[0] == 1, seg[0], -1)
        return jnp.stack([key, spot, seg[0]], axis=1)

    src_ids = join_core(ids_of(src_seg, src_pad, 0))
    tgt_ids = join_core(ids_of(tgt_seg, tgt_pad, 0))
    src_keys = jnp.stack([src_ids[:, :2], swap(src_ids[:, :2], "xl")])
    tgt_keys = jnp.stack([tgt_ids[:, :2], swap(tgt_ids[:, :2], "xl")])
    src_q = jnp.stack([src_ids[:, 2], src_ids[:, 1]])
    tgt_q = jnp.stack([tgt_ids[:, 2], tgt_ids[:, 1]])

    source = dot(src_x[0], order)
    enc_norm = join_core(norm(source, small_p[0], small_p[1]))
    enc_qkv = (dot(enc_norm, w_eqkv) + jnp.concatenate([own_half(2), none, own_half(3)])).astype(BF)
    enc_far = far_pairs(enc_qkv[:, half:], pairs)

    target = dot(tgt_x[0], order)

    bias_e, bias_d = hidden_bias(8), hidden_bias(27)
    enc_att, enc_lse = attend_pairs(
        enc_qkv, enc_qkv, pairs, enc_far, src_keys, src_q, pairs, (packed_three, bias_e, bias_d)
    )
    w_eo, = unpack_out(w_eo, 1)
    enc_one = source + sum_core(dot(enc_att, w_eo)) + small_p[4]

    def feed_fwd(resid, w_in, w_out, small_p, base, bias, earlier):
        normed = join_core(after(norm(resid, small_p[base], small_p[base + 1]), earlier))
        active, slope = gelu_parts(dot(normed, w_in) + bias)
        active = active.astype(BF)
        out = dot(active[:, :width], w_out[:, :width]) + dot(active[:, width:], w_out[:, width:])
        return normed, active, slope, resid + sum_core(out) + small_p[base + 2]

    dec_norm = join_core(after(norm(target, small_p[14], small_p[15]), enc_att))
    dec_qkv = (dot(dec_norm, w_dqkv) + jnp.concatenate([own_half(16), none, own_half(17)])).astype(BF)
    dec_far = swap(dec_qkv[:, half:], "xl")

    enc_ffn = feed_fwd(enc_one, w_e1, w_e2, small_p, 5, bias_e, dec_qkv)
    enc_two = enc_ffn[3]
    memory = join_core(norm(enc_two, small_p[12], small_p[13]))

    dec_arrays = [(dec_qkv, 0), (dec_qkv, pairs), (dec_qkv, 2 * pairs), (dec_far, 0), (dec_far, pairs)]
    cross_kv = (dot(memory, w_ckv) + jnp.concatenate([none, own_half(22)])).astype(BF)
    cross_far = far_pairs(cross_kv, pairs)
    w_so, w_co = unpack_out(after(w_out, enc_two), 2)
    self_att, self_lse = attend_fwd(True, dec_arrays, tgt_keys, tgt_q, pairs, (cross_kv, w_so, w_co))
    dec_one = target + sum_core(dot(self_att, w_so)) + small_p[18]
    cross_norm = join_core(norm(dec_one, small_p[19], small_p[20]))
    cross_q = (dot(cross_norm, w_cq) + own_half(21)).astype(BF)
    cross_att, cross_lse = attend_pairs(cross_q, cross_kv, 0, cross_far, src_keys, tgt_q, pairs)
    cross_far, cross_lse = jnp.concatenate(cross_far, axis=1), jnp.concatenate(cross_lse, axis=0)
    cross_arrays = [(cross_q, 0), (cross_kv, 0), (cross_kv, pairs), (cross_far, 0, 2), (cross_far, 1, 2)]
    dec_two = dec_one + sum_core(dot(cross_att, w_co)) + small_p[23]
    dec_ffn = feed_fwd(dec_two, w_d1, w_d2, small_p, 24, bias_d, cross_att)
    dec_out = reorder_wide(dec_ffn[3], order)

    small_grad = {}
    own_grad = {}

    def put_own(column, row):
        empty = jnp.zeros_like(row)
        own_grad[column] = jnp.where(
            first_core, jnp.concatenate([row, empty], axis=1), jnp.concatenate([empty, row], axis=1)
        )

    def put_hidden(column, row):
        row = row.reshape(2, 4, quarter).transpose(1, 0, 2).reshape(4, half).astype(BF)
        empty = jnp.zeros_like(row)
        row = jnp.where(
            first_core, jnp.concatenate([row, empty], axis=1), jnp.concatenate([empty, row], axis=1)
        )
        own_grad[column] = dot_b(row, hidden)

    def feed_back(resid, saved, w_in, w_out, small_p, base, gradient):
        normed, active, slope = saved[:3]
        branch = gradient.astype(BF)
        small_grad[base + 2] = jnp.sum(branch, axis=0, dtype=F32, keepdims=True)
        branch = join_core(branch)
        grad_out = [dot_t(active[:, :width], branch, BF), dot_t(active[:, width:], branch, BF)]
        grad_hidden = jnp.concatenate([
            (dot_b(branch, w_out[:, :width]) * slope[:, :width]).astype(BF),
            (dot_b(branch, w_out[:, width:]) * slope[:, width:]).astype(BF),
        ], axis=1)
        put_hidden(base + 3, jnp.sum(grad_hidden, axis=0, dtype=F32))
        grad_in = dot_t(normed, grad_hidden, BF)
        grad_normed = sum_core(dot_b(grad_hidden, w_in))
        for one in [grad_in] + grad_out:
            grad_normed = after(grad_normed, one)
        back, small_grad[base], small_grad[base + 1] = norm_back(resid, small_p[base], grad_normed)
        return gradient + back, grad_in, grad_out

    def out_back(gradient, attended, weight, column):
        branch = gradient.astype(BF)
        small_grad[column] = jnp.sum(branch, axis=0, dtype=F32, keepdims=True)
        branch = join_core(branch)
        return dot_t(attended, branch, BF), dot_b(branch, weight, BF)

    def in_back(resid, normed, grad_proj, weight, small_p, column, gradient):
        grad_weight = dot_t(normed, grad_proj, BF)
        grad_normed = after(sum_core(dot_b(grad_proj, weight)), grad_weight)
        back, small_grad[column], small_grad[column + 1] = norm_back(
            resid, small_p[column], grad_normed
        )
        return gradient + back, grad_weight

    def reduce_by_trade(value):
        value = value.reshape(16, 8 * rows, value.shape[1])
        return sum_by_trade(value, ("z", "y")).astype(BF)

    def along_x(*values):
        return scatter_x([v.reshape(4, 2 * rows, v.shape[1]) for v in values])

    def reduce(value):
        value = lax.psum_scatter(value, ("z", "y"), scatter_dimension=0, tiled=True)
        return lax.optimization_barrier(value)

    top = dot(out_cot[0], order)
    grad_two, g_d1, g_d2 = feed_back(dec_two, dec_ffn, w_d1, w_d2, small_p, 24, top)
    part_three = jnp.concatenate(g_d2 + [g_d1], axis=1)
    sum_three = reduce(part_three)

    g_co, grad_att = out_back(grad_two, cross_att, w_co, 23)
    cross_gq, ck0, cv0, ck1, cv1 = attend_back(
        False, cross_arrays + [(grad_att, 0)], src_keys, tgt_q, cross_lse, (part_three,)
    )
    cross_back = swap(jnp.concatenate([ck1, cv1], axis=1), "xl")
    put_own(21, jnp.sum(cross_gq, axis=0, dtype=F32, keepdims=True))
    grad_one, g_cq = in_back(dec_one, cross_norm, cross_gq, w_cq, small_p, 19, grad_two)

    g_so, grad_att = out_back(grad_one, self_att, w_so, 18)
    self_gq, sk0, sv0, sk1, sv1 = attend_back(
        True, dec_arrays + [(grad_att, 0)], tgt_keys, tgt_q, self_lse, (g_co, g_cq, g_so)
    )
    self_far = swap(jnp.concatenate([sk1, sv1], axis=1), "xl")
    dec_outs = repack_out((g_so, g_co))
    cross_gkv = after(jnp.concatenate([ck0, cv0], axis=1) + cross_back, self_gq).astype(BF)
    put_own(22, jnp.sum(cross_gkv[:, half:], axis=0, dtype=F32, keepdims=True))
    g_ckv = dot_t(memory, cross_gkv, BF)
    grad_memory = after(sum_core(dot_b(cross_gkv, w_ckv)), g_ckv)
    grad_memory = lax.reduce_precision(grad_memory, 8, 7)
    self_gkv = (jnp.concatenate([sk0, sv0], axis=1) + self_far).astype(BF)
    self_grad = jnp.concatenate([self_gq, self_gkv], axis=1)
    self_sum = jnp.sum(self_grad, axis=0, dtype=F32, keepdims=True)
    put_own(16, self_sum[:, :half])
    put_own(17, self_sum[:, 2 * half :])
    tgt_grad, g_dqkv = in_back(target, dec_norm, self_grad, w_dqkv, small_p, 14, grad_one)
    tgt_grad = reorder_wide(tgt_grad, order)

    enc_grad_two, small_grad[12], small_grad[13] = norm_back(
        enc_two, small_p[12], after(grad_memory, dec_outs)
    )

    enc_grad_one, g_e1, g_e2 = feed_back(enc_one, enc_ffn, w_e1, w_e2, small_p, 5, enc_grad_two)
    g_eo, grad_att = out_back(enc_grad_one, enc_att, w_eo, 4)
    part_two = jnp.concatenate(
        g_e2 + [g_e1, g_ckv, g_dqkv, g_cq, repack_out((g_eo,)), dec_outs], axis=1
    )
    sum_two = reduce(part_two)
    enc_gq, near, far = attend_pairs_back(
        enc_qkv, enc_qkv, pairs, enc_far, grad_att, src_keys, src_q, enc_lse, (part_two, sum_three)
    )
    enc_grad = jnp.concatenate(
        enc_gq + [(a + b).astype(BF) for a, b in zip(near, far)], axis=1
    )
    enc_sum = jnp.sum(enc_grad, axis=0, dtype=F32, keepdims=True)
    put_own(2, enc_sum[:, :half])
    put_own(3, enc_sum[:, 2 * half :])
    src_grad, g_eqkv = in_back(source, enc_norm, enc_grad, w_eqkv, small_p, 0, enc_grad_one)
    src_grad = reorder_wide(src_grad, order)

    stored = stack_rows(small_grad, LANES, width)
    owned = stack_rows(own_grad, LANES, width)
    g_small = (dot_b(eye, stored.astype(BF)) + lax.dot_general(
        order, owned.astype(BF), (((0,), (1,)), ((), ())), preferred_element_type=F32
    )).astype(BF)
    early = along_x(sum_three)
    sum_one = after(after(reduce_by_trade(g_eqkv), g_small), early)
    late = along_x(sum_one, sum_two)
    sum_small = after(g_small.reshape(64, 2 * rows, LANES), sum_one)
    sum_small = lax.all_to_all(sum_small, ("z", "y", "xh", "xl"), 0, 0)
    sum_small = jnp.sum(after(sum_small.astype(F32), late), axis=0)

    s_d2, s_d1 = early[:, :hid], early[:, hid:]
    s_eqkv, late = late[:, :n_qkv], late[:, n_qkv:]
    s_e2, s_e1, s_ckv, s_dqkv, s_cq = cut(late, 3, 8)
    s_eo, s_so, s_co = [late[:, late.shape[1] - j * half :][:, :half] for j in (3, 2, 1)]

    def from_cores(value):
        keep, send = pick(first_core, value[:rows], value[rows:])
        other = swap(send, "c")
        return pick(first_core, keep, other)

    low_small, high_small = from_cores(sum_small)
    grad_small = (low_small + high_small)[:, :n_small]
    lasts = early, s_eqkv, grad_small, late
    squares = sum(jnp.sum(part * part) for part in lasts)
    squares = jnp.full((8, LANES), squares)
    squares = squares + swap(squares, "c")
    squares = jnp.sum(gather_by_trade(squares, ("z", "xh", "y", "xl"), 64), axis=0)
    low, high = from_cores(jnp.concatenate([s_eqkv, s_e1, s_ckv, s_dqkv, s_cq, s_d1], axis=1))
    ups = jnp.stack([part[:, a : a + hid] for a in (n_qkv, low.shape[1] - hid) for part in (low, high)])
    ups = ups.reshape(2, 2, rows, 2, 4, quarter).transpose(0, 2, 4, 1, 3, 5).reshape(8 * rows, width)
    ups = reorder_wide(ups, hidden).reshape(2, rows, 2 * hid)

    def joined(start, count):
        at = [start + j * half for j in range(count)]
        return [part[:, a : a + half] for a in at for part in (low, high)]

    shards = [
        jnp.concatenate([part[:rows], part[rows:]], axis=1)
        for part in (s_eo, s_so, s_co)
    ] + [part[:, a : a + width] for part in (s_e2, s_d2) for a in (0, width)]
    shards = reorder_wide(jnp.concatenate(shards, axis=0), order)
    grad_enc = jnp.concatenate(joined(0, 3) + [shards[:rows], ups[0]], axis=1)
    at = n_qkv + hid
    grad_dec = jnp.concatenate(
        joined(at + 2 * half, 3) + [shards[rows : 2 * rows]] + joined(at + 5 * half, 1)
        + joined(at, 2) + [shards[2 * rows : 3 * rows], ups[1]], axis=1
    )
    shards = shards[3 * rows :]
    grad_down = jnp.concatenate([shards[:down_rows], shards[down_rows:]], axis=1)

    grad_norm = jnp.sqrt(squares[0, 0])
    factor = CLIP_LEVEL / jnp.maximum(grad_norm, CLIP_LEVEL)
    enc_all = adam_step(enc_master, enc_first, enc_second, grad_enc, factor, RATE_MATRIX, DECAY_RATE)
    dec_all = adam_step(dec_master, dec_first, dec_second, grad_dec, factor, RATE_MATRIX, DECAY_RATE)
    down_all = adam_step(
        down_master, down_first, down_second, grad_down, factor, RATE_MATRIX, DECAY_RATE
    )
    small_all_new = adam_step(
        small_master, small_first, small_second, grad_small, factor, RATE_SMALL, 0.0
    )
    return (
        dec_out[None], src_grad[None], tgt_grad[None], grad_norm,
        enc_all[0], dec_all[0], down_all[0], small_all_new[0],
        enc_all[1], dec_all[1], down_all[1], small_all_new[1],
        enc_all[2], dec_all[2], down_all[2], small_all_new[2],
        grad_small * factor,
    )


def solution(mesh):
    split = Mesh(mesh.devices.reshape(4, 2, 4, 2, 2), ALL_AXES)
    tokens = P(ROW_AXES, POS_AXES, None)
    marks = P(ROW_AXES, POS_AXES)
    shard = P(ALL_AXES, None)
    in_specs = (tokens,) * 3 + (marks,) * 4 + (shard,) * 12
    out_specs = (tokens,) * 3 + (P(),) + (shard,) * 13
    return jax.shard_map(
        per_device, mesh=split, in_specs=in_specs, out_specs=out_specs, check_vma=False
    )
```

```python
import jax
import jax.numpy as jnp
import numpy as np
from jax import lax
from jax.experimental import pallas as pl
from jax.experimental.pallas import tpu as pltpu
from jax.sharding import Mesh, PartitionSpec as P

HEAD = 64
STEP = 10
NORM_EPS = 1e-05
MASKED = -1000000000.0
BETA_FIRST = 0.9
BETA_SECOND = 0.999
ADAM_EPS = 1e-08
RATE_MATRIX = 0.1
RATE_SMALL = 0.5
DECAY_RATE = 0.01
CLIP_LEVEL = 1.0
BF = jnp.bfloat16
F32 = jnp.float32
PAIR = 2 * HEAD
LANES = 128
ROW_AXES = ("z", "xh", "y")
POS_AXES = ("xl", "c")
ALL_AXES = ("z", "xh", "y", "xl", "c")
SWAP = [(0, 1), (1, 0)]


def swap(value, axis):
    return lax.ppermute(value, axis, SWAP)


def along_ring(value, by):
    return lax.ppermute(value, ("xh", "xl"), [(i, (i + by) % 4) for i in range(4)])


def ring_gather(value):
    h = value.shape[0] // 2
    before, after_it = along_ring(value, 1), along_ring(value, 3)
    far = [along_ring(before[:h], 1), along_ring(after_it[h:], 3)]
    return jnp.concatenate([value, before, after_it] + far, axis=0)


def ring_scatter(value):
    own, down, up, far = value
    h = own.shape[0] // 2
    up_more, down_more = along_ring(far[:h], 1), along_ring(far[h:], 3)
    up = jnp.concatenate([add_wide(up[:h], up_more).astype(BF), up[h:]], axis=0)
    down = jnp.concatenate([down[:h], add_wide(down[h:], down_more).astype(BF)], axis=0)
    return add_wide(own, along_ring(up, 1), along_ring(down, 3))


def flip(value, bits):
    return lax.ppermute(value, ("xh", "xl"), [(i, i ^ bits) for i in range(4)])


def join_core(value):
    return jnp.concatenate([value, swap(value, "c")], axis=0)


def sum_core(partial):
    mine = partial.shape[0] // 2
    return partial[:mine] + swap(partial[mine:], "c")


def after(value, earlier):
    one = lax.slice(earlier, (0,) * earlier.ndim, (1,) * earlier.ndim)
    return value + one.reshape(()).astype(value.dtype) * 0


def add_wide(*values):
    total = values[0].astype(F32)
    for value in values[1:]:
        total = total + value.astype(F32)
    return total


def scatter_x(values):
    here = lax.axis_index("xh") * 2 + lax.axis_index("xl")

    def piece(spot):
        return jnp.concatenate(
            [lax.dynamic_index_in_dim(value, spot, 0, keepdims=False) for value in values], axis=1
        )

    total = piece(here).astype(F32)
    for bits in (1, 2, 3):
        total = total + flip(piece(here ^ bits), bits).astype(F32)
    return total


def gather_by_trade(value, axes, n):
    return lax.all_to_all(jnp.broadcast_to(value[None], (n,) + value.shape), axes, 0, 0)


def sum_by_trade(value, axes):
    return jnp.sum(lax.all_to_all(value, axes, 0, 0).astype(F32), axis=0)


def feature_order(width):
    rest = width // 32
    new = np.arange(width)
    z, y, xh, r = new // (8 * rest), (new // (2 * rest)) % 4, (new // rest) % 2, new % rest
    return ((z * 2 + xh) * 4 + y) * rest + r


def hidden_order(width):
    n = width // 64
    new = np.arange(width)
    c, g, y = new // (32 * n), (new // (16 * n)) % 2, (new // (4 * n)) % 4
    xh, xl, i = (new // (2 * n)) % 2, (new // n) % 2, new % n
    return ((((xh * 4 + y) * 2 + xl) * 2 + c) * 2 + g) * n + i


def head_order(width, core):
    r = width // 128
    own = np.arange(width // 2)
    z, xh = own // (32 * r), (own // (16 * r)) % 2
    y, xl, c, i = (own // (4 * r)) % 4, (own // (2 * r)) % 2, (own // r) % 2, own % r
    return np.concatenate([
        (c != core) * (width // 2) + ((((z * 4 + y) * 2 + xh) * 2 + xl) * 2 + cols) * r + i
        for cols in range(2)
    ])


def near_order(width, here):
    r = width // 128
    new = np.arange(width)
    x = (here + jnp.asarray((0, 3, 1, 2))[new // (32 * r)]) % 4
    z, y, c, i = (new // (8 * r)) % 4, (new // (2 * r)) % 4, (new // r) % 2, new % r
    return (((z * 2 + x // 2) * 4 + y) * 4 + (x % 2) * 2 + c) * r + i


def near_head_order(width, here, core):
    r = width // 128
    own = np.arange(width // 2)
    z, xh = own // (32 * r), (own // (16 * r)) % 2
    y, xl, c, i = (own // (4 * r)) % 4, (own // (2 * r)) % 2, (own // r) % 2, own % r
    apart = jnp.asarray((0, 2, 3, 1))[(xh * 2 + xl - here) % 4]
    return jnp.concatenate([
        (c != core) * (width // 2) + (((apart * 2 + z) * 4 + y) * 2 + cols) * r + i for cols in range(2)
    ])


def one_hot(picks, width):
    rows = lax.broadcasted_iota(jnp.int32, (width, picks.shape[0]), 0)
    return (rows == jnp.asarray(picks, jnp.int32)[None, :]).astype(BF)


def dot(left, right, kind=F32):
    return jnp.dot(left, right, preferred_element_type=kind)


def dot_t(left, right, kind=F32):
    return lax.dot_general(left, right, (((0,), (0,)), ((), ())), preferred_element_type=kind)


def dot_b(left, right, kind=F32):
    return lax.dot_general(left, right, (((1,), (1,)), ((), ())), preferred_element_type=kind)


def two_parts(value):
    high = lax.reduce_precision(value, 8, 7)
    return high.astype(BF), (value - high).astype(BF)


def reorder_wide(value, order):
    high, low = two_parts(value)
    both = dot_b(jnp.concatenate([high, low], axis=0), order)
    return both[: value.shape[0]] + both[value.shape[0] :]


def norm_stats(x):
    center = x - jnp.mean(x, axis=-1, keepdims=True)
    spread = jnp.mean(center * center, axis=-1, keepdims=True)
    scale = lax.rsqrt(spread + NORM_EPS)
    return center * scale, scale


def norm(x, gain, shift):
    unit, scale = norm_stats(x)
    return (unit * gain + shift).astype(BF)


def norm_back(x, gain, gradient):
    unit, scale = norm_stats(x)
    inner = gradient * gain
    back = scale * (
        inner
        - jnp.mean(inner, axis=-1, keepdims=True)
        - unit * jnp.mean(inner * unit, axis=-1, keepdims=True)
    )
    return (
        back,
        jnp.sum(gradient * unit, axis=0, keepdims=True),
        jnp.sum(gradient, axis=0, keepdims=True),
    )


def gelu_parts(u):
    cdf = 0.5 * (1.0 + lax.erf(u * (0.5**0.5)))
    pdf = jnp.exp(-0.5 * u * u) * (1.0 / np.sqrt(2.0 * np.pi)).astype(np.float32)
    return u * cdf, cdf + u * pdf


def lane_mask(value, which):
    lane = lax.broadcasted_iota(jnp.int32, value.shape, 1)
    return jnp.where((lane // HEAD) == which, value, jnp.zeros_like(value))


def allowed_of(causal, ids_ref, qid_ref, part):
    seg = ids_ref[part, :, 0:1] == qid_ref[0:1, :]
    if causal:
        seg = seg & (ids_ref[part, :, 1:2] <= qid_ref[1:2, :])
    return seg


def scores_t(keys, query, allowed):
    raw = lax.dot_general(keys, query, (((1,), (1,)), ((), ())), preferred_element_type=F32)
    return jnp.where(allowed, raw, MASKED)


def attend_kernel(causal, q_ref, k0_ref, v0_ref, k1_ref, v1_ref, ids_ref, qid_ref, o_ref, lse_ref):
    query = q_ref[...] * jnp.asarray(HEAD**-0.5, BF)
    allowed = [allowed_of(causal, ids_ref, qid_ref, part) for part in range(2)]
    mixed = []
    for head in range(2):
        one = lane_mask(query, head)
        scores = [scores_t(ref[...], one, ok) for ref, ok in zip((k0_ref, k1_ref), allowed)]
        top = jnp.maximum(
            jnp.max(scores[0], axis=0, keepdims=True), jnp.max(scores[1], axis=0, keepdims=True)
        )
        expo = [jnp.exp(s - top) for s in scores]
        total = jnp.sum(expo[0], axis=0, keepdims=True) + jnp.sum(expo[1], axis=0, keepdims=True)
        share = 1.0 / total
        out = 0.0
        for ref, e in zip((v0_ref, v1_ref), expo):
            out = out + lax.dot_general(
                ref[...], (e * share).astype(BF), (((0,), (0,)), ((), ())), preferred_element_type=F32
            )
        mixed.append(out)
        lse_ref[0, head : head + 1, :] = top + jnp.log(total)
    both = jnp.concatenate([mixed[0][:HEAD], mixed[1][HEAD:]], axis=0)
    o_ref[...] = both.T.astype(BF)


def attend_back_kernel(
    causal, q_ref, k0_ref, v0_ref, k1_ref, v1_ref, g_ref, ids_ref, qid_ref, lse_ref,
    dq_ref, dk0_ref, dv0_ref, dk1_ref, dv1_ref,
):
    query = q_ref[...] * jnp.asarray(HEAD**-0.5, BF)
    grad = g_ref[...]
    allowed = [allowed_of(causal, ids_ref, qid_ref, part) for part in range(2)]
    keys = (k0_ref[...], k1_ref[...])
    values = (v0_ref[...], v1_ref[...])
    grad_q = 0.0
    grad_k = [0.0, 0.0]
    grad_v = [0.0, 0.0]
    for head in range(2):
        one = lane_mask(query, head)
        grad_one = lane_mask(grad, head)
        lse = lse_ref[0, head : head + 1, :]
        probs = [jnp.exp(scores_t(k, one, ok) - lse) for k, ok in zip(keys, allowed)]
        grad_p = [
            lax.dot_general(v, grad_one, (((1,), (1,)), ((), ())), preferred_element_type=F32)
            for v in values
        ]
        inner = jnp.sum(probs[0] * grad_p[0], axis=0, keepdims=True) + jnp.sum(
            probs[1] * grad_p[1], axis=0, keepdims=True
        )
        for part in range(2):
            grad_s = (probs[part] * (grad_p[part] - inner)).astype(BF)
            grad_v[part] = grad_v[part] + dot(probs[part].astype(BF), grad_one)
            grad_k[part] = grad_k[part] + dot(grad_s, one)
            grad_q = grad_q + lax.dot_general(
                lane_mask(keys[part], head), grad_s, (((0,), (0,)), ((), ())),
                preferred_element_type=F32,
            )
    dq_ref[...] = (grad_q * HEAD**-0.5).T.astype(BF)
    dk0_ref[...] = grad_k[0]
    dv0_ref[...] = grad_v[0]
    dk1_ref[...] = grad_k[1].astype(BF)
    dv1_ref[...] = grad_v[1].astype(BF)


def call_kernel(body, causal, arrays, ids, qid, extra, first, out_shape, out_specs):
    in_specs = [
        pl.BlockSpec(
            (a[0].shape[0], PAIR), lambda p, at=a[1], step=(a + (1,))[2]: (0, at + p * step)
        )
        for a in arrays
    ]
    in_specs.append(pl.BlockSpec(ids.shape, lambda p: (0, 0, 0)))
    in_specs.append(pl.BlockSpec(qid.shape, lambda p: (0, 0)))
    in_specs += [pl.BlockSpec((1,) + e.shape[1:], lambda p: (p, 0, 0)) for e in extra]

    in_specs += [pl.BlockSpec(memory_space=pl.ANY) for f in first]
    n_in = len(in_specs)

    def kernel(*refs):
        body(causal, *refs[: n_in - len(first)], *refs[n_in:])

    pairs = extra[0].shape[0] if extra else out_shape[1].shape[0]
    return pl.pallas_call(
        kernel,
        grid=(pairs,),
        in_specs=in_specs,
        out_specs=out_specs,
        out_shape=out_shape,
        compiler_params=pltpu.CompilerParams(vmem_limit_bytes=56 * 1024 * 1024),
        cost_estimate=pl.CostEstimate(flops=0, bytes_accessed=0, transcendentals=0),
    )(*[a[0] for a in arrays], ids, qid, *extra, *first)


def attend_fwd(causal, arrays, ids, qid, pairs, first=()):
    n_q = qid.shape[1]
    out_shape = (
        jax.ShapeDtypeStruct((n_q, pairs * PAIR), BF),
        jax.ShapeDtypeStruct((pairs, 2, n_q), F32),
    )
    out_specs = (
        pl.BlockSpec((n_q, PAIR), lambda p: (0, p)),
        pl.BlockSpec((1, 2, n_q), lambda p: (p, 0, 0)),
    )
    return call_kernel(
        attend_kernel, causal, arrays, ids, qid, (), first, out_shape, out_specs,
    )


def attend_back(causal, arrays, ids, qid, lse, first=()):
    pairs, n_q, n_k = lse.shape[0], qid.shape[1], ids.shape[1]
    wide = pairs * PAIR
    out_shape = (
        jax.ShapeDtypeStruct((n_q, wide), BF),
        jax.ShapeDtypeStruct((n_k, wide), F32),
        jax.ShapeDtypeStruct((n_k, wide), F32),
        jax.ShapeDtypeStruct((n_k, wide), BF),
        jax.ShapeDtypeStruct((n_k, wide), BF),
    )
    out_specs = tuple(pl.BlockSpec((s.shape[0], PAIR), lambda p: (0, p)) for s in out_shape)
    return call_kernel(
        attend_back_kernel, causal, arrays, ids, qid, (lse,), first, out_shape, out_specs,
    )


def far_pairs(keys_values, pairs):
    half = pairs * PAIR
    return [
        swap(jnp.concatenate([
            keys_values[:, p * PAIR : (p + 1) * PAIR],
            keys_values[:, half + p * PAIR : half + (p + 1) * PAIR],
        ], axis=1), "xl")
        for p in range(pairs)
    ]


def attend_pairs(query, near, at, far, ids, qid, pairs, first=()):
    done = []
    for p in range(pairs):
        arrays = [(query, p), (near, at + p), (near, at + pairs + p), (far[p], 0), (far[p], 1)]
        done.append(attend_fwd(False, arrays, ids, qid, 1, first))
    return jnp.concatenate([d[0] for d in done], axis=1), [d[1] for d in done]


def attend_pairs_back(query, near, at, far, grad, ids, qid, lse, first=()):
    pairs = len(lse)
    grad_q, near_k, near_v, sent = [], [], [], []
    for p in range(pairs):
        arrays = [
            (query, p), (near, at + p), (near, at + pairs + p), (far[p], 0), (far[p], 1), (grad, p)
        ]
        gq, k0, v0, k1, v1 = attend_back(False, arrays, ids, qid, lse[p], first)
        grad_q.append(gq)
        near_k.append(k0)
        near_v.append(v0)
        sent.append(swap(jnp.concatenate([k1, v1], axis=1), "xl"))
    far_k, far_v = [f[:, :PAIR] for f in sent], [f[:, PAIR:] for f in sent]
    return grad_q, near_k + near_v, far_k + far_v


def stack_rows(blocks, height, width):
    spots, parts = list(blocks), list(blocks.values())

    def kernel(*refs):
        out = refs[-1]
        out[...] = jnp.zeros(out.shape, F32)
        for spot, ref in zip(spots, refs):
            out[spot : spot + ref.shape[0], :] = ref[...]

    return pl.pallas_call(kernel, out_shape=jax.ShapeDtypeStruct((height, width), F32))(*parts)


def adam_step(master, first, second, gradient, factor, rate, decay):
    clipped = gradient * factor
    first_new = BETA_FIRST * first + (1 - BETA_FIRST) * clipped
    second_new = BETA_SECOND * second + (1 - BETA_SECOND) * clipped * clipped
    first_hat = first_new / (1 - BETA_FIRST**STEP)
    second_hat = second_new / (1 - BETA_SECOND**STEP)
    master_new = master - rate * (first_hat / (jnp.sqrt(second_hat) + ADAM_EPS) + decay * master)
    return (master_new, first_new, second_new)


def per_device(
    src_x, tgt_x, out_cot, src_seg, tgt_seg, src_pad, tgt_pad,
    enc_master, dec_master, down_master, small_master,
    enc_first, dec_first, down_first, small_first,
    enc_second, dec_second, down_second, small_second,
):
    width = src_x.shape[-1]
    half = width // 2
    hid = 2 * width
    pairs = half // PAIR
    rows = enc_master.shape[0]
    down_rows = down_master.shape[0]
    n_small = small_master.shape[1]
    core = lax.axis_index("c")
    first_core = core == 0
    order = one_hot(feature_order(width), width)
    hidden = one_hot(hidden_order(width), width)
    place = one_hot(jnp.where(first_core, head_order(width, 0), head_order(width, 1)), width)
    quarter = width // 4
    here = lax.axis_index("xh") * 2 + lax.axis_index("xl")
    order_e = one_hot(near_order(width, here), width)
    place_e = one_hot(near_head_order(width, here, core), width)

    encb, decb, downb = enc_master.astype(BF), dec_master.astype(BF), down_master.astype(BF)
    smallb = jnp.pad(small_master.astype(BF), ((0, 0), (0, LANES - n_small)))

    def block(matrix, index):
        return matrix[:, index * width : (index + 1) * width]

    def halves(matrix):
        n = matrix.shape[1] // 2
        return matrix[:, :n], matrix[:, n:]

    ups = jnp.concatenate([encb[:, 4 * width :], decb[:, 8 * width :]], axis=0).reshape(-1, width)
    ups = dot(ups, hidden, BF).reshape(2, rows, 4, 2, 2, quarter)

    def up_halves(index):
        return [
            jnp.concatenate([ups[index, :, z, c, g] for g in range(2) for z in range(4)], axis=1)
            for c in range(2)
        ]

    col_blocks = [
        halves(block(encb, 0)), halves(block(encb, 1)), halves(block(encb, 2)), (smallb, smallb),
        up_halves(0), halves(block(decb, 5)), halves(block(decb, 6)),
        halves(block(decb, 0)), halves(block(decb, 1)), halves(block(decb, 2)), halves(block(decb, 4)),
        up_halves(1),
    ]
    cols0 = jnp.concatenate([b[0] for b in col_blocks], axis=1)
    cols1 = jnp.concatenate([b[1] for b in col_blocks], axis=1)
    mine = jnp.where(first_core, cols0, cols1)
    theirs = swap(jnp.where(first_core, cols1, cols0), "c")
    cols = jnp.concatenate(
        [jnp.where(first_core, mine, theirs), jnp.where(first_core, theirs, mine)], axis=0
    )
    shards = dot(jnp.concatenate(
        [block(encb, 3), block(decb, 3), block(decb, 7), downb[:, :width], downb[:, width:]], axis=0
    ), order, BF)
    out_rows = [shards[j * rows : (j + 1) * rows] for j in range(3)]
    out_rows = jnp.concatenate([
        jnp.concatenate([part[:, :half] for part in out_rows], axis=1),
        jnp.concatenate([part[:, half:] for part in out_rows], axis=1),
    ], axis=0)

    def down_packed(index):
        at = 3 * rows + index * down_rows
        middle = at + down_rows // 2
        return jnp.concatenate([shards[at:middle], shards[middle : at + down_rows]], axis=1)

    n_qkv, n_one = 3 * half, 3 * half + LANES
    n_up = cols.shape[1] - hid
    packed_one = jnp.concatenate([cols[:, :n_one], out_rows[:, :half]], axis=1)
    packed = jnp.concatenate([
        down_packed(0), cols[:, n_one:n_up], out_rows[:, half:], down_packed(1), cols[:, n_up:]
    ], axis=1)
    sizes = (n_qkv, LANES, half, hid, hid, 2 * half, n_qkv, half, 2 * half, hid, hid)
    starts = [int(v) for v in np.cumsum((0,) + sizes)]
    full_one = gather_by_trade(packed_one, ("z", "y"), 16).reshape(width // 4, starts[3])
    found = [packed, flip(packed, 1), flip(packed, 2), flip(after(packed, full_one), 3)]
    full_one = ring_gather(full_one)
    packed = []
    for spot in range(4):
        part = found[0]
        for bits in (1, 2, 3):
            part = jnp.where((here ^ bits) == spot, found[bits], part)
        packed.append(part)
    packed = jnp.concatenate(packed, axis=0)
    full_two = lax.all_gather(packed[:, : starts[9] - starts[3]], ("z", "y"), axis=0, tiled=True)
    packed_three = packed[:, starts[9] - starts[3] :]
    full_three = lax.all_gather(packed_three, ("z", "y"), axis=0, tiled=True)

    def cut(full, first, last):
        base = starts[first]
        return [full[:, starts[j] - base : starts[j + 1] - base] for j in range(first, last)]

    w_eqkv, small_all, w_eo = cut(full_one, 0, 3)
    w_e2, w_e1, w_ckv, w_dqkv, w_cq, w_out = cut(full_two, 3, 9)
    w_d2, w_d1 = cut(full_three, 9, 11)

    def pick(which, low, high):
        return jnp.where(which, low, high), jnp.where(which, high, low)

    def unpack_out(low, high, place, count):
        kept, sent = pick(first_core, low, high)
        stored = dot_t(place, jnp.concatenate([kept, swap(sent, "c")], axis=0), BF)
        return [
            jnp.concatenate([stored[:half, cut], stored[half:, cut]], axis=1)
            for cut in (slice(j * half, (j + 1) * half) for j in range(count))
        ]

    def repack_out(grads):
        stacked = jnp.concatenate([
            jnp.concatenate([g[:, :half] for g in grads], axis=1),
            jnp.concatenate([g[:, half:] for g in grads], axis=1),
        ], axis=0)
        stored = dot(place, stacked, BF)
        low, high = pick(first_core, stored[:half], swap(stored[half:], "c"))
        return jnp.concatenate([low, high], axis=0)

    eye = one_hot(np.arange(width), width)
    small_e = dot_t(small_all, eye)
    small_own = dot_b(small_all.T, order_e)
    small_p = dot(small_own.astype(BF), order)

    def own_half(column):
        row = small_own[column]
        return jnp.where(first_core, row[:half], row[half:])

    def hidden_bias(column):
        stored = dot(after(small_own[column : column + 4], enc_qkv).astype(BF), hidden)
        stored = jnp.where(first_core, stored[:, :half], stored[:, half:])
        return stored.reshape(4, 2, quarter).transpose(1, 0, 2).reshape(1, hid)

    none = jnp.zeros((half,), F32)

    def ids_of(seg, pad, at):
        n = seg.shape[1]
        spot = (lax.axis_index("xl") * 2 + core) * n + jnp.arange(n, dtype=jnp.int32)
        key = jnp.where(pad[0] == 1, seg[0], -1)
        return jnp.stack([key, spot, seg[0]], axis=1)

    src_ids = join_core(ids_of(src_seg, src_pad, 0))
    tgt_ids = join_core(ids_of(tgt_seg, tgt_pad, 0))
    src_keys = jnp.stack([src_ids[:, :2], swap(src_ids[:, :2], "xl")])
    tgt_keys = jnp.stack([tgt_ids[:, :2], swap(tgt_ids[:, :2], "xl")])
    src_q = jnp.stack([src_ids[:, 2], src_ids[:, 1]])
    tgt_q = jnp.stack([tgt_ids[:, 2], tgt_ids[:, 1]])

    source = dot(src_x[0], order)
    source_e = dot(src_x[0], order_e)
    enc_norm = join_core(norm(source_e, small_e[0], small_e[1]))
    enc_qkv = (dot(enc_norm, w_eqkv) + jnp.concatenate([own_half(2), none, own_half(3)])).astype(BF)
    enc_far = far_pairs(enc_qkv[:, half:], pairs)

    target = dot(tgt_x[0], order)

    bias_e, bias_d = hidden_bias(8), hidden_bias(27)
    enc_att, enc_lse = attend_pairs(
        enc_qkv, enc_qkv, pairs, enc_far, src_keys, src_q, pairs, (packed_three, bias_e, bias_d)
    )
    by_z = after(w_eo, enc_qkv).reshape(4, 2, 16 * rows, half)
    w_eo, = unpack_out(by_z[:, 0].reshape(half, half), by_z[:, 1].reshape(half, half), place_e, 1)
    enc_one = source + sum_core(dot(enc_att, w_eo)) + small_p[4]

    def feed_fwd(resid, w_in, w_out, small_p, base, bias, earlier):
        normed = join_core(after(norm(resid, small_p[base], small_p[base + 1]), earlier))
        active, slope = gelu_parts(dot(normed, w_in) + bias)
        active = active.astype(BF)
        out = dot(active[:, :width], w_out[:, :width]) + dot(active[:, width:], w_out[:, width:])
        return normed, active, slope, resid + sum_core(out) + small_p[base + 2]

    dec_norm = join_core(after(norm(target, small_p[14], small_p[15]), enc_att))
    dec_qkv = (dot(dec_norm, w_dqkv) + jnp.concatenate([own_half(16), none, own_half(17)])).astype(BF)
    dec_far = swap(dec_qkv[:, half:], "xl")

    enc_ffn = feed_fwd(enc_one, w_e1, w_e2, small_p, 5, bias_e, dec_qkv)
    enc_two = enc_ffn[3]
    memory = join_core(norm(enc_two, small_p[12], small_p[13]))

    dec_arrays = [(dec_qkv, 0), (dec_qkv, pairs), (dec_qkv, 2 * pairs), (dec_far, 0), (dec_far, pairs)]
    cross_kv = (dot(memory, w_ckv) + jnp.concatenate([none, own_half(22)])).astype(BF)
    cross_far = far_pairs(cross_kv, pairs)
    w_out = after(w_out, enc_two)
    w_so, w_co = unpack_out(w_out[:half], w_out[half:], place, 2)
    self_att, self_lse = attend_fwd(True, dec_arrays, tgt_keys, tgt_q, pairs, (cross_kv, w_so, w_co, cross_far[0]))
    dec_one = target + sum_core(dot(self_att, w_so)) + small_p[18]
    cross_norm = join_core(norm(dec_one, small_p[19], small_p[20]))
    cross_q = (dot(cross_norm, w_cq) + own_half(21)).astype(BF)
    cross_att, cross_lse = attend_pairs(cross_q, cross_kv, 0, cross_far, src_keys, tgt_q, pairs)
    cross_far, cross_lse = jnp.concatenate(cross_far, axis=1), jnp.concatenate(cross_lse, axis=0)
    cross_arrays = [(cross_q, 0), (cross_kv, 0), (cross_kv, pairs), (cross_far, 0, 2), (cross_far, 1, 2)]
    dec_two = dec_one + sum_core(dot(cross_att, w_co)) + small_p[23]
    dec_ffn = feed_fwd(dec_two, w_d1, w_d2, small_p, 24, bias_d, cross_att)
    dec_out = reorder_wide(dec_ffn[3], order)

    small_grad = {}
    own_grad = {}

    def put_own(column, row):
        empty = jnp.zeros_like(row)
        own_grad[column] = jnp.where(
            first_core, jnp.concatenate([row, empty], axis=1), jnp.concatenate([empty, row], axis=1)
        )

    def put_hidden(column, row):
        row = row.reshape(2, 4, quarter).transpose(1, 0, 2).reshape(4, half).astype(BF)
        empty = jnp.zeros_like(row)
        row = jnp.where(
            first_core, jnp.concatenate([row, empty], axis=1), jnp.concatenate([empty, row], axis=1)
        )
        own_grad[column] = dot_b(row, hidden)

    def feed_back(resid, saved, w_in, w_out, small_p, base, gradient):
        normed, active, slope = saved[:3]
        branch = gradient.astype(BF)
        small_grad[base + 2] = jnp.sum(branch, axis=0, dtype=F32, keepdims=True)
        branch = join_core(branch)
        grad_out = [dot_t(active[:, :width], branch, BF), dot_t(active[:, width:], branch, BF)]
        grad_hidden = jnp.concatenate([
            (dot_b(branch, w_out[:, :width]) * slope[:, :width]).astype(BF),
            (dot_b(branch, w_out[:, width:]) * slope[:, width:]).astype(BF),
        ], axis=1)
        put_hidden(base + 3, jnp.sum(grad_hidden, axis=0, dtype=F32))
        grad_in = dot_t(normed, grad_hidden, BF)
        grad_normed = sum_core(dot_b(grad_hidden, w_in))
        for one in [grad_in] + grad_out:
            grad_normed = after(grad_normed, one)
        back, small_grad[base], small_grad[base + 1] = norm_back(resid, small_p[base], grad_normed)
        return gradient + back, grad_in, grad_out

    def out_back(gradient, attended, weight, column):
        branch = gradient.astype(BF)
        small_grad[column] = jnp.sum(branch, axis=0, dtype=F32, keepdims=True)
        branch = join_core(branch)
        return dot_t(attended, branch, BF), dot_b(branch, weight, BF)

    def in_back(resid, normed, grad_proj, weight, small_p, column, gradient):
        grad_weight = dot_t(normed, grad_proj, BF)
        grad_normed = sum_core(dot_b(grad_proj, weight))
        if gradient is not None:
            grad_normed = after(grad_normed, grad_weight)
        back, small_grad[column], small_grad[column + 1] = norm_back(
            resid, small_p[column], grad_normed
        )
        return (back if gradient is None else gradient + back), grad_weight

    def along_x(*values):
        return scatter_x([v.reshape(4, 2 * rows, v.shape[1]) for v in values])

    def reduce(value):
        value = lax.psum_scatter(value, ("z", "y"), scatter_dimension=0, tiled=True)
        return lax.optimization_barrier(value)

    top = dot(out_cot[0], order)
    grad_two, g_d1, g_d2 = feed_back(dec_two, dec_ffn, w_d1, w_d2, small_p, 24, top)
    part_three = jnp.concatenate(g_d2 + [g_d1], axis=1)
    sum_three = reduce(part_three)

    g_co, grad_att = out_back(grad_two, cross_att, w_co, 23)
    cross_gq, ck0, cv0, ck1, cv1 = attend_back(
        False, cross_arrays + [(grad_att, 0)], src_keys, tgt_q, cross_lse, (part_three,)
    )
    cross_back = swap(jnp.concatenate([ck1, cv1], axis=1), "xl")
    put_own(21, jnp.sum(cross_gq, axis=0, dtype=F32, keepdims=True))
    grad_one, g_cq = in_back(dec_one, cross_norm, cross_gq, w_cq, small_p, 19, grad_two)

    g_so, grad_att = out_back(grad_one, self_att, w_so, 18)
    self_gq, sk0, sv0, sk1, sv1 = attend_back(
        True, dec_arrays + [(grad_att, 0)], tgt_keys, tgt_q, self_lse, (g_co, g_cq, g_so)
    )
    self_far = swap(jnp.concatenate([sk1, sv1], axis=1), "xl")
    dec_outs = repack_out((g_so, g_co))
    cross_gkv = after(jnp.concatenate([ck0, cv0], axis=1) + cross_back, self_gq).astype(BF)
    put_own(22, jnp.sum(cross_gkv[:, half:], axis=0, dtype=F32, keepdims=True))
    g_ckv = dot_t(memory, cross_gkv, BF)
    grad_memory = after(sum_core(dot_b(cross_gkv, w_ckv)), g_ckv)
    grad_memory = lax.reduce_precision(grad_memory, 8, 7)
    self_gkv = (jnp.concatenate([sk0, sv0], axis=1) + self_far).astype(BF)
    self_grad = jnp.concatenate([self_gq, self_gkv], axis=1)
    self_sum = jnp.sum(self_grad, axis=0, dtype=F32, keepdims=True)
    put_own(16, self_sum[:, :half])
    put_own(17, self_sum[:, 2 * half :])
    tgt_grad, g_dqkv = in_back(target, dec_norm, self_grad, w_dqkv, small_p, 14, grad_one)
    tgt_grad = reorder_wide(tgt_grad, order)

    enc_grad_two, small_grad[12], small_grad[13] = norm_back(
        enc_two, small_p[12], after(grad_memory, dec_outs)
    )

    enc_grad_one, g_e1, g_e2 = feed_back(enc_one, enc_ffn, w_e1, w_e2, small_p, 5, enc_grad_two)
    g_eo, grad_att = out_back(enc_grad_one, enc_att, w_eo, 4)
    part_two = jnp.concatenate(
        g_e2 + [g_e1, g_ckv, g_dqkv, g_cq, repack_out((g_eo,)), dec_outs], axis=1
    )
    sum_two = reduce(part_two)
    enc_gq, near, far = attend_pairs_back(
        enc_qkv, enc_qkv, pairs, enc_far, grad_att, src_keys, src_q, enc_lse, (part_two, sum_three)
    )
    enc_grad = jnp.concatenate(
        enc_gq + [(a + b).astype(BF) for a, b in zip(near, far)], axis=1
    )
    enc_sum = jnp.sum(enc_grad, axis=0, dtype=F32, keepdims=True)
    put_own(2, enc_sum[:, :half])
    put_own(3, enc_sum[:, 2 * half :])
    back, g_eqkv = in_back(source_e, enc_norm, enc_grad, w_eqkv, small_e, 0, None)
    src_grad = reorder_wide(enc_grad_one, order) + reorder_wide(back, order_e)
    own_grad[0] = dot_b(
        jnp.concatenate([small_grad.pop(0), small_grad.pop(1)], axis=0).astype(BF), order_e
    )

    stored = stack_rows(small_grad, LANES, width)
    owned = stack_rows(own_grad, LANES, width)
    owned = owned + dot_b(stored.astype(BF), order)
    g_small = lax.dot_general(
        order_e, owned.astype(BF), (((0,), (1,)), ((), ())), preferred_element_type=F32
    ).astype(BF)
    early = along_x(sum_three)
    sum_small = ring_scatter(g_small.reshape(4, quarter, LANES))
    sum_one = after(ring_scatter(g_eqkv.reshape(4, quarter, n_qkv)), g_small)
    sum_one = jnp.concatenate([sum_one.astype(BF), sum_small.astype(BF)], axis=1)
    sum_one = sum_by_trade(sum_one.reshape(16, 2 * rows, n_one), ("z", "y"))
    late = along_x(sum_two)
    sum_one = after(after(sum_one, early), late)
    s_eqkv, sum_small = sum_one[:, :n_qkv], sum_one[:, n_qkv:]

    s_d2, s_d1 = early[:, :hid], early[:, hid:]
    s_e2, s_e1, s_ckv, s_dqkv, s_cq = cut(late, 3, 8)
    s_eo, s_so, s_co = [late[:, late.shape[1] - j * half :][:, :half] for j in (3, 2, 1)]

    def from_cores(value):
        keep, send = pick(first_core, value[:rows], value[rows:])
        other = swap(send, "c")
        return pick(first_core, keep, other)

    low_small, high_small = from_cores(sum_small)
    grad_small = (low_small + high_small)[:, :n_small]
    lasts = early, s_eqkv, grad_small, late
    squares = sum(jnp.sum(part * part) for part in lasts)
    squares = jnp.full((8, LANES), squares)
    squares = squares + swap(squares, "c")
    squares = jnp.sum(gather_by_trade(squares, ("z", "xh", "y", "xl"), 64), axis=0)
    low, high = from_cores(jnp.concatenate([s_eqkv, s_e1, s_ckv, s_dqkv, s_cq, s_d1], axis=1))
    ups = jnp.stack([part[:, a : a + hid] for a in (n_qkv, low.shape[1] - hid) for part in (low, high)])
    ups = ups.reshape(2, 2, rows, 2, 4, quarter).transpose(0, 2, 4, 1, 3, 5).reshape(8 * rows, width)
    ups = reorder_wide(ups, hidden).reshape(2, rows, 2 * hid)

    def joined(start, count):
        at = [start + j * half for j in range(count)]
        return [part[:, a : a + half] for a in at for part in (low, high)]

    shards = [
        jnp.concatenate([part[:rows], part[rows:]], axis=1)
        for part in (s_eo, s_so, s_co)
    ] + [part[:, a : a + width] for part in (s_e2, s_d2) for a in (0, width)]
    shards = reorder_wide(jnp.concatenate(shards, axis=0), order)
    grad_enc = jnp.concatenate(joined(0, 3) + [shards[:rows], ups[0]], axis=1)
    at = n_qkv + hid
    grad_dec = jnp.concatenate(
        joined(at + 2 * half, 3) + [shards[rows : 2 * rows]] + joined(at + 5 * half, 1)
        + joined(at, 2) + [shards[2 * rows : 3 * rows], ups[1]], axis=1
    )
    shards = shards[3 * rows :]
    grad_down = jnp.concatenate([shards[:down_rows], shards[down_rows:]], axis=1)

    grad_norm = jnp.sqrt(squares[0, 0])
    factor = CLIP_LEVEL / jnp.maximum(grad_norm, CLIP_LEVEL)
    enc_all = adam_step(enc_master, enc_first, enc_second, grad_enc, factor, RATE_MATRIX, DECAY_RATE)
    dec_all = adam_step(dec_master, dec_first, dec_second, grad_dec, factor, RATE_MATRIX, DECAY_RATE)
    down_all = adam_step(
        down_master, down_first, down_second, grad_down, factor, RATE_MATRIX, DECAY_RATE
    )
    small_all_new = adam_step(
        small_master, small_first, small_second, grad_small, factor, RATE_SMALL, 0.0
    )
    return (
        dec_out[None], src_grad[None], tgt_grad[None], grad_norm,
        enc_all[0], dec_all[0], down_all[0], small_all_new[0],
        enc_all[1], dec_all[1], down_all[1], small_all_new[1],
        enc_all[2], dec_all[2], down_all[2], small_all_new[2],
        grad_small * factor,
    )


def solution(mesh):
    split = Mesh(mesh.devices.reshape(4, 2, 4, 2, 2), ALL_AXES)
    tokens = P(ROW_AXES, POS_AXES, None)
    marks = P(ROW_AXES, POS_AXES)
    shard = P(ALL_AXES, None)
    in_specs = (tokens,) * 3 + (marks,) * 4 + (shard,) * 12
    out_specs = (tokens,) * 3 + (P(),) + (shard,) * 13
    return jax.shard_map(
        per_device, mesh=split, in_specs=in_specs, out_specs=out_specs, check_vma=False
    )
```

```python
import jax
import jax.numpy as jnp
import numpy as np
from jax import lax
from jax.experimental import pallas as pl
from jax.experimental.pallas import tpu as pltpu
from jax.sharding import Mesh, PartitionSpec as P

HEAD = 64
STEP = 10
NORM_EPS = 1e-05
MASKED = -1000000000.0
BETA_FIRST = 0.9
BETA_SECOND = 0.999
ADAM_EPS = 1e-08
RATE_MATRIX = 0.1
RATE_SMALL = 0.5
DECAY_RATE = 0.01
CLIP_LEVEL = 1.0
BF = jnp.bfloat16
F32 = jnp.float32
PAIR = 2 * HEAD
LANES = 128
SMALL_ROWS = 32
ROW_AXES = ("z", "xh", "y")
POS_AXES = ("xl", "c")
ALL_AXES = ("z", "xh", "y", "xl", "c")
SWAP = [(0, 1), (1, 0)]


def swap(value, axis):
    return lax.ppermute(value, axis, SWAP)


def along_ring(value, by):
    return lax.ppermute(value, ("xh", "xl"), [(i, (i + by) % 4) for i in range(4)])


def ring_gather(value):
    h = value.shape[0] // 2
    before, after_it = along_ring(value, 1), along_ring(value, 3)
    far = [along_ring(before[:h], 1), along_ring(after_it[h:], 3)]
    return jnp.concatenate([value, before, after_it] + far, axis=0)


def ring_scatter(value):
    own, down, up, far = value
    h = own.shape[0] // 2
    up_more, down_more = along_ring(far[:h], 1), along_ring(far[h:], 3)
    up = jnp.concatenate([add_wide(up[:h], up_more).astype(BF), up[h:]], axis=0)
    down = jnp.concatenate([down[:h], add_wide(down[h:], down_more).astype(BF)], axis=0)
    return add_wide(own, along_ring(up, 1), along_ring(down, 3))


def flip(value, bits):
    return lax.ppermute(value, ("xh", "xl"), [(i, i ^ bits) for i in range(4)])


def join_core(value):
    return jnp.concatenate([value, swap(value, "c")], axis=0)


def far_half(partial):
    return swap(partial[partial.shape[0] // 2 :], "c")


def sum_core(partial):
    mine = partial.shape[0] // 2
    return partial[:mine] + swap(partial[mine:], "c")


def after(value, earlier):
    one = lax.slice(earlier, (0,) * earlier.ndim, (1,) * earlier.ndim)
    return value + one.reshape(()).astype(value.dtype) * 0


def add_wide(*values):
    total = values[0].astype(F32)
    for value in values[1:]:
        total = total + value.astype(F32)
    return total


def scatter_x(values):
    here = lax.axis_index("xh") * 2 + lax.axis_index("xl")

    def piece(spot):
        return jnp.concatenate(
            [lax.dynamic_index_in_dim(value, spot, 0, keepdims=False) for value in values], axis=1
        )

    total = piece(here).astype(F32)
    for bits in (1, 2, 3):
        total = total + flip(piece(here ^ bits), bits).astype(F32)
    return total


def gather_by_trade(value, axes, n):
    return lax.all_to_all(jnp.broadcast_to(value[None], (n,) + value.shape), axes, 0, 0)


def sum_by_trade(value, axes):
    return jnp.sum(lax.all_to_all(value, axes, 0, 0).astype(F32), axis=0)


def feature_order(width):
    rest = width // 32
    new = np.arange(width)
    z, y, xh, r = new // (8 * rest), (new // (2 * rest)) % 4, (new // rest) % 2, new % rest
    return ((z * 2 + xh) * 4 + y) * rest + r


def hidden_order(width):
    n = width // 64
    new = np.arange(width)
    c, g, y = new // (32 * n), (new // (16 * n)) % 2, (new // (4 * n)) % 4
    xh, xl, i = (new // (2 * n)) % 2, (new // n) % 2, new % n
    return ((((xh * 4 + y) * 2 + xl) * 2 + c) * 2 + g) * n + i


def head_order(width, core):
    r = width // 128
    own = np.arange(width // 2)
    z, xh = own // (32 * r), (own // (16 * r)) % 2
    y, xl, c, i = (own // (4 * r)) % 4, (own // (2 * r)) % 2, (own // r) % 2, own % r
    return np.concatenate([
        (c != core) * (width // 2) + ((((z * 4 + y) * 2 + xh) * 2 + xl) * 2 + cols) * r + i
        for cols in range(2)
    ])


def near_order(width, here):
    r = width // 128
    new = np.arange(width)
    x = (here + jnp.asarray((0, 3, 1, 2))[new // (32 * r)]) % 4
    z, y, c, i = (new // (8 * r)) % 4, (new // (2 * r)) % 4, (new // r) % 2, new % r
    return (((z * 2 + x // 2) * 4 + y) * 4 + (x % 2) * 2 + c) * r + i


def near_head_order(width, here, core):
    r = width // 128
    own = np.arange(width // 2)
    z, xh = own // (32 * r), (own // (16 * r)) % 2
    y, xl, c, i = (own // (4 * r)) % 4, (own // (2 * r)) % 2, (own // r) % 2, own % r
    apart = jnp.asarray((0, 2, 3, 1))[(xh * 2 + xl - here) % 4]
    return jnp.concatenate([
        (c != core) * (width // 2) + (((apart * 2 + z) * 4 + y) * 2 + cols) * r + i for cols in range(2)
    ])


def one_hot(picks, width):
    rows = lax.broadcasted_iota(jnp.int32, (width, picks.shape[0]), 0)
    return (rows == jnp.asarray(picks, jnp.int32)[None, :]).astype(BF)


def dot(left, right, kind=F32):
    return jnp.dot(left, right, preferred_element_type=kind)


def dot_t(left, right, kind=F32):
    return lax.dot_general(left, right, (((0,), (0,)), ((), ())), preferred_element_type=kind)


def dot_b(left, right, kind=F32):
    return lax.dot_general(left, right, (((1,), (1,)), ((), ())), preferred_element_type=kind)


def two_parts(value):
    high = lax.reduce_precision(value, 8, 7)
    return high.astype(BF), (value - high).astype(BF)


def reorder_wide(value, order):
    high, low = two_parts(value)
    both = dot_b(jnp.concatenate([high, low], axis=0), order)
    return both[: value.shape[0]] + both[value.shape[0] :]


def norm_stats(x):
    center = x - jnp.mean(x, axis=-1, keepdims=True)
    spread = jnp.mean(center * center, axis=-1, keepdims=True)
    scale = lax.rsqrt(spread + NORM_EPS)
    return center * scale, scale


def norm(x, gain, shift):
    unit, scale = norm_stats(x)
    return (unit * gain + shift).astype(BF)


def whole(array, rows=None):
    return pl.BlockSpec((rows or array.shape[0],) + array.shape[1:], lambda i: (0,) * array.ndim)


def norm_back(x, partial, far, small, gain, gradient, rounded, first=()):
    n, width = x.shape
    extra = () if gradient is None else (gradient,)

    def kernel(x_ref, near_ref, far_ref, small_ref, *refs):
        total_ref, branch_ref, rows_ref = refs[len(extra) + len(first) :]
        unit, scale = norm_stats(x_ref[...])
        grad = near_ref[...] + far_ref[...]
        if rounded:
            grad = grad.astype(BF).astype(F32)
        inner = grad * small_ref[gain : gain + 1, :]
        total = scale * (
            inner
            - jnp.mean(inner, axis=-1, keepdims=True)
            - unit * jnp.mean(inner * unit, axis=-1, keepdims=True)
        )
        if extra:
            total = total + refs[0][...]
        total_ref[...] = total
        branch = total.astype(BF)
        branch_ref[...] = branch
        rows_ref[...] = jnp.zeros(rows_ref.shape, F32)
        rows_ref[0:1, :] = jnp.sum(grad * unit, axis=0, keepdims=True)
        rows_ref[1:2, :] = jnp.sum(grad, axis=0, keepdims=True)
        rows_ref[2:3, :] = jnp.sum(branch.astype(F32), axis=0, keepdims=True)

    shapes = ((n, width), F32), ((n, width), BF), ((8, width), F32)
    return pl.pallas_call(
        kernel,
        grid=(1,),
        in_specs=[whole(x), whole(partial, n), whole(far), whole(small, SMALL_ROWS)]
        + [whole(e) for e in extra] + [pl.BlockSpec(memory_space=pl.ANY)] * len(first),
        out_specs=[pl.BlockSpec(shape, lambda i: (0, 0)) for shape, kind in shapes],
        out_shape=[jax.ShapeDtypeStruct(shape, kind) for shape, kind in shapes],
    )(x, partial, far, small, *extra, *first)


def gelu_parts(u):
    cdf = 0.5 * (1.0 + lax.erf(u * (0.5**0.5)))
    pdf = jnp.exp(-0.5 * u * u) * (1.0 / np.sqrt(2.0 * np.pi)).astype(np.float32)
    return u * cdf, cdf + u * pdf


def lane_mask(value, which):
    lane = lax.broadcasted_iota(jnp.int32, value.shape, 1)
    return jnp.where((lane // HEAD) == which, value, jnp.zeros_like(value))


def allowed_of(causal, ids_ref, qid_ref, part):
    seg = ids_ref[part, :, 0:1] == qid_ref[0:1, :]
    if causal:
        seg = seg & (ids_ref[part, :, 1:2] <= qid_ref[1:2, :])
    return seg


def scores_t(keys, query, allowed):
    raw = lax.dot_general(keys, query, (((1,), (1,)), ((), ())), preferred_element_type=F32)
    return jnp.where(allowed, raw, MASKED)


def attend_kernel(causal, q_ref, k0_ref, v0_ref, k1_ref, v1_ref, ids_ref, qid_ref, o_ref, lse_ref):
    query = q_ref[...] * jnp.asarray(HEAD**-0.5, BF)
    allowed = [allowed_of(causal, ids_ref, qid_ref, part) for part in range(2)]
    mixed = []
    for head in range(2):
        one = lane_mask(query, head)
        scores = [scores_t(ref[...], one, ok) for ref, ok in zip((k0_ref, k1_ref), allowed)]
        top = jnp.maximum(
            jnp.max(scores[0], axis=0, keepdims=True), jnp.max(scores[1], axis=0, keepdims=True)
        )
        expo = [jnp.exp(s - top) for s in scores]
        total = jnp.sum(expo[0], axis=0, keepdims=True) + jnp.sum(expo[1], axis=0, keepdims=True)
        share = 1.0 / total
        out = 0.0
        for ref, e in zip((v0_ref, v1_ref), expo):
            out = out + lax.dot_general(
                ref[...], (e * share).astype(BF), (((0,), (0,)), ((), ())), preferred_element_type=F32
            )
        mixed.append(out)
        lse_ref[0, head : head + 1, :] = top + jnp.log(total)
    both = jnp.concatenate([mixed[0][:HEAD], mixed[1][HEAD:]], axis=0)
    o_ref[...] = both.T.astype(BF)


def attend_back_kernel(
    causal, q_ref, k0_ref, v0_ref, k1_ref, v1_ref, g_ref, ids_ref, qid_ref, lse_ref,
    dq_ref, dk0_ref, dv0_ref, dk1_ref, dv1_ref,
):
    query = q_ref[...] * jnp.asarray(HEAD**-0.5, BF)
    grad = g_ref[...]
    allowed = [allowed_of(causal, ids_ref, qid_ref, part) for part in range(2)]
    keys = (k0_ref[...], k1_ref[...])
    values = (v0_ref[...], v1_ref[...])
    grad_q = 0.0
    grad_k = [0.0, 0.0]
    grad_v = [0.0, 0.0]
    for head in range(2):
        one = lane_mask(query, head)
        grad_one = lane_mask(grad, head)
        lse = lse_ref[0, head : head + 1, :]
        probs = [jnp.exp(scores_t(k, one, ok) - lse) for k, ok in zip(keys, allowed)]
        grad_p = [
            lax.dot_general(v, grad_one, (((1,), (1,)), ((), ())), preferred_element_type=F32)
            for v in values
        ]
        inner = jnp.sum(probs[0] * grad_p[0], axis=0, keepdims=True) + jnp.sum(
            probs[1] * grad_p[1], axis=0, keepdims=True
        )
        for part in range(2):
            grad_s = (probs[part] * (grad_p[part] - inner)).astype(BF)
            grad_v[part] = grad_v[part] + dot(probs[part].astype(BF), grad_one)
            grad_k[part] = grad_k[part] + dot(grad_s, one)
            grad_q = grad_q + lax.dot_general(
                lane_mask(keys[part], head), grad_s, (((0,), (0,)), ((), ())),
                preferred_element_type=F32,
            )
    dq_ref[...] = (grad_q * HEAD**-0.5).T.astype(BF)
    dk0_ref[...] = grad_k[0]
    dv0_ref[...] = grad_v[0]
    dk1_ref[...] = grad_k[1].astype(BF)
    dv1_ref[...] = grad_v[1].astype(BF)


def call_kernel(body, causal, arrays, ids, qid, extra, first, out_shape, out_specs):
    in_specs = [
        pl.BlockSpec(
            (a[0].shape[0], PAIR), lambda p, at=a[1], step=(a + (1,))[2]: (0, at + p * step)
        )
        for a in arrays
    ]
    in_specs.append(pl.BlockSpec(ids.shape, lambda p: (0, 0, 0)))
    in_specs.append(pl.BlockSpec(qid.shape, lambda p: (0, 0)))
    in_specs += [pl.BlockSpec((1,) + e.shape[1:], lambda p: (p, 0, 0)) for e in extra]

    in_specs += [pl.BlockSpec(memory_space=pl.ANY) for f in first]
    n_in = len(in_specs)

    def kernel(*refs):
        body(causal, *refs[: n_in - len(first)], *refs[n_in:])

    pairs = extra[0].shape[0] if extra else out_shape[1].shape[0]
    return pl.pallas_call(
        kernel,
        grid=(pairs,),
        in_specs=in_specs,
        out_specs=out_specs,
        out_shape=out_shape,
        compiler_params=pltpu.CompilerParams(vmem_limit_bytes=56 * 1024 * 1024),
        cost_estimate=pl.CostEstimate(flops=0, bytes_accessed=0, transcendentals=0),
    )(*[a[0] for a in arrays], ids, qid, *extra, *first)


def attend_fwd(causal, arrays, ids, qid, pairs, first=()):
    n_q = qid.shape[1]
    out_shape = (
        jax.ShapeDtypeStruct((n_q, pairs * PAIR), BF),
        jax.ShapeDtypeStruct((pairs, 2, n_q), F32),
    )
    out_specs = (
        pl.BlockSpec((n_q, PAIR), lambda p: (0, p)),
        pl.BlockSpec((1, 2, n_q), lambda p: (p, 0, 0)),
    )
    return call_kernel(
        attend_kernel, causal, arrays, ids, qid, (), first, out_shape, out_specs,
    )


def attend_back(causal, arrays, ids, qid, lse, first=()):
    pairs, n_q, n_k = lse.shape[0], qid.shape[1], ids.shape[1]
    wide = pairs * PAIR
    out_shape = (
        jax.ShapeDtypeStruct((n_q, wide), BF),
        jax.ShapeDtypeStruct((n_k, wide), F32),
        jax.ShapeDtypeStruct((n_k, wide), F32),
        jax.ShapeDtypeStruct((n_k, wide), BF),
        jax.ShapeDtypeStruct((n_k, wide), BF),
    )
    out_specs = tuple(pl.BlockSpec((s.shape[0], PAIR), lambda p: (0, p)) for s in out_shape)
    return call_kernel(
        attend_back_kernel, causal, arrays, ids, qid, (lse,), first, out_shape, out_specs,
    )


def join_grads(queries, near, far):
    fars = list({id(f): f for f, at in far}.values())
    n, k = near[0].shape[0], len(queries)
    width = sum(v.shape[1] for v in list(queries) + list(near))

    def kernel(*refs):
        out, at = refs[-1], 0
        for ref in refs[:k]:
            out[:, at : at + ref.shape[1]] = ref[...]
            at += ref.shape[1]
        far_refs = dict(zip([id(f) for f in fars], refs[k + len(near) : -1]))
        for ref, (f, first) in zip(refs[k : k + len(near)], far):
            w = ref.shape[1]
            total = ref[...] + far_refs[id(f)][:, first : first + w].astype(F32)
            out[:, at : at + w] = total.astype(BF)
            at += w

    arrays = list(queries) + list(near) + fars
    return pl.pallas_call(
        kernel,
        grid=(1,),
        in_specs=[whole(a) for a in arrays],
        out_specs=pl.BlockSpec((n, width), lambda i: (0, 0)),
        out_shape=jax.ShapeDtypeStruct((n, width), BF),
        compiler_params=pltpu.CompilerParams(vmem_limit_bytes=56 * 1024 * 1024),
    )(*arrays)


def far_pairs(keys_values, pairs):
    half = pairs * PAIR
    return [
        swap(jnp.concatenate([
            keys_values[:, p * PAIR : (p + 1) * PAIR],
            keys_values[:, half + p * PAIR : half + (p + 1) * PAIR],
        ], axis=1), "xl")
        for p in range(pairs)
    ]


def attend_pairs(query, near, at, far, ids, qid, pairs, first=()):
    done = []
    for p in range(pairs):
        arrays = [(query, p), (near, at + p), (near, at + pairs + p), (far[p], 0), (far[p], 1)]
        done.append(attend_fwd(False, arrays, ids, qid, 1, first))
    return jnp.concatenate([d[0] for d in done], axis=1), [d[1] for d in done]


def attend_pairs_back(query, near, at, far, grad, ids, qid, lse, first=()):
    pairs = len(lse)
    grad_q, near_k, near_v, sent = [], [], [], []
    for p in range(pairs):
        arrays = [
            (query, p), (near, at + p), (near, at + pairs + p), (far[p], 0), (far[p], 1), (grad, p)
        ]
        gq, k0, v0, k1, v1 = attend_back(False, arrays, ids, qid, lse[p], first)
        grad_q.append(gq)
        near_k.append(k0)
        near_v.append(v0)
        sent.append(swap(jnp.concatenate([k1, v1], axis=1), "xl"))
    return grad_q, near_k + near_v, [(f, 0) for f in sent] + [(f, PAIR) for f in sent]


def adam_step(master, first, second, gradient, factor, rate, decay):
    clipped = gradient * factor
    first_new = BETA_FIRST * first + (1 - BETA_FIRST) * clipped
    second_new = BETA_SECOND * second + (1 - BETA_SECOND) * clipped * clipped
    first_hat = first_new / (1 - BETA_FIRST**STEP)
    second_hat = second_new / (1 - BETA_SECOND**STEP)
    master_new = master - rate * (first_hat / (jnp.sqrt(second_hat) + ADAM_EPS) + decay * master)
    return (master_new, first_new, second_new)


def per_device(
    src_x, tgt_x, out_cot, src_seg, tgt_seg, src_pad, tgt_pad,
    enc_master, dec_master, down_master, small_master,
    enc_first, dec_first, down_first, small_first,
    enc_second, dec_second, down_second, small_second,
):
    width = src_x.shape[-1]
    half = width // 2
    hid = 2 * width
    pairs = half // PAIR
    rows = enc_master.shape[0]
    down_rows = down_master.shape[0]
    n_small = small_master.shape[1]
    core = lax.axis_index("c")
    first_core = core == 0
    order = one_hot(feature_order(width), width)
    hidden = one_hot(hidden_order(width), width)
    place = one_hot(jnp.where(first_core, head_order(width, 0), head_order(width, 1)), width)
    quarter = width // 4
    here = lax.axis_index("xh") * 2 + lax.axis_index("xl")
    order_e = one_hot(near_order(width, here), width)
    place_e = one_hot(near_head_order(width, here, core), width)

    encb, decb, downb = enc_master.astype(BF), dec_master.astype(BF), down_master.astype(BF)
    smallb = jnp.pad(small_master.astype(BF), ((0, 0), (0, LANES - n_small)))

    def block(matrix, index):
        return matrix[:, index * width : (index + 1) * width]

    def halves(matrix):
        n = matrix.shape[1] // 2
        return matrix[:, :n], matrix[:, n:]

    ups = jnp.concatenate([encb[:, 4 * width :], decb[:, 8 * width :]], axis=0).reshape(-1, width)
    ups = dot(ups, hidden, BF).reshape(2, rows, 4, 2, 2, quarter)

    def up_halves(index):
        return [
            jnp.concatenate([ups[index, :, z, c, g] for g in range(2) for z in range(4)], axis=1)
            for c in range(2)
        ]

    col_blocks = [
        halves(block(encb, 0)), halves(block(encb, 1)), halves(block(encb, 2)), (smallb, smallb),
        up_halves(0), halves(block(decb, 5)), halves(block(decb, 6)),
        halves(block(decb, 0)), halves(block(decb, 1)), halves(block(decb, 2)), halves(block(decb, 4)),
        up_halves(1),
    ]
    cols0 = jnp.concatenate([b[0] for b in col_blocks], axis=1)
    cols1 = jnp.concatenate([b[1] for b in col_blocks], axis=1)
    mine = jnp.where(first_core, cols0, cols1)
    theirs = swap(jnp.where(first_core, cols1, cols0), "c")
    cols = jnp.concatenate(
        [jnp.where(first_core, mine, theirs), jnp.where(first_core, theirs, mine)], axis=0
    )
    shards = dot(jnp.concatenate(
        [block(encb, 3), block(decb, 3), block(decb, 7), downb[:, :width], downb[:, width:]], axis=0
    ), order, BF)
    out_rows = [shards[j * rows : (j + 1) * rows] for j in range(3)]
    out_rows = jnp.concatenate([
        jnp.concatenate([part[:, :half] for part in out_rows], axis=1),
        jnp.concatenate([part[:, half:] for part in out_rows], axis=1),
    ], axis=0)

    def down_packed(index):
        at = 3 * rows + index * down_rows
        middle = at + down_rows // 2
        return jnp.concatenate([shards[at:middle], shards[middle : at + down_rows]], axis=1)

    n_qkv, n_one = 3 * half, 3 * half + LANES
    n_up = cols.shape[1] - hid
    packed_one = jnp.concatenate([cols[:, :n_one], out_rows[:, :half]], axis=1)
    packed = jnp.concatenate([
        down_packed(0), cols[:, n_one:n_up], out_rows[:, half:], down_packed(1), cols[:, n_up:]
    ], axis=1)
    sizes = (n_qkv, LANES, half, hid, hid, 2 * half, n_qkv, half, 2 * half, hid, hid)
    starts = [int(v) for v in np.cumsum((0,) + sizes)]
    full_one = gather_by_trade(packed_one, ("z", "y"), 16).reshape(width // 4, starts[3])
    found = [packed, flip(packed, 1), flip(packed, 2), flip(after(packed, full_one), 3)]
    full_one = ring_gather(full_one)
    packed = []
    for spot in range(4):
        part = found[0]
        for bits in (1, 2, 3):
            part = jnp.where((here ^ bits) == spot, found[bits], part)
        packed.append(part)
    packed = jnp.concatenate(packed, axis=0)
    full_two = lax.all_gather(packed[:, : starts[9] - starts[3]], ("z", "y"), axis=0, tiled=True)
    packed_three = packed[:, starts[9] - starts[3] :]
    full_three = lax.all_gather(packed_three, ("z", "y"), axis=0, tiled=True)

    def cut(full, first, last):
        base = starts[first]
        return [full[:, starts[j] - base : starts[j + 1] - base] for j in range(first, last)]

    w_eqkv, small_all, w_eo = cut(full_one, 0, 3)
    w_e2, w_e1, w_ckv, w_dqkv, w_cq, w_out = cut(full_two, 3, 9)
    w_d2, w_d1 = cut(full_three, 9, 11)

    def pick(which, low, high):
        return jnp.where(which, low, high), jnp.where(which, high, low)

    def unpack_out(low, high, place, count):
        kept, sent = pick(first_core, low, high)
        stored = dot_t(place, jnp.concatenate([kept, swap(sent, "c")], axis=0), BF)
        return [
            jnp.concatenate([stored[:half, cut], stored[half:, cut]], axis=1)
            for cut in (slice(j * half, (j + 1) * half) for j in range(count))
        ]

    def repack_out(grads):
        stacked = jnp.concatenate([
            jnp.concatenate([g[:, :half] for g in grads], axis=1),
            jnp.concatenate([g[:, half:] for g in grads], axis=1),
        ], axis=0)
        stored = dot(place, stacked, BF)
        low, high = pick(first_core, stored[:half], swap(stored[half:], "c"))
        return jnp.concatenate([low, high], axis=0)

    eye = one_hot(np.arange(width), width)
    small_e = dot_t(small_all, eye)
    small_own = dot_b(small_all.T, order_e)
    small_p = dot(small_own.astype(BF), order)

    def own_half(column):
        row = small_own[column]
        return jnp.where(first_core, row[:half], row[half:])

    def hidden_bias(column):
        stored = dot(after(small_own[column : column + 4], enc_qkv).astype(BF), hidden)
        stored = jnp.where(first_core, stored[:, :half], stored[:, half:])
        return stored.reshape(4, 2, quarter).transpose(1, 0, 2).reshape(1, hid)

    none = jnp.zeros((half,), F32)

    def ids_of(seg, pad, at):
        n = seg.shape[1]
        spot = (lax.axis_index("xl") * 2 + core) * n + jnp.arange(n, dtype=jnp.int32)
        key = jnp.where(pad[0] == 1, seg[0], -1)
        return jnp.stack([key, spot, seg[0]], axis=1)

    src_ids = join_core(ids_of(src_seg, src_pad, 0))
    tgt_ids = join_core(ids_of(tgt_seg, tgt_pad, 0))
    src_keys = jnp.stack([src_ids[:, :2], swap(src_ids[:, :2], "xl")])
    tgt_keys = jnp.stack([tgt_ids[:, :2], swap(tgt_ids[:, :2], "xl")])
    src_q = jnp.stack([src_ids[:, 2], src_ids[:, 1]])
    tgt_q = jnp.stack([tgt_ids[:, 2], tgt_ids[:, 1]])

    source = dot(src_x[0], order)
    source_e = dot(src_x[0], order_e)
    enc_norm = join_core(norm(source_e, small_e[0], small_e[1]))
    enc_qkv = (dot(enc_norm, w_eqkv) + jnp.concatenate([own_half(2), none, own_half(3)])).astype(BF)
    enc_far = far_pairs(enc_qkv[:, half:], pairs)

    target = dot(tgt_x[0], order)

    bias_e, bias_d = hidden_bias(8), hidden_bias(27)
    enc_att, enc_lse = attend_pairs(
        enc_qkv, enc_qkv, pairs, enc_far, src_keys, src_q, pairs, (packed_three, bias_e, bias_d)
    )
    by_z = after(w_eo, enc_qkv).reshape(4, 2, 16 * rows, half)
    w_eo, = unpack_out(by_z[:, 0].reshape(half, half), by_z[:, 1].reshape(half, half), place_e, 1)
    dec_norm = join_core(after(norm(target, small_p[14], small_p[15]), enc_att))
    dec_qkv = (dot(dec_norm, w_dqkv) + jnp.concatenate([own_half(16), none, own_half(17)])).astype(BF)
    dec_far = swap(dec_qkv[:, half:], "xl")

    def feed_fwd(normed, w_in, w_out, bias):
        active, slope = gelu_parts(dot(normed, w_in) + bias)
        active = active.astype(BF)
        out = dot(active[:, :width], w_out[:, :width]) + dot(active[:, width:], w_out[:, width:])
        return active, slope, out

    enc_one = source + sum_core(dot(enc_att, w_eo)) + small_p[4]
    enc_feed = join_core(after(norm(enc_one, small_p[5], small_p[6]), dec_qkv))
    enc_active, enc_slope, part = feed_fwd(enc_feed, w_e1, w_e2, bias_e)
    enc_two = enc_one + sum_core(part) + small_p[7]
    memory = join_core(norm(enc_two, small_p[12], small_p[13]))

    dec_arrays = [(dec_qkv, 0), (dec_qkv, pairs), (dec_qkv, 2 * pairs), (dec_far, 0), (dec_far, pairs)]
    cross_kv = (dot(memory, w_ckv) + jnp.concatenate([none, own_half(22)])).astype(BF)
    cross_far = far_pairs(cross_kv, pairs)
    w_out = after(w_out, enc_two)
    w_so, w_co = unpack_out(w_out[:half], w_out[half:], place, 2)
    self_att, self_lse = attend_fwd(
        True, dec_arrays, tgt_keys, tgt_q, pairs, (cross_kv, w_so, w_co, cross_far[0])
    )
    dec_one = target + sum_core(dot(self_att, w_so)) + small_p[18]
    cross_norm = join_core(norm(dec_one, small_p[19], small_p[20]))
    cross_q = (dot(cross_norm, w_cq) + own_half(21)).astype(BF)
    cross_att, cross_lse = attend_pairs(cross_q, cross_kv, 0, cross_far, src_keys, tgt_q, pairs)
    cross_far, cross_lse = jnp.concatenate(cross_far, axis=1), jnp.concatenate(cross_lse, axis=0)
    cross_arrays = [(cross_q, 0), (cross_kv, 0), (cross_kv, pairs), (cross_far, 0, 2), (cross_far, 1, 2)]
    dec_two = dec_one + sum_core(dot(cross_att, w_co)) + small_p[23]
    dec_feed = join_core(norm(dec_two, small_p[24], small_p[25]))
    dec_active, dec_slope, part = feed_fwd(dec_feed, w_d1, w_d2, bias_d)
    dec_out = reorder_wide(dec_two + sum_core(part) + small_p[26], order)

    ones = jnp.ones((8, 2 * src_x.shape[1]), BF)

    def column_sums(value):
        return dot(ones[:, : value.shape[0]], value)

    def feed_back(branch, normed, active, slope, w_in, w_out):
        grad_out = [dot_t(active[:, :width], branch, BF), dot_t(active[:, width:], branch, BF)]
        grad_hidden = jnp.concatenate([
            (dot_b(branch, w_out[:, :width]) * slope[:, :width]).astype(BF),
            (dot_b(branch, w_out[:, width:]) * slope[:, width:]).astype(BF),
        ], axis=1)
        grad_in = dot_t(normed, grad_hidden, BF)
        return column_sums(grad_hidden), grad_in, grad_out, dot_b(grad_hidden, w_in)

    def along_x(*values):
        return scatter_x([v.reshape(4, 2 * rows, v.shape[1]) for v in values])

    def reduce(value):
        value = lax.psum_scatter(value, ("z", "y"), scatter_dimension=0, tiled=True)
        return lax.optimization_barrier(value)

    top = dot(out_cot[0], order)
    rows_top = column_sums(top.astype(BF))
    branch = join_core(top.astype(BF))
    hidden_d, g_d1, g_d2, part = feed_back(branch, dec_feed, dec_active, dec_slope, w_d1, w_d2)
    part_three = jnp.concatenate(g_d2 + [g_d1], axis=1)
    sum_three = reduce(part_three)
    grad_two, branch, rows_24 = norm_back(dec_two, part, far_half(part), small_p, 24, top, False)

    branch = join_core(branch)
    grad_att = dot_b(branch, w_co, BF)
    cross_gq, ck0, cv0, ck1, cv1 = attend_back(
        False, cross_arrays + [(grad_att, 0)], src_keys, tgt_q, cross_lse, (part_three,)
    )
    cross_back = swap(jnp.concatenate([ck1, cv1], axis=1), "xl")
    g_co, g_cq = dot_t(cross_att, branch, BF), dot_t(cross_norm, cross_gq, BF)
    part = dot_b(cross_gq, w_cq)
    grad_one, branch, rows_19 = norm_back(
        dec_one, part, far_half(part), small_p, 19, grad_two, False, (g_cq,)
    )

    branch = join_core(branch)
    grad_att = dot_b(branch, w_so, BF)
    g_so = dot_t(self_att, branch, BF)
    self_gq, sk0, sv0, sk1, sv1 = attend_back(
        True, dec_arrays + [(grad_att, 0)], tgt_keys, tgt_q, self_lse, (g_co, g_cq, g_so)
    )
    self_far = swap(jnp.concatenate([sk1, sv1], axis=1), "xl")
    dec_outs = repack_out((g_so, g_co))
    cross_gkv = after(jnp.concatenate([ck0, cv0], axis=1) + cross_back, self_gq).astype(BF)
    part = dot_b(cross_gkv, w_ckv)
    g_ckv = dot_t(memory, cross_gkv, BF)
    enc_grad_two, branch, rows_12 = norm_back(
        enc_two, part, far_half(part), small_p, 12, None, True, (g_ckv, dec_outs)
    )

    self_gkv = (jnp.concatenate([sk0, sv0], axis=1) + self_far).astype(BF)
    self_grad = jnp.concatenate([self_gq, self_gkv], axis=1)
    g_dqkv = dot_t(dec_norm, self_grad, BF)

    branch = join_core(branch)
    hidden_e, g_e1, g_e2, part = feed_back(branch, enc_feed, enc_active, enc_slope, w_e1, w_e2)
    enc_grad_one, branch, rows_5 = norm_back(
        enc_one, part, far_half(part), small_p, 5, enc_grad_two, False, (g_e1, g_e2[0], g_e2[1])
    )
    branch = join_core(branch)
    grad_att, g_eo = dot_b(branch, w_eo, BF), dot_t(enc_att, branch, BF)
    part_two = jnp.concatenate(
        g_e2 + [g_e1, g_ckv, g_dqkv, g_cq, repack_out((g_eo,)), dec_outs], axis=1
    )
    sum_two = reduce(part_two)
    enc_gq, near, far = attend_pairs_back(
        enc_qkv, enc_qkv, pairs, enc_far, grad_att, src_keys, src_q, enc_lse, (part_two, sum_three)
    )
    self_grad_late = after(self_grad, enc_gq[-1])
    part = dot_b(self_grad_late, w_dqkv)
    tgt_grad, _, rows_14 = norm_back(target, part, far_half(part), small_p, 14, grad_one, False)

    near[0] = after(near[0], rows_14)
    enc_grad = join_grads(enc_gq, near, far)
    g_eqkv = dot_t(enc_norm, enc_grad, BF)
    part = dot_b(enc_grad, w_eqkv)
    back, _, rows_0 = norm_back(source_e, part, far_half(part), small_e, 0, None, False)
    src_grad = reorder_wide(enc_grad_one, order) + reorder_wide(back, order_e)

    tgt_grad = reorder_wide(tgt_grad, order)

    blocks = [rows_24, rows_19, rows_14, rows_12, rows_5, rows_top]
    columns = [(24, 25, 23), (19, 20, 18), (14, 15), (12, 13, 7), (5, 6, 4), (26,), (0, 1)]
    own_rows = [dot_b(jnp.concatenate(blocks, axis=0).astype(BF), order), dot_b(rows_0.astype(BF), order_e)]
    by_z = jnp.concatenate([
        jnp.concatenate([value[:, z * quarter :][:, :quarter], value[:, half * 2 + z * quarter :][:, :quarter]], axis=1)
        for value in (hidden_e, hidden_d) for z in range(4)
    ], axis=0)
    own_rows.append(dot_b(
        by_z.astype(BF), jnp.where(first_core, hidden[:, :half], hidden[:, half:])
    ))
    columns += [(c,) for base in (8, 27) for c in range(base, base + 4)]
    own_rows = jnp.concatenate(own_rows, axis=0).astype(BF)
    picks = np.full(LANES, -1)
    for j, names in enumerate(columns):
        for i, column in enumerate(names):
            picks[column] = 8 * j + i
    own_rows = dot_t(own_rows, one_hot(picks, own_rows.shape[0]), BF)

    sums = [column_sums(value) for value in (enc_grad, self_grad_late, cross_gq, cross_gkv[:, half:])]
    half_rows = jnp.concatenate(
        [sums[0][:, :half], sums[0][:, 2 * half :], sums[1][:, :half], sums[1][:, 2 * half :], sums[2], sums[3]],
        axis=0,
    ).astype(BF)
    picks = np.full(LANES, -1)
    for j, column in enumerate((2, 3, 16, 17, 21, 22)):
        picks[column] = 8 * j
    half_rows = dot_t(half_rows, one_hot(picks, 48), BF)
    empty = jnp.zeros_like(half_rows)
    own_rows = own_rows + jnp.where(
        first_core,
        jnp.concatenate([half_rows, empty], axis=0), jnp.concatenate([empty, half_rows], axis=0),
    )
    g_small = dot_t(order_e, own_rows, BF)
    early = along_x(sum_three)
    sum_small = ring_scatter(g_small.reshape(4, quarter, LANES))
    sum_one = after(ring_scatter(g_eqkv.reshape(4, quarter, n_qkv)), g_small)
    sum_one = jnp.concatenate([sum_one.astype(BF), sum_small.astype(BF)], axis=1)
    sum_one = sum_by_trade(sum_one.reshape(16, 2 * rows, n_one), ("z", "y"))
    late = along_x(sum_two)
    sum_one = after(after(sum_one, early), late)
    s_eqkv, sum_small = sum_one[:, :n_qkv], sum_one[:, n_qkv:]

    s_d2, s_d1 = early[:, :hid], early[:, hid:]
    s_e2, s_e1, s_ckv, s_dqkv, s_cq = cut(late, 3, 8)
    s_eo, s_so, s_co = [late[:, late.shape[1] - j * half :][:, :half] for j in (3, 2, 1)]

    def from_cores(value):
        keep, send = pick(first_core, value[:rows], value[rows:])
        other = swap(send, "c")
        return pick(first_core, keep, other)

    low_small, high_small = from_cores(sum_small)
    grad_small = (low_small + high_small)[:, :n_small]
    lasts = early, s_eqkv, grad_small, late
    squares = sum(jnp.sum(part * part) for part in lasts)
    squares = jnp.full((8, LANES), squares)
    squares = squares + swap(squares, "c")
    squares = jnp.sum(gather_by_trade(squares, ("z", "xh", "y", "xl"), 64), axis=0)
    low, high = from_cores(jnp.concatenate([s_eqkv, s_e1, s_ckv, s_dqkv, s_cq, s_d1], axis=1))
    ups = jnp.stack([part[:, a : a + hid] for a in (n_qkv, low.shape[1] - hid) for part in (low, high)])
    ups = ups.reshape(2, 2, rows, 2, 4, quarter).transpose(0, 2, 4, 1, 3, 5).reshape(8 * rows, width)
    ups = reorder_wide(ups, hidden).reshape(2, rows, 2 * hid)

    def joined(start, count):
        at = [start + j * half for j in range(count)]
        return [part[:, a : a + half] for a in at for part in (low, high)]

    shards = [
        jnp.concatenate([part[:rows], part[rows:]], axis=1)
        for part in (s_eo, s_so, s_co)
    ] + [part[:, a : a + width] for part in (s_e2, s_d2) for a in (0, width)]
    shards = reorder_wide(jnp.concatenate(shards, axis=0), order)
    grad_enc = jnp.concatenate(joined(0, 3) + [shards[:rows], ups[0]], axis=1)
    at = n_qkv + hid
    grad_dec = jnp.concatenate(
        joined(at + 2 * half, 3) + [shards[rows : 2 * rows]] + joined(at + 5 * half, 1)
        + joined(at, 2) + [shards[2 * rows : 3 * rows], ups[1]], axis=1
    )
    shards = shards[3 * rows :]
    grad_down = jnp.concatenate([shards[:down_rows], shards[down_rows:]], axis=1)

    grad_norm = jnp.sqrt(squares[0, 0])
    factor = CLIP_LEVEL / jnp.maximum(grad_norm, CLIP_LEVEL)
    enc_all = adam_step(enc_master, enc_first, enc_second, grad_enc, factor, RATE_MATRIX, DECAY_RATE)
    dec_all = adam_step(dec_master, dec_first, dec_second, grad_dec, factor, RATE_MATRIX, DECAY_RATE)
    down_all = adam_step(
        down_master, down_first, down_second, grad_down, factor, RATE_MATRIX, DECAY_RATE
    )
    small_all_new = adam_step(
        small_master, small_first, small_second, grad_small, factor, RATE_SMALL, 0.0
    )
    return (
        dec_out[None], src_grad[None], tgt_grad[None], grad_norm,
        enc_all[0], dec_all[0], down_all[0], small_all_new[0],
        enc_all[1], dec_all[1], down_all[1], small_all_new[1],
        enc_all[2], dec_all[2], down_all[2], small_all_new[2],
        grad_small * factor,
    )


def solution(mesh):
    split = Mesh(mesh.devices.reshape(4, 2, 4, 2, 2), ALL_AXES)
    tokens = P(ROW_AXES, POS_AXES, None)
    marks = P(ROW_AXES, POS_AXES)
    shard = P(ALL_AXES, None)
    in_specs = (tokens,) * 3 + (marks,) * 4 + (shard,) * 12
    out_specs = (tokens,) * 3 + (P(),) + (shard,) * 13
    return jax.shard_map(
        per_device, mesh=split, in_specs=in_specs, out_specs=out_specs, check_vma=False
    )
```

```python
import jax
import jax.numpy as jnp
import numpy as np
from jax import lax
from jax.experimental import pallas as pl
from jax.experimental.pallas import tpu as pltpu
from jax.sharding import Mesh, PartitionSpec as P

HEAD = 64
STEP = 10
NORM_EPS = 1e-05
MASKED = -1000000000.0
BETA_FIRST = 0.9
BETA_SECOND = 0.999
ADAM_EPS = 1e-08
RATE_MATRIX = 0.1
RATE_SMALL = 0.5
DECAY_RATE = 0.01
CLIP_LEVEL = 1.0
BF = jnp.bfloat16
F32 = jnp.float32
PAIR = 2 * HEAD
LANES = 128
SMALL_ROWS = 32
ROW_AXES = ("z", "xh", "y")
POS_AXES = ("xl", "c")
ALL_AXES = ("z", "xh", "y", "xl", "c")
SWAP = [(0, 1), (1, 0)]


def swap(value, axis):
    return lax.ppermute(value, axis, SWAP)


def along_ring(value, by):
    return lax.ppermute(value, ("xh", "xl"), [(i, (i + by) % 4) for i in range(4)])


def ring_gather(value):
    h = value.shape[0] // 2
    before, after_it = along_ring(value, 1), along_ring(value, 3)
    far = [along_ring(before[:h], 1), along_ring(after_it[h:], 3)]
    return jnp.concatenate([value, before, after_it] + far, axis=0)


def ring_scatter(value):
    own, down, up, far = value
    h = own.shape[0] // 2
    up_more, down_more = along_ring(far[:h], 1), along_ring(far[h:], 3)
    up = jnp.concatenate([add_wide(up[:h], up_more).astype(BF), up[h:]], axis=0)
    down = jnp.concatenate([down[:h], add_wide(down[h:], down_more).astype(BF)], axis=0)
    return add_wide(own, along_ring(up, 1), along_ring(down, 3))


def flip(value, bits):
    return lax.ppermute(value, ("xh", "xl"), [(i, i ^ bits) for i in range(4)])


def join_core(value):
    return jnp.concatenate([value, swap(value, "c")], axis=0)


def far_half(partial):
    return swap(partial[partial.shape[0] // 2 :], "c")


def sum_core(partial):
    mine = partial.shape[0] // 2
    return partial[:mine] + swap(partial[mine:], "c")


def after(value, earlier):
    one = lax.slice(earlier, (0,) * earlier.ndim, (1,) * earlier.ndim)
    return value + one.reshape(()).astype(value.dtype) * 0


def add_wide(*values):
    total = values[0].astype(F32)
    for value in values[1:]:
        total = total + value.astype(F32)
    return total


def scatter_x(values):
    here = lax.axis_index("xh") * 2 + lax.axis_index("xl")

    def piece(spot):
        return jnp.concatenate(
            [lax.dynamic_index_in_dim(value, spot, 0, keepdims=False) for value in values], axis=1
        )

    total = piece(here).astype(F32)
    for bits in (1, 2, 3):
        total = total + flip(piece(here ^ bits), bits).astype(F32)
    return total


def gather_by_trade(value, axes, n):
    return lax.all_to_all(jnp.broadcast_to(value[None], (n,) + value.shape), axes, 0, 0)


def sum_by_trade(value, axes):
    return jnp.sum(lax.all_to_all(value, axes, 0, 0).astype(F32), axis=0)


def feature_order(width):
    rest = width // 32
    new = np.arange(width)
    z, y, xh, r = new // (8 * rest), (new // (2 * rest)) % 4, (new // rest) % 2, new % rest
    return ((z * 2 + xh) * 4 + y) * rest + r


def hidden_order(width):
    n = width // 64
    new = np.arange(width)
    c, g, y = new // (32 * n), (new // (16 * n)) % 2, (new // (4 * n)) % 4
    xh, xl, i = (new // (2 * n)) % 2, (new // n) % 2, new % n
    return ((((xh * 4 + y) * 2 + xl) * 2 + c) * 2 + g) * n + i


def head_order(width, core):
    r = width // 128
    own = np.arange(width // 2)
    z, xh = own // (32 * r), (own // (16 * r)) % 2
    y, xl, c, i = (own // (4 * r)) % 4, (own // (2 * r)) % 2, (own // r) % 2, own % r
    return np.concatenate([
        (c != core) * (width // 2) + ((((z * 4 + y) * 2 + xh) * 2 + xl) * 2 + cols) * r + i
        for cols in range(2)
    ])


def near_order(width, here):
    r = width // 128
    new = np.arange(width)
    x = (here + jnp.asarray((0, 3, 1, 2))[new // (32 * r)]) % 4
    z, y, c, i = (new // (8 * r)) % 4, (new // (2 * r)) % 4, (new // r) % 2, new % r
    return (((z * 2 + x // 2) * 4 + y) * 4 + (x % 2) * 2 + c) * r + i


def near_head_order(width, here, core):
    r = width // 128
    own = np.arange(width // 2)
    z, xh = own // (32 * r), (own // (16 * r)) % 2
    y, xl, c, i = (own // (4 * r)) % 4, (own // (2 * r)) % 2, (own // r) % 2, own % r
    apart = jnp.asarray((0, 2, 3, 1))[(xh * 2 + xl - here) % 4]
    return jnp.concatenate([
        (c != core) * (width // 2) + (((apart * 2 + z) * 4 + y) * 2 + cols) * r + i for cols in range(2)
    ])


def one_hot(picks, width):
    rows = lax.broadcasted_iota(jnp.int32, (width, picks.shape[0]), 0)
    return (rows == jnp.asarray(picks, jnp.int32)[None, :]).astype(BF)


def dot(left, right, kind=F32):
    return jnp.dot(left, right, preferred_element_type=kind)


def dot_t(left, right, kind=F32):
    return lax.dot_general(left, right, (((0,), (0,)), ((), ())), preferred_element_type=kind)


def dot_b(left, right, kind=F32):
    return lax.dot_general(left, right, (((1,), (1,)), ((), ())), preferred_element_type=kind)


def two_parts(value):
    high = lax.reduce_precision(value, 8, 7)
    return high.astype(BF), (value - high).astype(BF)


def reorder_wide(value, order):
    high, low = two_parts(value)
    both = dot_b(jnp.concatenate([high, low], axis=0), order)
    return both[: value.shape[0]] + both[value.shape[0] :]


def norm_stats(x):
    center = x - jnp.mean(x, axis=-1, keepdims=True)
    spread = jnp.mean(center * center, axis=-1, keepdims=True)
    scale = lax.rsqrt(spread + NORM_EPS)
    return center * scale, scale


def norm(x, gain, shift):
    unit, scale = norm_stats(x)
    return (unit * gain + shift).astype(BF)


def whole(array, rows=None):
    return pl.BlockSpec((rows or array.shape[0],) + array.shape[1:], lambda i: (0,) * array.ndim)


def norm_back(x, partial, far, small, gain, gradient, rounded, first=()):
    n, width = x.shape
    extra = () if gradient is None else (gradient,)

    def kernel(x_ref, near_ref, far_ref, small_ref, *refs):
        total_ref, branch_ref, rows_ref = refs[len(extra) + len(first) :]
        unit, scale = norm_stats(x_ref[...])
        grad = near_ref[...] + far_ref[...]
        if rounded:
            grad = grad.astype(BF).astype(F32)
        inner = grad * small_ref[gain : gain + 1, :]
        total = scale * (
            inner
            - jnp.mean(inner, axis=-1, keepdims=True)
            - unit * jnp.mean(inner * unit, axis=-1, keepdims=True)
        )
        if extra:
            total = total + refs[0][...]
        total_ref[...] = total
        branch = total.astype(BF)
        branch_ref[...] = branch
        rows_ref[...] = jnp.zeros(rows_ref.shape, F32)
        rows_ref[0:1, :] = jnp.sum(grad * unit, axis=0, keepdims=True)
        rows_ref[1:2, :] = jnp.sum(grad, axis=0, keepdims=True)
        rows_ref[2:3, :] = jnp.sum(branch.astype(F32), axis=0, keepdims=True)

    shapes = ((n, width), F32), ((n, width), BF), ((8, width), F32)
    return pl.pallas_call(
        kernel,
        grid=(1,),
        in_specs=[whole(x), whole(partial, n), whole(far), whole(small, SMALL_ROWS)]
        + [whole(e) for e in extra] + [pl.BlockSpec(memory_space=pl.ANY)] * len(first),
        out_specs=[pl.BlockSpec(shape, lambda i: (0, 0)) for shape, kind in shapes],
        out_shape=[jax.ShapeDtypeStruct(shape, kind) for shape, kind in shapes],
    )(x, partial, far, small, *extra, *first)


def gelu_parts(u):
    cdf = 0.5 * (1.0 + lax.erf(u * (0.5**0.5)))
    pdf = jnp.exp(-0.5 * u * u) * (1.0 / np.sqrt(2.0 * np.pi)).astype(np.float32)
    return u * cdf, cdf + u * pdf


def lane_mask(value, which):
    lane = lax.broadcasted_iota(jnp.int32, value.shape, 1)
    return jnp.where((lane // HEAD) == which, value, jnp.zeros_like(value))


def allowed_of(causal, ids_ref, qid_ref, part):
    seg = ids_ref[part, :, 0:1] == qid_ref[0:1, :]
    if causal:
        seg = seg & (ids_ref[part, :, 1:2] <= qid_ref[1:2, :])
    return seg


def scores_t(keys, query, allowed):
    raw = lax.dot_general(keys, query, (((1,), (1,)), ((), ())), preferred_element_type=F32)
    return jnp.where(allowed, raw, MASKED)


def attend_kernel(causal, q_ref, k0_ref, v0_ref, k1_ref, v1_ref, ids_ref, qid_ref, o_ref, lse_ref):
    query = q_ref[...] * jnp.asarray(HEAD**-0.5, BF)
    allowed = [allowed_of(causal, ids_ref, qid_ref, part) for part in range(2)]
    mixed = []
    for head in range(2):
        one = lane_mask(query, head)
        scores = [scores_t(ref[...], one, ok) for ref, ok in zip((k0_ref, k1_ref), allowed)]
        top = jnp.maximum(
            jnp.max(scores[0], axis=0, keepdims=True), jnp.max(scores[1], axis=0, keepdims=True)
        )
        expo = [jnp.exp(s - top) for s in scores]
        total = jnp.sum(expo[0], axis=0, keepdims=True) + jnp.sum(expo[1], axis=0, keepdims=True)
        share = 1.0 / total
        out = 0.0
        for ref, e in zip((v0_ref, v1_ref), expo):
            out = out + lax.dot_general(
                ref[...], (e * share).astype(BF), (((0,), (0,)), ((), ())), preferred_element_type=F32
            )
        mixed.append(out)
        lse_ref[0, head : head + 1, :] = top + jnp.log(total)
    both = jnp.concatenate([mixed[0][:HEAD], mixed[1][HEAD:]], axis=0)
    o_ref[...] = both.T.astype(BF)


def attend_back_kernel(
    causal, q_ref, k0_ref, v0_ref, k1_ref, v1_ref, g_ref, ids_ref, qid_ref, lse_ref,
    dq_ref, dk0_ref, dv0_ref, dk1_ref, dv1_ref,
):
    query = q_ref[...] * jnp.asarray(HEAD**-0.5, BF)
    grad = g_ref[...]
    allowed = [allowed_of(causal, ids_ref, qid_ref, part) for part in range(2)]
    keys = (k0_ref[...], k1_ref[...])
    values = (v0_ref[...], v1_ref[...])
    grad_q = 0.0
    grad_k = [0.0, 0.0]
    grad_v = [0.0, 0.0]
    for head in range(2):
        one = lane_mask(query, head)
        grad_one = lane_mask(grad, head)
        lse = lse_ref[0, head : head + 1, :]
        probs = [jnp.exp(scores_t(k, one, ok) - lse) for k, ok in zip(keys, allowed)]
        grad_p = [
            lax.dot_general(v, grad_one, (((1,), (1,)), ((), ())), preferred_element_type=F32)
            for v in values
        ]
        inner = jnp.sum(probs[0] * grad_p[0], axis=0, keepdims=True) + jnp.sum(
            probs[1] * grad_p[1], axis=0, keepdims=True
        )
        for part in range(2):
            grad_s = (probs[part] * (grad_p[part] - inner)).astype(BF)
            grad_v[part] = grad_v[part] + dot(probs[part].astype(BF), grad_one)
            grad_k[part] = grad_k[part] + dot(grad_s, one)
            grad_q = grad_q + lax.dot_general(
                lane_mask(keys[part], head), grad_s, (((0,), (0,)), ((), ())),
                preferred_element_type=F32,
            )
    dq_ref[...] = (grad_q * HEAD**-0.5).T.astype(BF)
    dk0_ref[...] = grad_k[0]
    dv0_ref[...] = grad_v[0]
    dk1_ref[...] = grad_k[1].astype(BF)
    dv1_ref[...] = grad_v[1].astype(BF)


def call_kernel(body, causal, arrays, ids, qid, extra, first, out_shape, out_specs):
    in_specs = [
        pl.BlockSpec(
            (a[0].shape[0], PAIR), lambda p, at=a[1], step=(a + (1,))[2]: (0, at + p * step)
        )
        for a in arrays
    ]
    in_specs.append(pl.BlockSpec(ids.shape, lambda p: (0, 0, 0)))
    in_specs.append(pl.BlockSpec(qid.shape, lambda p: (0, 0)))
    in_specs += [pl.BlockSpec((1,) + e.shape[1:], lambda p: (p, 0, 0)) for e in extra]

    in_specs += [pl.BlockSpec(memory_space=pl.ANY) for f in first]
    n_in = len(in_specs)

    def kernel(*refs):
        body(causal, *refs[: n_in - len(first)], *refs[n_in:])

    pairs = extra[0].shape[0] if extra else out_shape[1].shape[0]
    return pl.pallas_call(
        kernel,
        grid=(pairs,),
        in_specs=in_specs,
        out_specs=out_specs,
        out_shape=out_shape,
        compiler_params=pltpu.CompilerParams(vmem_limit_bytes=56 * 1024 * 1024),
        cost_estimate=pl.CostEstimate(flops=0, bytes_accessed=0, transcendentals=0),
    )(*[a[0] for a in arrays], ids, qid, *extra, *first)


def attend_fwd(causal, arrays, ids, qid, pairs, first=()):
    n_q = qid.shape[1]
    out_shape = (
        jax.ShapeDtypeStruct((n_q, pairs * PAIR), BF),
        jax.ShapeDtypeStruct((pairs, 2, n_q), F32),
    )
    out_specs = (
        pl.BlockSpec((n_q, PAIR), lambda p: (0, p)),
        pl.BlockSpec((1, 2, n_q), lambda p: (p, 0, 0)),
    )
    return call_kernel(
        attend_kernel, causal, arrays, ids, qid, (), first, out_shape, out_specs,
    )


def attend_back(causal, arrays, ids, qid, lse, first=()):
    pairs, n_q, n_k = lse.shape[0], qid.shape[1], ids.shape[1]
    wide = pairs * PAIR
    out_shape = (
        jax.ShapeDtypeStruct((n_q, wide), BF),
        jax.ShapeDtypeStruct((n_k, wide), F32),
        jax.ShapeDtypeStruct((n_k, wide), F32),
        jax.ShapeDtypeStruct((n_k, wide), BF),
        jax.ShapeDtypeStruct((n_k, wide), BF),
    )
    out_specs = tuple(pl.BlockSpec((s.shape[0], PAIR), lambda p: (0, p)) for s in out_shape)
    return call_kernel(
        attend_back_kernel, causal, arrays, ids, qid, (lse,), first, out_shape, out_specs,
    )


def join_grads(queries, near, far):
    fars = list({id(f): f for f, at in far}.values())
    n, k = near[0].shape[0], len(queries)
    width = sum(v.shape[1] for v in list(queries) + list(near))

    def kernel(*refs):
        out, at = refs[-1], 0
        for ref in refs[:k]:
            out[:, at : at + ref.shape[1]] = ref[...]
            at += ref.shape[1]
        far_refs = dict(zip([id(f) for f in fars], refs[k + len(near) : -1]))
        for ref, (f, first) in zip(refs[k : k + len(near)], far):
            w = ref.shape[1]
            total = ref[...] + far_refs[id(f)][:, first : first + w].astype(F32)
            out[:, at : at + w] = total.astype(BF)
            at += w

    arrays = list(queries) + list(near) + fars
    return pl.pallas_call(
        kernel,
        grid=(1,),
        in_specs=[whole(a) for a in arrays],
        out_specs=pl.BlockSpec((n, width), lambda i: (0, 0)),
        out_shape=jax.ShapeDtypeStruct((n, width), BF),
        compiler_params=pltpu.CompilerParams(vmem_limit_bytes=56 * 1024 * 1024),
    )(*arrays)


def far_pairs(keys_values, pairs):
    half = pairs * PAIR
    return [
        swap(jnp.concatenate([
            keys_values[:, p * PAIR : (p + 1) * PAIR],
            keys_values[:, half + p * PAIR : half + (p + 1) * PAIR],
        ], axis=1), "xl")
        for p in range(pairs)
    ]


def attend_pairs(query, near, at, far, ids, qid, pairs, first=()):
    done = []
    for p in range(pairs):
        arrays = [(query, p), (near, at + p), (near, at + pairs + p), (far[p], 0), (far[p], 1)]
        done.append(attend_fwd(False, arrays, ids, qid, 1, first))
    return jnp.concatenate([d[0] for d in done], axis=1), [d[1] for d in done]


def attend_pairs_back(query, near, at, far, grad, ids, qid, lse, first=()):
    pairs = len(lse)
    grad_q, near_k, near_v, sent = [], [], [], []
    for p in range(pairs):
        arrays = [
            (query, p), (near, at + p), (near, at + pairs + p), (far[p], 0), (far[p], 1), (grad, p)
        ]
        gq, k0, v0, k1, v1 = attend_back(False, arrays, ids, qid, lse[p], first)
        grad_q.append(gq)
        near_k.append(k0)
        near_v.append(v0)
        sent.append(swap(jnp.concatenate([k1, v1], axis=1), "xl"))
    return grad_q, near_k + near_v, [(f, 0) for f in sent] + [(f, PAIR) for f in sent]


def adam_step(master, first, second, gradient, factor, rate, decay):
    clipped = gradient * factor
    first_new = BETA_FIRST * first + (1 - BETA_FIRST) * clipped
    second_new = BETA_SECOND * second + (1 - BETA_SECOND) * clipped * clipped
    first_hat = first_new / (1 - BETA_FIRST**STEP)
    second_hat = second_new / (1 - BETA_SECOND**STEP)
    master_new = master - rate * (first_hat / (jnp.sqrt(second_hat) + ADAM_EPS) + decay * master)
    return (master_new, first_new, second_new)


def per_device(
    src_x, tgt_x, out_cot, src_seg, tgt_seg, src_pad, tgt_pad,
    enc_master, dec_master, down_master, small_master,
    enc_first, dec_first, down_first, small_first,
    enc_second, dec_second, down_second, small_second,
):
    width = src_x.shape[-1]
    half = width // 2
    hid = 2 * width
    pairs = half // PAIR
    rows = enc_master.shape[0]
    down_rows = down_master.shape[0]
    n_small = small_master.shape[1]
    core = lax.axis_index("c")
    first_core = core == 0
    order = one_hot(feature_order(width), width)
    hidden = one_hot(hidden_order(width), width)
    place = one_hot(jnp.where(first_core, head_order(width, 0), head_order(width, 1)), width)
    quarter = width // 4
    here = lax.axis_index("xh") * 2 + lax.axis_index("xl")
    order_e = one_hot(near_order(width, here), width)
    place_e = one_hot(near_head_order(width, here, core), width)

    encb, decb, downb = enc_master.astype(BF), dec_master.astype(BF), down_master.astype(BF)
    smallb = jnp.pad(small_master.astype(BF), ((0, 0), (0, LANES - n_small)))

    def block(matrix, index):
        return matrix[:, index * width : (index + 1) * width]

    def halves(matrix):
        n = matrix.shape[1] // 2
        return matrix[:, :n], matrix[:, n:]

    ups = jnp.concatenate([encb[:, 4 * width :], decb[:, 8 * width :]], axis=0).reshape(-1, width)
    ups = dot(ups, hidden, BF).reshape(2, rows, 4, 2, 2, quarter)

    def up_halves(index):
        return [
            jnp.concatenate([ups[index, :, z, c, g] for g in range(2) for z in range(4)], axis=1)
            for c in range(2)
        ]

    col_blocks = [
        halves(block(encb, 0)), halves(block(encb, 1)), halves(block(encb, 2)), (smallb, smallb),
        up_halves(0), halves(block(decb, 5)), halves(block(decb, 6)),
        halves(block(decb, 0)), halves(block(decb, 1)), halves(block(decb, 2)), halves(block(decb, 4)),
        up_halves(1),
    ]
    cols0 = jnp.concatenate([b[0] for b in col_blocks], axis=1)
    cols1 = jnp.concatenate([b[1] for b in col_blocks], axis=1)
    mine = jnp.where(first_core, cols0, cols1)
    theirs = swap(jnp.where(first_core, cols1, cols0), "c")
    cols = jnp.concatenate(
        [jnp.where(first_core, mine, theirs), jnp.where(first_core, theirs, mine)], axis=0
    )
    shards = dot(jnp.concatenate(
        [block(encb, 3), block(decb, 3), block(decb, 7), downb[:, :width], downb[:, width:]], axis=0
    ), order, BF)
    out_rows = [shards[j * rows : (j + 1) * rows] for j in range(3)]
    out_rows = jnp.concatenate([
        jnp.concatenate([part[:, :half] for part in out_rows], axis=1),
        jnp.concatenate([part[:, half:] for part in out_rows], axis=1),
    ], axis=0)

    def down_packed(index):
        at = 3 * rows + index * down_rows
        middle = at + down_rows // 2
        return jnp.concatenate([shards[at:middle], shards[middle : at + down_rows]], axis=1)

    n_qkv, n_one = 3 * half, 3 * half + LANES
    n_up = cols.shape[1] - hid
    packed_one = jnp.concatenate([cols[:, :n_one], out_rows[:, :half]], axis=1)
    packed = jnp.concatenate([
        down_packed(0), cols[:, n_one:n_up], out_rows[:, half:], down_packed(1), cols[:, n_up:]
    ], axis=1)
    sizes = (n_qkv, LANES, half, hid, hid, 2 * half, n_qkv, half, 2 * half, hid, hid)
    starts = [int(v) for v in np.cumsum((0,) + sizes)]
    full_one = gather_by_trade(packed_one, ("z", "y"), 16).reshape(width // 4, starts[3])
    found = [packed, flip(packed, 1), flip(packed, 2), flip(after(packed, full_one), 3)]
    full_one = ring_gather(full_one)
    packed = []
    for spot in range(4):
        part = found[0]
        for bits in (1, 2, 3):
            part = jnp.where((here ^ bits) == spot, found[bits], part)
        packed.append(part)
    packed = jnp.concatenate(packed, axis=0)
    full_two = lax.all_gather(packed[:, : starts[9] - starts[3]], ("z", "y"), axis=0, tiled=True)
    packed_three = packed[:, starts[9] - starts[3] :]
    full_three = lax.all_gather(packed_three, ("z", "y"), axis=0, tiled=True)

    def cut(full, first, last):
        base = starts[first]
        return [full[:, starts[j] - base : starts[j + 1] - base] for j in range(first, last)]

    w_eqkv, small_all, w_eo = cut(full_one, 0, 3)
    w_e2, w_e1, w_ckv, w_dqkv, w_cq, w_out = cut(full_two, 3, 9)
    w_d2, w_d1 = cut(full_three, 9, 11)

    def pick(which, low, high):
        return jnp.where(which, low, high), jnp.where(which, high, low)

    def unpack_out(low, high, place, count):
        kept, sent = pick(first_core, low, high)
        stored = dot_t(place, jnp.concatenate([kept, swap(sent, "c")], axis=0), BF)
        return [
            jnp.concatenate([stored[:half, cut], stored[half:, cut]], axis=1)
            for cut in (slice(j * half, (j + 1) * half) for j in range(count))
        ]

    def repack_out(grads):
        stacked = jnp.concatenate([
            jnp.concatenate([g[:, :half] for g in grads], axis=1),
            jnp.concatenate([g[:, half:] for g in grads], axis=1),
        ], axis=0)
        stored = dot(place, stacked, BF)
        low, high = pick(first_core, stored[:half], swap(stored[half:], "c"))
        return jnp.concatenate([low, high], axis=0)

    eye = one_hot(np.arange(width), width)
    small_e = dot_t(small_all, eye)
    small_own = dot_b(small_all.T, order_e)
    small_p = dot(small_own.astype(BF), order)

    def own_half(column):
        row = small_own[column]
        return jnp.where(first_core, row[:half], row[half:])

    def hidden_bias(column):
        stored = dot(after(small_own[column : column + 4], enc_qkv).astype(BF), hidden)
        stored = jnp.where(first_core, stored[:, :half], stored[:, half:])
        return stored.reshape(4, 2, quarter).transpose(1, 0, 2).reshape(1, hid)

    none = jnp.zeros((half,), F32)

    def ids_of(seg, pad, at):
        n = seg.shape[1]
        spot = (lax.axis_index("xl") * 2 + core) * n + jnp.arange(n, dtype=jnp.int32)
        key = jnp.where(pad[0] == 1, seg[0], -1)
        return jnp.stack([key, spot, seg[0]], axis=1)

    src_ids = join_core(ids_of(src_seg, src_pad, 0))
    tgt_ids = join_core(ids_of(tgt_seg, tgt_pad, 0))
    src_keys = jnp.stack([src_ids[:, :2], swap(src_ids[:, :2], "xl")])
    tgt_keys = jnp.stack([tgt_ids[:, :2], swap(tgt_ids[:, :2], "xl")])
    src_q = jnp.stack([src_ids[:, 2], src_ids[:, 1]])
    tgt_q = jnp.stack([tgt_ids[:, 2], tgt_ids[:, 1]])

    source = dot(src_x[0], order)
    source_e = dot(src_x[0], order_e)
    enc_norm = join_core(norm(source_e, small_e[0], small_e[1]))
    enc_qkv = (dot(enc_norm, w_eqkv) + jnp.concatenate([own_half(2), none, own_half(3)])).astype(BF)
    enc_far = far_pairs(enc_qkv[:, half:], pairs)

    target = dot(tgt_x[0], order)

    bias_e, bias_d = hidden_bias(8), hidden_bias(27)
    enc_att, enc_lse = attend_pairs(
        enc_qkv, enc_qkv, pairs, enc_far, src_keys, src_q, pairs, (packed_three, bias_e, bias_d)
    )
    by_z = after(w_eo, enc_qkv).reshape(4, 2, 16 * rows, half)
    w_eo, = unpack_out(by_z[:, 0].reshape(half, half), by_z[:, 1].reshape(half, half), place_e, 1)
    dec_norm = join_core(after(norm(target, small_p[14], small_p[15]), enc_att))
    dec_qkv = (dot(dec_norm, w_dqkv) + jnp.concatenate([own_half(16), none, own_half(17)])).astype(BF)
    dec_far = swap(dec_qkv[:, half:], "xl")

    def feed_fwd(normed, w_in, w_out, bias):
        active, slope = gelu_parts(dot(normed, w_in) + bias)
        active = active.astype(BF)
        out = dot(active[:, :width], w_out[:, :width]) + dot(active[:, width:], w_out[:, width:])
        return active, slope, out

    enc_one = source + sum_core(dot(enc_att, w_eo)) + small_p[4]
    enc_feed = join_core(after(norm(enc_one, small_p[5], small_p[6]), dec_qkv))
    enc_active, enc_slope, part = feed_fwd(enc_feed, w_e1, w_e2, bias_e)
    enc_two = enc_one + sum_core(part) + small_p[7]
    memory = join_core(norm(enc_two, small_p[12], small_p[13]))

    dec_arrays = [(dec_qkv, 0), (dec_qkv, pairs), (dec_qkv, 2 * pairs), (dec_far, 0), (dec_far, pairs)]
    cross_kv = (dot(memory, w_ckv) + jnp.concatenate([none, own_half(22)])).astype(BF)
    cross_far = far_pairs(cross_kv, pairs)
    w_out = after(w_out, enc_two)
    w_so, w_co = unpack_out(w_out[:half], w_out[half:], place, 2)
    self_att, self_lse = attend_fwd(
        True, dec_arrays, tgt_keys, tgt_q, pairs, (cross_kv, w_so, w_co, cross_far[0])
    )
    dec_one = target + sum_core(dot(self_att, w_so)) + small_p[18]
    cross_norm = join_core(norm(dec_one, small_p[19], small_p[20]))
    cross_q = (dot(cross_norm, w_cq) + own_half(21)).astype(BF)
    cross_att, cross_lse = attend_pairs(cross_q, cross_kv, 0, cross_far, src_keys, tgt_q, pairs)
    cross_far, cross_lse = jnp.concatenate(cross_far, axis=1), jnp.concatenate(cross_lse, axis=0)
    cross_arrays = [(cross_q, 0), (cross_kv, 0), (cross_kv, pairs), (cross_far, 0, 2), (cross_far, 1, 2)]
    dec_two = dec_one + sum_core(dot(cross_att, w_co)) + small_p[23]
    dec_feed = join_core(norm(dec_two, small_p[24], small_p[25]))
    dec_active, dec_slope, part = feed_fwd(dec_feed, w_d1, w_d2, bias_d)
    dec_out = reorder_wide(dec_two + sum_core(part) + small_p[26], order)

    ones = jnp.ones((8, 2 * src_x.shape[1]), BF)

    def column_sums(value):
        return dot(ones[:, : value.shape[0]], value)

    def feed_back(branch, normed, active, slope, w_in, w_out):
        grad_out = [dot_t(active[:, :width], branch, BF), dot_t(active[:, width:], branch, BF)]
        grad_hidden = jnp.concatenate([
            (dot_b(branch, w_out[:, :width]) * slope[:, :width]).astype(BF),
            (dot_b(branch, w_out[:, width:]) * slope[:, width:]).astype(BF),
        ], axis=1)
        grad_in = dot_t(normed, grad_hidden, BF)
        return column_sums(grad_hidden), grad_in, grad_out, dot_b(grad_hidden, w_in)

    def along_x(*values):
        return scatter_x([v.reshape(4, 2 * rows, v.shape[1]) for v in values])

    def reduce(value):
        value = lax.psum_scatter(value, ("z", "y"), scatter_dimension=0, tiled=True)
        return lax.optimization_barrier(value)

    top = dot(out_cot[0], order)
    rows_top = column_sums(top.astype(BF))
    branch = join_core(top.astype(BF))
    hidden_d, g_d1, g_d2, part = feed_back(branch, dec_feed, dec_active, dec_slope, w_d1, w_d2)
    part_three = jnp.concatenate(g_d2 + [g_d1], axis=1)
    sum_three = reduce(part_three)
    grad_two, branch, rows_24 = norm_back(dec_two, part, far_half(part), small_p, 24, top, False)

    branch = join_core(branch)
    grad_att = dot_b(branch, w_co, BF)
    cross_gq, ck0, cv0, ck1, cv1 = attend_back(
        False, cross_arrays + [(grad_att, 0)], src_keys, tgt_q, cross_lse, (part_three,)
    )
    cross_back = swap(jnp.concatenate([ck1, cv1], axis=1), "xl")
    g_co, g_cq = dot_t(cross_att, branch, BF), dot_t(cross_norm, cross_gq, BF)
    part = dot_b(cross_gq, w_cq)
    grad_one, branch, rows_19 = norm_back(
        dec_one, part, far_half(part), small_p, 19, grad_two, False, (g_cq,)
    )

    branch = join_core(branch)
    grad_att = dot_b(branch, w_so, BF)
    g_so = dot_t(self_att, branch, BF)
    self_gq, sk0, sv0, sk1, sv1 = attend_back(
        True, dec_arrays + [(grad_att, 0)], tgt_keys, tgt_q, self_lse, (g_co, g_cq, g_so)
    )
    self_far = swap(jnp.concatenate([sk1, sv1], axis=1), "xl")
    dec_outs = repack_out((g_so, g_co))
    cross_gkv = after(jnp.concatenate([ck0, cv0], axis=1) + cross_back, self_gq).astype(BF)
    part = dot_b(cross_gkv, w_ckv)
    g_ckv = dot_t(memory, cross_gkv, BF)
    enc_grad_two, branch, rows_12 = norm_back(
        enc_two, part, far_half(part), small_p, 12, None, True, (g_ckv, dec_outs)
    )

    self_gkv = (jnp.concatenate([sk0, sv0], axis=1) + self_far).astype(BF)
    self_grad = jnp.concatenate([self_gq, self_gkv], axis=1)
    g_dqkv = dot_t(dec_norm, self_grad, BF)

    branch = join_core(branch)
    hidden_e, g_e1, g_e2, part = feed_back(branch, enc_feed, enc_active, enc_slope, w_e1, w_e2)
    enc_grad_one, branch, rows_5 = norm_back(
        enc_one, part, far_half(part), small_p, 5, enc_grad_two, False, (g_e1, g_e2[0], g_e2[1])
    )
    branch = join_core(branch)
    grad_att, g_eo = dot_b(branch, w_eo, BF), dot_t(enc_att, branch, BF)
    part_two = jnp.concatenate(
        g_e2 + [g_e1, g_ckv, g_dqkv, g_cq, repack_out((g_eo,)), dec_outs], axis=1
    )
    sum_two = reduce(part_two)
    enc_gq, near, far = attend_pairs_back(
        enc_qkv, enc_qkv, pairs, enc_far, grad_att, src_keys, src_q, enc_lse, (part_two, sum_three)
    )
    self_grad_late = after(self_grad, enc_gq[-1])
    part = dot_b(self_grad_late, w_dqkv)
    tgt_grad, _, rows_14 = norm_back(target, part, far_half(part), small_p, 14, grad_one, False)

    near[0] = after(near[0], rows_14)
    enc_grad = join_grads(enc_gq, near, far)
    g_eqkv = dot_t(enc_norm, enc_grad, BF)
    part = dot_b(enc_grad, w_eqkv)
    back, _, rows_0 = norm_back(source_e, part, far_half(part), small_e, 0, None, False)
    src_grad = reorder_wide(enc_grad_one, order) + reorder_wide(back, order_e)

    tgt_grad = reorder_wide(tgt_grad, order)

    blocks = [rows_24, rows_19, rows_14, rows_12, rows_5, rows_top]
    columns = [(24, 25, 23), (19, 20, 18), (14, 15), (12, 13, 7), (5, 6, 4), (26,), (0, 1)]
    own_rows = [dot_b(jnp.concatenate(blocks, axis=0).astype(BF), order), dot_b(rows_0.astype(BF), order_e)]
    by_z = jnp.concatenate([
        jnp.concatenate([value[:, z * quarter :][:, :quarter], value[:, half * 2 + z * quarter :][:, :quarter]], axis=1)
        for value in (hidden_e, hidden_d) for z in range(4)
    ], axis=0)
    own_rows.append(dot_b(
        by_z.astype(BF), jnp.where(first_core, hidden[:, :half], hidden[:, half:])
    ))
    columns += [(c,) for base in (8, 27) for c in range(base, base + 4)]
    own_rows = jnp.concatenate(own_rows, axis=0).astype(BF)
    picks = np.full(LANES, -1)
    for j, names in enumerate(columns):
        for i, column in enumerate(names):
            picks[column] = 8 * j + i
    own_rows = dot_t(own_rows, one_hot(picks, own_rows.shape[0]), BF)

    sums = [column_sums(value) for value in (enc_grad, self_grad_late, cross_gq, cross_gkv[:, half:])]
    half_rows = jnp.concatenate(
        [sums[0][:, :half], sums[0][:, 2 * half :], sums[1][:, :half], sums[1][:, 2 * half :], sums[2], sums[3]],
        axis=0,
    ).astype(BF)
    picks = np.full(LANES, -1)
    for j, column in enumerate((2, 3, 16, 17, 21, 22)):
        picks[column] = 8 * j
    half_rows = dot_t(half_rows, one_hot(picks, 48), BF)
    empty = jnp.zeros_like(half_rows)
    own_rows = own_rows + jnp.where(
        first_core,
        jnp.concatenate([half_rows, empty], axis=0), jnp.concatenate([empty, half_rows], axis=0),
    )
    g_small = dot_t(order_e, own_rows, BF)
    early = along_x(after(sum_three, g_eqkv))
    sum_small = ring_scatter(g_small.reshape(4, quarter, LANES))
    sum_one = after(ring_scatter(g_eqkv.reshape(4, quarter, n_qkv)), g_small)
    sum_one = jnp.concatenate([sum_one.astype(BF), sum_small.astype(BF)], axis=1)
    sum_one = sum_by_trade(sum_one.reshape(16, 2 * rows, n_one), ("z", "y"))
    late = along_x(sum_two)
    sum_one = after(after(sum_one, early), late)
    s_eqkv, sum_small = sum_one[:, :n_qkv], sum_one[:, n_qkv:]

    s_d2, s_d1 = early[:, :hid], early[:, hid:]
    s_e2, s_e1, s_ckv, s_dqkv, s_cq = cut(late, 3, 8)
    s_eo, s_so, s_co = [late[:, late.shape[1] - j * half :][:, :half] for j in (3, 2, 1)]

    def from_cores(value):
        keep, send = pick(first_core, value[:rows], value[rows:])
        other = swap(send, "c")
        return pick(first_core, keep, other)

    low_small, high_small = from_cores(sum_small)
    grad_small = (low_small + high_small)[:, :n_small]
    lasts = early, s_eqkv, grad_small, late
    squares = sum(jnp.sum(part * part) for part in lasts)
    squares = jnp.full((8, LANES), squares)
    squares = squares + swap(squares, "c")
    squares = jnp.sum(gather_by_trade(squares, ("z", "xh", "y", "xl"), 64), axis=0)
    low, high = from_cores(jnp.concatenate([s_eqkv, s_e1, s_ckv, s_dqkv, s_cq, s_d1], axis=1))
    ups = jnp.stack([part[:, a : a + hid] for a in (n_qkv, low.shape[1] - hid) for part in (low, high)])
    ups = ups.reshape(2, 2, rows, 2, 4, quarter).transpose(0, 2, 4, 1, 3, 5).reshape(8 * rows, width)
    ups = reorder_wide(ups, hidden).reshape(2, rows, 2 * hid)

    def joined(start, count):
        at = [start + j * half for j in range(count)]
        return [part[:, a : a + half] for a in at for part in (low, high)]

    shards = [
        jnp.concatenate([part[:rows], part[rows:]], axis=1)
        for part in (s_eo, s_so, s_co)
    ] + [part[:, a : a + width] for part in (s_e2, s_d2) for a in (0, width)]
    shards = reorder_wide(jnp.concatenate(shards, axis=0), order)
    grad_enc = jnp.concatenate(joined(0, 3) + [shards[:rows], ups[0]], axis=1)
    at = n_qkv + hid
    grad_dec = jnp.concatenate(
        joined(at + 2 * half, 3) + [shards[rows : 2 * rows]] + joined(at + 5 * half, 1)
        + joined(at, 2) + [shards[2 * rows : 3 * rows], ups[1]], axis=1
    )
    shards = shards[3 * rows :]
    grad_down = jnp.concatenate([shards[:down_rows], shards[down_rows:]], axis=1)

    grad_norm = jnp.sqrt(squares[0, 0])
    factor = CLIP_LEVEL / jnp.maximum(grad_norm, CLIP_LEVEL)
    enc_all = adam_step(enc_master, enc_first, enc_second, grad_enc, factor, RATE_MATRIX, DECAY_RATE)
    dec_all = adam_step(dec_master, dec_first, dec_second, grad_dec, factor, RATE_MATRIX, DECAY_RATE)
    down_all = adam_step(
        down_master, down_first, down_second, grad_down, factor, RATE_MATRIX, DECAY_RATE
    )
    small_all_new = adam_step(
        small_master, small_first, small_second, grad_small, factor, RATE_SMALL, 0.0
    )
    return (
        dec_out[None], src_grad[None], tgt_grad[None], grad_norm,
        enc_all[0], dec_all[0], down_all[0], small_all_new[0],
        enc_all[1], dec_all[1], down_all[1], small_all_new[1],
        enc_all[2], dec_all[2], down_all[2], small_all_new[2],
        grad_small * factor,
    )


def solution(mesh):
    split = Mesh(mesh.devices.reshape(4, 2, 4, 2, 2), ALL_AXES)
    tokens = P(ROW_AXES, POS_AXES, None)
    marks = P(ROW_AXES, POS_AXES)
    shard = P(ALL_AXES, None)
    in_specs = (tokens,) * 3 + (marks,) * 4 + (shard,) * 12
    out_specs = (tokens,) * 3 + (P(),) + (shard,) * 13
    return jax.shard_map(
        per_device, mesh=split, in_specs=in_specs, out_specs=out_specs, check_vma=False
    )
```
